32 devices in a mesh: dp: 8 (over y, x, core), seq: 4 (over z).
Axes of the slice: x: 2, y: 2, z: 4, core: 2. Of those that a mesh axis runs over, the one named last changes fastest.
Arguments:
- char_embeds: bfloat16 [128, 320, 128], P('dp', 'seq'), may hold values from -6 to 6
- lengths: int32 [128], P('dp'), may hold values from 14 to 320, as said below
- conv_weight: bfloat16 [36, 128, 224], replicated, may hold values from -0.25 to 0.25
- conv_bias: bfloat16 [1792], replicated, may hold values from -3 to 3
- hwy_weight: bfloat16 [1, 1792, 3584], replicated, may hold values from -0.125 to 0.125
- hwy_bias: bfloat16 [1, 3584], replicated, may hold values from -3 to 3
- gru_in_weight: bfloat16 [1792, 3072], replicated, may hold values from -0.125 to 0.125
- gru_in_bias: bfloat16 [3072], replicated, may hold values from -3 to 3
- gru_rec_weight: bfloat16 [2, 512, 1536], replicated, may hold values from -0.25 to 0.25
- gru_rec_bias: bfloat16 [2, 1536], replicated, may hold values from 0.5 to 1.5
- out_grad: bfloat16 [128, 64, 1024], P('dp', 'seq'), may hold values from -6 to 6
Outputs:
- encoded: bfloat16 [128, 64, 1024], P('dp', 'seq')
- chars_grad: float32 [128, 320, 128], P('dp', 'seq')
- conv_weight_grad: float32 [36, 128, 224], replicated
- conv_bias_grad: float32 [1792], replicated
- hwy_weight_grad: float32 [1, 1792, 3584], P(None, None, 'dp')
- hwy_bias_grad: float32 [1, 3584], replicated
- gru_in_weight_grad: float32 [1792, 3072], P(None, 'dp')
- gru_in_bias_grad: float32 [3072], replicated
- gru_rec_weight_grad: float32 [2, 512, 1536], replicated
- gru_rec_bias_grad: float32 [2, 1536], replicated
The draws below stay inside these ranges and needn't reach their ends.
Inputs may be any that keep to these rules, and one draw needn't show every extreme that they name: `lengths`: in every aligned block of 16 sentences (those of one dp index) one sentence, drawn from the seed, has all 320 characters.
All inputs are finite; a program needn't handle non-finite values.
Results may differ from the reference program's by a relative error of at most 0.012.
Values may be sent and summed in bfloat16 or wider, within the bound.
A program may use at most 320 MiB of HBM per device.

```python
import jax
import jax.numpy as jnp
from jax import lax

EMB = 128
FILT = 224
NWID = 8
STRIDE = 5
HID = 512
HWY_LAYERS = 1
MICRO = 4
B_DEV = 16
TAPS = 36
CH = 1792
SENTS = 128
POOLED = 64
CHARS = 320


def draw_lengths(key, part):
    key = jax.random.fold_in(key, 7)
    base_key, pick_key = jax.random.split(key)
    lowest = CHARS // 24 + 1
    base_lengths = jax.random.randint(base_key, (SENTS,), lowest, CHARS + 1, dtype=jnp.int32)
    block_count = SENTS // B_DEV
    chosen = jax.random.randint(pick_key, (block_count, 1), 0, B_DEV, dtype=jnp.int32)
    full_row = (jnp.arange(B_DEV, dtype=jnp.int32)[None, :] == chosen).reshape(SENTS)
    return jnp.where(full_row, CHARS, base_lengths).astype(jnp.int32)


def block_levels(stream_key, extent, shards, smallest, largest):
    def one(dim, parts):
        heights = jax.random.uniform(jax.random.fold_in(jax.random.fold_in(stream_key, 6), dim), (parts,), jnp.float32, smallest / len(shards), largest / len(shards))
        return jnp.repeat(jnp.exp(heights), extent[dim] // parts).reshape((-1,) + (1,) * (len(extent) - dim - 1))

    loudness = one(*shards[0])
    for cut in shards[1:]:
        loudness = loudness * one(*cut)
    return loudness


def normal_values(stream_key, shape, spread, bound, cuts=(), kind=jnp.bfloat16):
    loudness = block_levels(stream_key, shape, cuts, -0.22, 0.18) if cuts else 1.0
    result = jax.random.normal(stream_key, shape, jnp.float32) * spread * loudness
    return jnp.minimum(jnp.maximum(result, -bound), bound).astype(kind)


def setup_inputs(seed: int = 0) -> dict:
    key_of = jax.random.split(jax.random.key(seed), 12)
    return {
        "char_embeds": normal_values(key_of[0], (SENTS, CHARS, EMB), 1.0, 6.0, ((0, 8), (1, 4))),
        "lengths": draw_lengths(jax.random.fold_in(key_of[11], 71), 0),
        "conv_weight": normal_values(key_of[2], (TAPS, EMB, FILT), (4 * EMB) ** -0.5, 0.25),
        "conv_bias": normal_values(key_of[3], (CH,), 0.5, 3.0),
        "hwy_weight": normal_values(key_of[4], (HWY_LAYERS, CH, 2 * CH), CH ** -0.5, 0.125),
        "hwy_bias": normal_values(key_of[5], (HWY_LAYERS, 2 * CH), 0.5, 3.0),
        "gru_in_weight": normal_values(key_of[6], (CH, 6 * HID), CH ** -0.5, 0.125),
        "gru_in_bias": normal_values(key_of[7], (6 * HID,), 0.5, 3.0),
        "gru_rec_weight": normal_values(key_of[8], (2, HID, 3 * HID), HID ** -0.5, 0.25),
        "gru_rec_bias": jnp.clip(jax.random.uniform(key_of[9], (2, 3 * HID), jnp.float32, 0.5, 1.5), 0.5, 1.5).astype(jnp.bfloat16),
        "out_grad": normal_values(key_of[10], (SENTS, POOLED, 2 * HID), 1.0, 6.0, ((0, 8), (1, 4))),
    }


@jax.custom_vjp
def low(v):
    return lax.optimization_barrier(v.astype(jnp.bfloat16)).astype(jnp.float32)

@jax.custom_vjp
def low_back(v):
    return v

def low_keep(v):
    return (low(v), None)

def low_pass(kept, grad):
    return (grad,)

def back_keep(v):
    return (v, None)

def back_low(kept, grad):
    return (low(grad),)
low.defvjp(low_keep, low_pass)
low_back.defvjp(back_keep, back_low)

def product(left_side, right_side):
    return jnp.dot(left_side, right_side, precision=lax.Precision.HIGHEST, preferred_element_type=jnp.float32)

def gru_sweep(gate_steps, live_steps, weight, bias_row):
    hidden_units = weight.shape[0]

    def advance(hidden_state, step_item):
        gate_in, live_now = step_item
        recur_pre = low_back(product(low(hidden_state), weight) + bias_row)
        reset_gate = jax.nn.sigmoid(gate_in[:, :hidden_units] + recur_pre[:, :hidden_units])
        update = jax.nn.sigmoid(gate_in[:, hidden_units:2 * hidden_units] + recur_pre[:, hidden_units:2 * hidden_units])
        fresh_state = jnp.tanh(gate_in[:, 2 * hidden_units:] + reset_gate * recur_pre[:, 2 * hidden_units:])
        moved_state = (1.0 - update) * fresh_state + update * hidden_state
        after_state = jnp.where(live_now[:, None] > 0, moved_state, hidden_state)
        return (after_state, live_now[:, None] * after_state)
    start_state = jnp.zeros((gate_steps.shape[1], hidden_units), jnp.float32)
    final_state, emitted = lax.scan(advance, start_state, (gate_steps, live_steps))
    return emitted

def encode(length_group, char_embeds, conv_weight, conv_bias, hwy_weight, hwy_bias, gru_in_weight, gru_in_bias, gru_rec_weight, gru_rec_bias):
    group_size = char_embeds.shape[0]
    left_reach = (NWID - 1) // 2
    channels = NWID * FILT
    positions = jnp.arange(CHARS, dtype=jnp.int32)
    char_live = positions[None, :] < length_group[:, None]
    masked = jnp.where(char_live[:, :, None], char_embeds, 0.0)
    padded = jnp.pad(masked, ((0, 0), (left_reach, NWID - 1 - left_reach), (0, 0)))
    pieces = []
    for tap_count in range(1, NWID + 1):
        lead_taps = (tap_count - 1) // 2
        first_tap = tap_count * (tap_count - 1) // 2
        columns = jnp.concatenate([padded[:, left_reach + offset:left_reach + offset + CHARS] for offset in range(-lead_taps, tap_count - lead_taps)], axis=2)
        kernel = conv_weight[first_tap:first_tap + tap_count].reshape(tap_count * EMB, FILT)
        pieces.append(product(columns.reshape(group_size * CHARS, tap_count * EMB), kernel))
    conv_pre = low_back(jnp.concatenate(pieces, axis=1) + conv_bias)
    activity = jax.nn.silu(conv_pre) * char_live.reshape(-1, 1).astype(jnp.float32)
    pooled_sum = lax.optimization_barrier(jnp.sum(activity.reshape(group_size, POOLED, STRIDE, channels), axis=2))
    segments = jnp.arange(POOLED, dtype=jnp.int32)
    live_count = jnp.clip(length_group[:, None] - STRIDE * segments[None, :], 0, STRIDE).astype(jnp.float32)
    pooled = pooled_sum / jnp.maximum(live_count, 1.0)[:, :, None]
    stream_in = low(pooled.reshape(group_size * POOLED, channels))
    for level_index in range(HWY_LAYERS):
        highway_pre = low_back(product(stream_in, hwy_weight[level_index]) + hwy_bias[level_index])
        carry_gate = jax.nn.sigmoid(highway_pre[:, channels:])
        mixed_out = carry_gate * jax.nn.silu(highway_pre[:, :channels]) + (1.0 - carry_gate) * stream_in
        stream_in = low(mixed_out)
    gate_pre = low_back(product(stream_in, gru_in_weight) + gru_in_bias)
    gate_pre = gate_pre.reshape(group_size, POOLED, 2, 3 * HID)
    seg_live = (segments[None, :] < (length_group[:, None] + STRIDE - 1) // STRIDE).astype(jnp.float32)
    live_steps = seg_live.T
    ahead_steps = jnp.transpose(gate_pre[:, :, 0], (1, 0, 2))
    behind_steps = jnp.transpose(gate_pre[:, :, 1], (1, 0, 2))[::-1]
    ahead_out = gru_sweep(ahead_steps, live_steps, gru_rec_weight[0], gru_rec_bias[0])
    behind_out = gru_sweep(behind_steps, live_steps[::-1], gru_rec_weight[1], gru_rec_bias[1])[::-1]
    return jnp.concatenate([jnp.transpose(ahead_out, (1, 0, 2)), jnp.transpose(behind_out, (1, 0, 2))], axis=2)

def reference(char_embeds, lengths, conv_weight, conv_bias, hwy_weight, hwy_bias, gru_in_weight, gru_in_bias, gru_rec_weight, gru_rec_bias, out_grad):
    group_size = B_DEV // MICRO
    group_total = SENTS // group_size
    params = tuple((array_in.astype(jnp.float32) for array_in in (conv_weight, conv_bias, hwy_weight, hwy_bias, gru_in_weight, gru_in_bias, gru_rec_weight, gru_rec_bias)))
    embeds = char_embeds.astype(jnp.float32).reshape(group_total, group_size, CHARS, EMB)
    cotangent = out_grad.astype(jnp.float32).reshape(group_total, group_size, POOLED, 2 * HID)
    length_groups = lengths.reshape(group_total, group_size)
    zeros_init = tuple((jnp.zeros(array_in.shape, jnp.float32) for array_in in params))

    def one_group(totals, inputs):
        embed_group, length_group, cot_group = inputs

        def forward_fn(embed_in, *weights):
            return encode(length_group, embed_in, *weights)
        encoded, pullback = jax.vjp(forward_fn, embed_group, *params)
        grad_tuple = pullback(cot_group)
        totals = tuple((running + addend for running, addend in zip(totals, grad_tuple[1:])))
        return (totals, (encoded, grad_tuple[0]))
    totals, (encoded, chars_grad) = lax.scan(one_group, zeros_init, (embeds, length_groups, cotangent))
    encoded_out = encoded.reshape(SENTS, POOLED, 2 * HID).astype(jnp.bfloat16)
    chars_grad = chars_grad.reshape(SENTS, CHARS, EMB)
    return (encoded_out, chars_grad, totals[0], totals[1], totals[2], totals[3], totals[4], totals[5], totals[6], totals[7])
```

```python
import functools

import jax
import jax.numpy as jnp
from jax import lax
from jax.experimental import pallas as pl
from jax.experimental.pallas import tpu as pltpu
from jax.sharding import PartitionSpec as P

NWID = 8
STRIDE = 5
LEAD = (NWID - 1) // 2
TILE = 256
F32 = jnp.float32
BF16 = jnp.bfloat16
VMEM_LIMIT = 61 * 2**20


def tile_taps(filters):
    found = []
    for tile in range(NWID * filters // TILE):
        first_width = tile * TILE // filters + 1
        last_width = (tile * TILE + TILE - 1) // filters + 1
        low, high = NWID, 0
        for width in range(first_width, last_width + 1):
            lead = (width - 1) // 2
            low, high = min(low, LEAD - lead), max(high, LEAD - lead + width)
        found.append((low, high))
    return found


def dense_taps(conv_weight):
    _, embed, filters = conv_weight.shape
    columns = []
    for width in range(1, NWID + 1):
        lead, first = (width - 1) // 2, width * (width - 1) // 2
        block = conv_weight[first : first + width].reshape(width * embed, filters)
        above = (LEAD - lead) * embed
        columns.append(jnp.pad(block, ((above, NWID * embed - above - width * embed), (0, 0))))
    return jnp.concatenate(columns, axis=1)


def sparse_taps(dense, embed, filters):
    found = []
    for width in range(1, NWID + 1):
        lead = (width - 1) // 2
        rows = slice((LEAD - lead) * embed, (LEAD - lead + width) * embed)
        block = dense[rows, (width - 1) * filters : width * filters]
        found.append(block.reshape(width, embed, filters))
    return jnp.concatenate(found, axis=0)


def sigmoid(value):
    return 0.5 * jnp.tanh(0.5 * value) + 0.5


def dot(left, right):
    return jnp.dot(left, right, preferred_element_type=F32)


def dot_nt(left, right):
    return lax.dot_general(left, right, (((1,), (1,)), ((), ())), preferred_element_type=F32)


def dot_tn(left, right):
    return lax.dot_general(left, right, (((0,), (0,)), ((), ())), preferred_element_type=F32)


def row_lengths(lens_ref, count, which):
    found = jnp.zeros(which.shape, jnp.int32)
    for place in range(count):
        found = jnp.where(which == place, lens_ref[place], found)
    return found


def one_hot(rows, columns, target):
    places = lax.broadcasted_iota(jnp.int32, (rows, columns), 1)
    return jnp.where(places == target, 1.0, 0.0).astype(BF16)


def row_ids(rows):
    return lax.broadcasted_iota(jnp.int32, (rows, 1), 0)


def shift_rows(value, count):
    if count == 0:
        return value
    rows = value.shape[0]
    ids = row_ids(rows)
    moved = pltpu.roll(value, count % rows, axis=0)
    keep = ids >= count if count > 0 else ids < rows + count
    return jnp.where(keep, moved, 0.0)


def ahead_kernel(
    sizes, lens_ref, chars_ref, taps_ref, conv_bias_ref, hwy_hbm, hwy_bias_ref,
    pooled_ref, high_ref, slope_ref, cross_ref, c1_ref, c2_ref, c3_ref,
    hwy_ref, stack_ref, sem,
):
    sentences, span, segments, channels, embed, filters = sizes
    rows = sentences * segments
    load = pltpu.make_async_copy(hwy_hbm, hwy_ref, sem)
    load.start()
    ids = row_ids(rows)
    segment, sentence = ids // sentences, ids % sentences
    length = row_lengths(lens_ref, sentences, sentence)
    live = []
    planes = {}
    for place in range(STRIDE):
        time = segment * STRIDE + place
        alive = time < length
        live.append(alive.astype(F32))
        target = jnp.where(alive, sentence * span + time, -1)
        plane = dot(one_hot(rows, sentences * span, target), chars_ref[...])
        for hop in (-1, 0, 1):
            planes[hop, place] = shift_rows(plane, -hop * sentences).astype(BF16)
    for place in range(STRIDE):
        for tap in range(NWID):
            spot = place + tap - LEAD
            part = planes[spot // STRIDE, spot % STRIDE]
            stack_ref[place, :, tap * embed : (tap + 1) * embed] = part
            cross_ref[tap * embed : (tap + 1) * embed, place * rows : (place + 1) * rows] = part.T
    count = jnp.clip(length - STRIDE * segment, 0, STRIDE).astype(F32)
    scale = 1.0 / jnp.maximum(count, 1.0)
    for tile, (low, high) in enumerate(tile_taps(filters)):
        cols = slice(tile * TILE, (tile + 1) * TILE)
        total = jnp.zeros((rows, TILE), F32)
        for place in range(STRIDE):
            pre = dot(
                stack_ref[place, :, low * embed : high * embed],
                taps_ref[low * embed : high * embed, cols],
            ) + conv_bias_ref[:, cols]
            gate = sigmoid(pre)
            act = pre * gate
            total = total + act * live[place]
            slope_ref[place, :, cols] = (gate + act * (1.0 - gate)).astype(BF16)
        pooled_ref[:, cols] = (total * scale).astype(BF16)
    load.wait()
    for tile in range(channels // TILE):
        cols = slice(tile * TILE, (tile + 1) * TILE)
        cols_2 = slice(channels + tile * TILE, channels + (tile + 1) * TILE)
        pre_1 = dot(pooled_ref[...], hwy_ref[:, cols]) + hwy_bias_ref[:, cols]
        pre_2 = dot(pooled_ref[...], hwy_ref[:, cols_2]) + hwy_bias_ref[:, cols_2]
        layer_in = pooled_ref[:, cols].astype(F32)
        gate, inner = sigmoid(pre_2), sigmoid(pre_1)
        act = pre_1 * inner
        off = 1.0 - gate
        high_ref[:, cols] = (gate * act + off * layer_in).astype(BF16)
        c1_ref[:, cols] = gate * (inner + act * (1.0 - inner))
        c2_ref[:, cols] = (act - layer_in) * gate * off
        c3_ref[:, cols] = off


def gru_kernel(
    sizes, core_ref, lens_ref, high_ref, cot_ref, in_hbm, in_bias_ref, rec_hbm, rec_bias_ref,
    states_ref, dgates_ref, rec_grad_ref, rec_bias_grad_ref, in_bias_grad_ref,
    in_ref, rec_ref, rec_t_ref, gates_ref, coef_ref, prior_ref, emit_ref, sems,
):
    sentences, segments, hidden, height = sizes
    core = core_ref[0]
    wide = 3 * hidden
    pairs = 2 * sentences
    steps = segments * height
    rows = segments * pairs
    loads = [
        pltpu.make_async_copy(
            in_hbm.at[:, pl.ds(pl.multiple_of(core * wide, 128), wide)], in_ref, sems.at[0]
        ),
        pltpu.make_async_copy(rec_hbm.at[core], rec_ref, sems.at[1]),
    ]
    for load in loads:
        load.start()
    ids = row_ids(steps)
    step, lane = ids // height, ids % height
    segment = jnp.where(core == 0, step, segments - 1 - step)
    real = lane < pairs
    order = jnp.where(
        real, (lane // sentences) * (segments * sentences) + segment * sentences + lane % sentences, -1
    )
    to_steps = one_hot(steps, rows, order)
    order_2 = jnp.where(real, lane * segments + segment, -1)
    length = row_lengths(lens_ref, pairs, lane)
    live = real & (segment < (length + STRIDE - 1) // STRIDE)
    alive = jnp.broadcast_to(live.astype(F32), (steps, 128))
    stepped = dot(to_steps, high_ref[...]).astype(BF16)
    loads[0].wait()
    gates_ref[...] = dot(stepped, in_ref[...]) + in_bias_ref[...]
    emit_ref[...] = alive
    loads[1].wait()
    rec_bias = rec_bias_ref[...]

    def ahead(index, state):
        at = pl.ds(pl.multiple_of(index * height, height), height)
        q = dot(state.astype(BF16), rec_ref[...]) + rec_bias
        gates = gates_ref[at, :]
        alive = emit_ref[at, 0:1] > 0.0
        reset = sigmoid(gates[:, :hidden] + q[:, :hidden])
        update = sigmoid(gates[:, hidden : 2 * hidden] + q[:, hidden : 2 * hidden])
        q_n = q[:, 2 * hidden :]
        fresh = jnp.tanh(gates[:, 2 * hidden :] + reset * q_n)
        keep = jnp.where(alive, update, 1.0)
        move = jnp.where(alive, 1.0 - update, 0.0)
        after = move * fresh + keep * state
        prior_ref[at, :] = state
        slope = move * (1.0 - fresh * fresh)
        slope_r = slope * reset
        coef_ref[at, :hidden] = slope_r * q_n * (1.0 - reset)
        coef_ref[at, hidden : 2 * hidden] = (state - fresh) * update * move
        coef_ref[at, 2 * hidden : wide] = slope_r
        coef_ref[at, wide : wide + hidden] = slope
        coef_ref[at, wide + hidden :] = keep
        gates_ref[at, :hidden] = jnp.where(alive, after, 0.0)
        return after

    lax.fori_loop(0, segments, ahead, jnp.zeros((height, hidden), F32), unroll=2)
    pick = one_hot(steps, rows, order_2)
    states_ref[...] = dot_tn(pick, gates_ref[:, :hidden].astype(BF16)).astype(BF16)
    gates_ref[:, :hidden] = dot(pick, cot_ref[...]) * alive[:, 0:1]
    rec_t_ref[...] = rec_ref[...].T

    def back(index, carried):
        at = pl.ds(pl.multiple_of((segments - 1 - index) * height, height), height)
        total = carried + gates_ref[at, :hidden]
        d_r = total * coef_ref[at, :hidden]
        d_z = total * coef_ref[at, hidden : 2 * hidden]
        d_q = total * coef_ref[at, 2 * hidden : wide]
        d_n = total * coef_ref[at, wide : wide + hidden]
        kept = total * coef_ref[at, wide + hidden :]
        coef_ref[at, :hidden] = d_r
        coef_ref[at, hidden : 2 * hidden] = d_z
        coef_ref[at, 2 * hidden : wide] = d_q
        coef_ref[at, wide : wide + hidden] = d_n
        low = jnp.concatenate([d_r, d_z, d_q], axis=1).astype(BF16)
        return kept + dot(low, rec_t_ref[...])

    lax.fori_loop(0, segments, back, jnp.zeros((height, hidden), F32), unroll=2)
    recur = coef_ref[:, :wide].astype(BF16)
    rec_grad_ref[...] = dot_tn(prior_ref[...].astype(BF16), recur)
    sums = jnp.sum(recur.astype(F32), axis=0, keepdims=True)
    rec_bias_grad_ref[...] = sums
    fresh = coef_ref[:, wide : wide + hidden].astype(BF16)
    in_bias_grad_ref[:, : 2 * hidden] = sums[:, : 2 * hidden]
    in_bias_grad_ref[:, 2 * hidden :] = jnp.sum(fresh.astype(F32), axis=0, keepdims=True)
    dgates_ref[:, : 2 * hidden] = dot_tn(to_steps, recur[:, : 2 * hidden]).astype(BF16)
    dgates_ref[:, 2 * hidden :] = dot_tn(to_steps, fresh).astype(BF16)


def back_kernel(
    sizes, lens_ref, dgates_ref, c1_ref, c2_ref, c3_ref, slope_ref, cross_ref, taps_ref, in_hbm, hwy_hbm,
    dpre_ref, hwy_bias_ref, dtaps_ref, conv_bias_ref, dchars_ref,
    in_ref, hwy_ref, dy_ref, dconv_ref, sems,
):
    sentences, span, segments, channels, embed, filters = sizes
    rows = sentences * segments
    tiles = channels // TILE
    loads = []
    for tile in range(tiles):
        at = pl.ds(tile * TILE, TILE)
        loads.append(pltpu.make_async_copy(in_hbm.at[at], in_ref.at[at], sems.at[0, tile]))
    for tile in range(tiles):
        at = pl.ds(tile * TILE, TILE)
        loads.append(pltpu.make_async_copy(hwy_hbm.at[at], hwy_ref.at[at], sems.at[1, tile]))
    for load in loads:
        load.start()
    ids = row_ids(rows)
    segment, sentence = ids // sentences, ids % sentences
    length = row_lengths(lens_ref, sentences, sentence)
    count = jnp.clip(length - STRIDE * segment, 0, STRIDE).astype(F32)
    scale = 1.0 / jnp.maximum(count, 1.0)
    for tile in range(tiles):
        cols = slice(tile * TILE, (tile + 1) * TILE)
        cols_2 = slice(channels + tile * TILE, channels + (tile + 1) * TILE)
        loads[tile].wait()
        dy = dot_nt(dgates_ref[...], in_ref[cols, :])
        d_1 = (dy * c1_ref[:, cols]).astype(BF16)
        d_2 = (dy * c2_ref[:, cols]).astype(BF16)
        dpre_ref[:, cols] = d_1
        dpre_ref[:, cols_2] = d_2
        hwy_bias_ref[:, cols] = jnp.sum(d_1.astype(F32), axis=0, keepdims=True)
        hwy_bias_ref[:, cols_2] = jnp.sum(d_2.astype(F32), axis=0, keepdims=True)
        dy_ref[:, cols] = dy * c3_ref[:, cols]
    for tile in range(tiles):
        cols = slice(tile * TILE, (tile + 1) * TILE)
        loads[tiles + tile].wait()
        dy = (dy_ref[:, cols] + dot_nt(dpre_ref[...], hwy_ref[cols, :])) * scale
        sums = jnp.zeros((1, TILE), F32)
        for place in range(STRIDE):
            alive = (segment * STRIDE + place < length).astype(F32)
            part = (dy * alive * slope_ref[place, :, cols].astype(F32)).astype(BF16)
            dconv_ref[place * rows : (place + 1) * rows, cols] = part
            sums = sums + jnp.sum(part.astype(F32), axis=0, keepdims=True)
        conv_bias_ref[:, cols] = sums
    spans = tile_taps(filters)
    for tile, (low, high) in enumerate(spans):
        cols = slice(tile * TILE, (tile + 1) * TILE)
        dtaps_ref[:, cols] = jnp.zeros((NWID * embed, TILE), F32)
        dtaps_ref[low * embed : high * embed, cols] = dot(
            cross_ref[low * embed : high * embed, :], dconv_ref[:, cols]
        )
    sums = {}
    for first in range(0, NWID, 2):
        begin = min(tile for tile, (low, high) in enumerate(spans) if low < first + 2 and high > first)
        part = dot_nt(
            dconv_ref[:, begin * TILE :], taps_ref[first * embed : (first + 2) * embed, begin * TILE :]
        )
        for tap in (first, first + 1):
            for place in range(STRIDE):
                spot = place + tap - LEAD
                key = (spot // STRIDE, spot % STRIDE)
                piece = part[place * rows : (place + 1) * rows, (tap - first) * embed : (tap - first + 1) * embed]
                sums[key] = sums[key] + piece if key in sums else piece
    total = jnp.zeros((sentences * span, embed), F32)
    out_ids = row_ids(sentences * span)
    out_sentence, out_time = out_ids // span, out_ids % span
    for place in range(STRIDE):
        plane = jnp.zeros((rows, embed), F32)
        for hop in (-1, 0, 1):
            if (hop, place) in sums:
                plane = plane + shift_rows(sums[hop, place], hop * sentences)
        plane = jnp.where(segment * STRIDE + place < length, plane, 0.0).astype(BF16)
        target = jnp.where(
            out_time % STRIDE == place, (out_time // STRIDE) * sentences + out_sentence, -1
        )
        total = total + dot(one_hot(sentences * span, rows, target), plane)
    dchars_ref[...] = total.astype(BF16)


VMEM = pl.BlockSpec(memory_space=pltpu.VMEM)
SMEM = pl.BlockSpec(memory_space=pltpu.SMEM)
ANY = pl.BlockSpec(memory_space=pl.ANY)


def params(**more):
    return pltpu.CompilerParams(vmem_limit_bytes=VMEM_LIMIT, **more)


def shape(*dims, dtype=F32):
    return jax.ShapeDtypeStruct(dims, dtype)


def local(
    char_embeds, lengths, conv_weight, conv_bias, hwy_weight, hwy_bias, gru_in_weight, gru_in_bias,
    gru_rec_weight, gru_rec_bias, out_grad,
):
    groups = lax.axis_size("seq")
    dps = lax.axis_size("dp")
    seq_place, dp_place = lax.axis_index("seq"), lax.axis_index("dp")
    core = dp_place % 2
    sentences = char_embeds.shape[0] // groups
    span = char_embeds.shape[1] * groups
    segments = span // STRIDE
    embed, filters = conv_weight.shape[1:]
    channels = NWID * filters
    hidden = gru_rec_weight.shape[1]
    wide = 3 * hidden
    rows = sentences * segments
    height = max(8, 2 * sentences)
    pair = [(i, i ^ 1) for i in range(dps)]

    def joined(own):
        other = lax.ppermute(own, "dp", pair)
        return jnp.where(core == 0, jnp.stack([own, other]), jnp.stack([other, own]))

    chars = lax.all_to_all(char_embeds, "seq", 0, 1, tiled=True).reshape(sentences * span, embed)
    lens = lax.dynamic_slice(lengths, (seq_place * sentences,), (sentences,))
    lens_pair = joined(lens).reshape(-1)
    cot = lax.all_to_all(out_grad, "seq", 0, 1, tiled=True)
    kept = lax.dynamic_slice_in_dim(cot, core * hidden, hidden, 2)
    given = lax.ppermute(lax.dynamic_slice_in_dim(cot, (1 - core) * hidden, hidden, 2), "dp", pair)
    cot = jnp.where(core == 0, jnp.stack([kept, given]), jnp.stack([given, kept]))
    cot = cot.reshape(2 * rows, hidden)
    taps = dense_taps(conv_weight)
    sizes = (sentences, span, segments, channels, embed, filters)
    pooled, high, slope, cross, c1, c2, c3 = pl.pallas_call(
        functools.partial(ahead_kernel, sizes),
        name="ahead",
        out_shape=[
            shape(rows, channels, dtype=BF16),
            shape(rows, channels, dtype=BF16),
            shape(STRIDE, rows, channels, dtype=BF16),
            shape(NWID * embed, STRIDE * rows, dtype=BF16),
            shape(rows, channels),
            shape(rows, channels),
            shape(rows, channels),
        ],
        in_specs=[SMEM, VMEM, VMEM, VMEM, ANY, VMEM],
        out_specs=[VMEM] * 7,
        scratch_shapes=[
            pltpu.VMEM((channels, 2 * channels), BF16),
            pltpu.VMEM((STRIDE, rows, NWID * embed), BF16),
            pltpu.SemaphoreType.DMA,
        ],
        compiler_params=params(),
    )(lens, chars, taps, conv_bias.astype(F32)[None], hwy_weight[0], hwy_bias.astype(F32))
    high_all = lax.all_gather(high, "dp", axis=0, tiled=True)
    pooled_all = lax.all_gather(pooled, "dp", axis=0, tiled=True)
    high_pair = joined(high).reshape(2 * rows, channels)
    in_bias = lax.dynamic_slice(gru_in_bias.astype(F32)[None], (0, core * wide), (1, wide))
    rec_bias = lax.dynamic_slice(gru_rec_bias.astype(F32), (core, 0), (1, wide))
    steps = segments * height
    states, dgates, rec_grad, rec_bias_grad, in_bias_grad = pl.pallas_call(
        functools.partial(gru_kernel, (sentences, segments, hidden, height)),
        name="gru",
        out_shape=[
            shape(2 * rows, hidden, dtype=BF16),
            shape(2 * rows, wide, dtype=BF16),
            shape(hidden, wide),
            shape(1, wide),
            shape(1, wide),
        ],
        in_specs=[SMEM, SMEM, VMEM, VMEM, ANY, VMEM, ANY, VMEM],
        out_specs=[VMEM] * 5,
        scratch_shapes=[
            pltpu.VMEM((channels, wide), BF16),
            pltpu.VMEM((hidden, wide), BF16),
            pltpu.VMEM((wide, hidden), BF16),
            pltpu.VMEM((steps, wide), F32),
            pltpu.VMEM((steps, 5 * hidden), F32),
            pltpu.VMEM((steps, hidden), F32),
            pltpu.VMEM((steps, 128), F32),
            pltpu.SemaphoreType.DMA((2,)),
        ],
        compiler_params=params(),
    )(core[None].astype(jnp.int32), lens_pair, high_pair, cot, gru_in_weight, in_bias, gru_rec_weight, rec_bias)

    def swapped(pair_rows):
        blocks = pair_rows.reshape((2, rows) + pair_rows.shape[1:])
        kept = lax.dynamic_index_in_dim(blocks, core, 0, False)
        given = lax.ppermute(lax.dynamic_index_in_dim(blocks, 1 - core, 0, False), "dp", pair)
        return jnp.where(
            core == 0, jnp.concatenate([kept, given], 1), jnp.concatenate([given, kept], 1)
        )

    encoded = swapped(states).reshape(sentences, segments, 2 * hidden)
    encoded = lax.all_to_all(encoded, "seq", 1, 0, tiled=True)
    dgates = swapped(dgates)
    dpre, hwy_bias_grad, dtaps, conv_bias_grad, dchars = pl.pallas_call(
        functools.partial(back_kernel, sizes),
        name="back",
        out_shape=[
            shape(rows, 2 * channels, dtype=BF16),
            shape(1, 2 * channels),
            shape(NWID * embed, channels),
            shape(1, channels),
            shape(sentences * span, embed, dtype=BF16),
        ],
        in_specs=[SMEM, VMEM, VMEM, VMEM, VMEM, VMEM, VMEM, VMEM, ANY, ANY],
        out_specs=[VMEM] * 5,
        scratch_shapes=[
            pltpu.VMEM((channels, 2 * wide), BF16),
            pltpu.VMEM((channels, 2 * channels), BF16),
            pltpu.VMEM((rows, channels), F32),
            pltpu.VMEM((STRIDE * rows, channels), BF16),
            pltpu.SemaphoreType.DMA((2, channels // TILE)),
        ],
        compiler_params=params(),
    )(lens, dgates, c1, c2, c3, slope, cross, taps, gru_in_weight, hwy_weight[0])
    dchars = lax.all_to_all(dchars.reshape(sentences, span, embed), "seq", 1, 0, tiled=True)

    dgates_all = lax.all_to_all(dgates, "dp", 1, 0, tiled=True)
    dpre_all = lax.all_to_all(dpre, "dp", 1, 0, tiled=True)
    in_grad = dot_tn(high_all, dgates_all).astype(BF16)
    hwy_grad = dot_tn(pooled_all, dpre_all).astype(BF16)
    in_grad = lax.psum(in_grad, "seq").astype(F32)
    hwy_grad = lax.psum(hwy_grad, "seq").astype(F32)

    is_first = (core == 0).astype(F32)

    def both(own):
        return jnp.stack([own * is_first, own * (1.0 - is_first)])

    small = [
        sparse_taps(dtaps, embed, filters),
        conv_bias_grad,
        hwy_bias_grad,
        both(in_bias_grad),
        both(rec_grad),
        both(rec_bias_grad),
    ]
    flat = jnp.concatenate([part.reshape(-1).astype(BF16) for part in small])
    flat = lax.psum(flat, ("dp", "seq")).astype(F32)
    summed, at = [], 0
    for part in small:
        summed.append(flat[at : at + part.size].reshape(part.shape))
        at += part.size
    return (
        encoded,
        dchars.astype(F32),
        summed[0],
        summed[1].reshape(-1),
        hwy_grad[None],
        summed[2],
        in_grad,
        summed[3].reshape(-1),
        summed[4],
        summed[5].reshape(2, wide),
    )


def solution(mesh):
    whole = P()
    split = P("dp", "seq", None)
    return jax.shard_map(
        local,
        mesh=mesh,
        in_specs=(split, P("dp")) + (whole,) * 8 + (split,),
        out_specs=(split, split, whole, whole, P(None, None, "dp"), whole, P(None, "dp"), whole, whole, whole),
        check_vma=False,
    )
```

```python
import functools

import jax
import jax.numpy as jnp
from jax import lax
from jax.experimental import pallas as pl
from jax.experimental.pallas import tpu as pltpu
from jax.sharding import PartitionSpec as P

MESH = pl.DeviceIdType.MESH
NWID = 8
STRIDE = 5
LEAD = (NWID - 1) // 2
TILE = 256
F32 = jnp.float32
BF16 = jnp.bfloat16
VMEM_LIMIT = 61 * 2**20


def tile_taps(filters):
    found = []
    for tile in range(NWID * filters // TILE):
        first_width = tile * TILE // filters + 1
        last_width = (tile * TILE + TILE - 1) // filters + 1
        low, high = NWID, 0
        for width in range(first_width, last_width + 1):
            lead = (width - 1) // 2
            low, high = min(low, LEAD - lead), max(high, LEAD - lead + width)
        found.append((low, high))
    return found


def lay_taps(weight_ref, taps_ref):
    _, embed, filters = weight_ref.shape
    for tile, (low, high) in enumerate(tile_taps(filters)):
        for spot in range(low, high):
            pieces = []
            begin, end = tile * TILE, (tile + 1) * TILE
            while begin < end:
                width = begin // filters + 1
                stop = min(end, width * filters)
                tap = spot - LEAD + (width - 1) // 2
                if 0 <= tap < width:
                    block = weight_ref[width * (width - 1) // 2 + tap]
                    pieces.append(block[:, begin - (width - 1) * filters : stop - (width - 1) * filters])
                else:
                    pieces.append(jnp.zeros((embed, stop - begin), BF16))
                begin = stop
            laid = pieces[0] if len(pieces) == 1 else jnp.concatenate(pieces, axis=1)
            taps_ref[spot * embed : (spot + 1) * embed, tile * TILE : (tile + 1) * TILE] = laid
        for spot in list(range(low)) + list(range(high, NWID)):
            taps_ref[spot * embed : (spot + 1) * embed, tile * TILE : (tile + 1) * TILE] = jnp.zeros(
                (embed, TILE), BF16
            )


def sigmoid(value):
    return 0.5 * jnp.tanh(0.5 * value) + 0.5


def dot(left, right):
    return jnp.dot(left, right, preferred_element_type=F32)


def dot_nt(left, right):
    return lax.dot_general(left, right, (((1,), (1,)), ((), ())), preferred_element_type=F32)


def dot_tn(left, right):
    return lax.dot_general(left, right, (((0,), (0,)), ((), ())), preferred_element_type=F32)


def row_lengths(lens_ref, count, which):
    found = jnp.zeros(which.shape, jnp.int32)
    for place in range(count):
        found = jnp.where(which == place, lens_ref[place], found)
    return found


def one_hot(rows, columns, target):
    places = lax.broadcasted_iota(jnp.int32, (rows, columns), 1)
    return jnp.where(places == target, 1.0, 0.0).astype(BF16)


def row_ids(rows):
    return lax.broadcasted_iota(jnp.int32, (rows, 1), 0)


def shift_rows(value, count):
    if count == 0:
        return value
    rows = value.shape[0]
    ids = row_ids(rows)
    moved = pltpu.roll(value, count % rows, axis=0)
    keep = ids >= count if count > 0 else ids < rows + count
    return jnp.where(keep, moved, 0.0)


def ahead_kernel(
    sizes, lens_ref, chars_ref, weight_ref, conv_bias_ref, hwy_hbm, hwy_bias_ref,
    pooled_ref, high_ref, slope_ref, cross_ref, c1_ref, c2_ref, c3_ref, taps_ref,
    hwy_ref, stack_ref, sem,
):
    sentences, span, segments, channels, embed, filters = sizes
    rows = sentences * segments
    load = pltpu.make_async_copy(hwy_hbm, hwy_ref, sem)
    load.start()
    lay_taps(weight_ref, taps_ref)
    ids = row_ids(rows)
    segment, sentence = ids // sentences, ids % sentences
    length = row_lengths(lens_ref, sentences, sentence)
    live = []
    planes = {}
    for place in range(STRIDE):
        time = segment * STRIDE + place
        alive = time < length
        live.append(alive.astype(F32))
        target = jnp.where(alive, sentence * span + time, -1)
        plane = dot(one_hot(rows, sentences * span, target), chars_ref[...])
        for hop in (-1, 0, 1):
            planes[hop, place] = shift_rows(plane, -hop * sentences).astype(BF16)
    for place in range(STRIDE):
        for tap in range(NWID):
            spot = place + tap - LEAD
            part = planes[spot // STRIDE, spot % STRIDE]
            stack_ref[place, :, tap * embed : (tap + 1) * embed] = part
            cross_ref[tap * embed : (tap + 1) * embed, place * rows : (place + 1) * rows] = part.T
    count = jnp.clip(length - STRIDE * segment, 0, STRIDE).astype(F32)
    scale = 1.0 / jnp.maximum(count, 1.0)
    for tile, (low, high) in enumerate(tile_taps(filters)):
        cols = slice(tile * TILE, (tile + 1) * TILE)
        total = jnp.zeros((rows, TILE), F32)
        for place in range(STRIDE):
            pre = dot(
                stack_ref[place, :, low * embed : high * embed],
                taps_ref[low * embed : high * embed, cols],
            ) + conv_bias_ref[:, cols]
            gate = sigmoid(pre)
            act = pre * gate
            total = total + act * live[place]
            slope_ref[place, :, cols] = (gate + act * (1.0 - gate)).astype(BF16)
        pooled_ref[:, cols] = (total * scale).astype(BF16)
    load.wait()
    for tile in range(channels // TILE):
        cols = slice(tile * TILE, (tile + 1) * TILE)
        cols_2 = slice(channels + tile * TILE, channels + (tile + 1) * TILE)
        pre_1 = dot(pooled_ref[...], hwy_ref[:, cols]) + hwy_bias_ref[:, cols]
        pre_2 = dot(pooled_ref[...], hwy_ref[:, cols_2]) + hwy_bias_ref[:, cols_2]
        layer_in = pooled_ref[:, cols].astype(F32)
        gate, inner = sigmoid(pre_2), sigmoid(pre_1)
        act = pre_1 * inner
        off = 1.0 - gate
        high_ref[:, cols] = (gate * act + off * layer_in).astype(BF16)
        c1_ref[:, cols] = gate * (inner + act * (1.0 - inner))
        c2_ref[:, cols] = (act - layer_in) * gate * off
        c3_ref[:, cols] = off


def gru_kernel(
    sizes, core_ref, lens_ref, high_ref, cot_ref, in_hbm, in_bias_ref, rec_hbm, rec_bias_ref,
    states_ref, dgates_ref, rec_part_ref,
    in_ref, rec_ref, rec_t_ref, gates_ref, coef_ref, prior_ref, emit_ref, bias_ref, sems,
):
    sentences, segments, hidden, height = sizes
    core = core_ref[0]
    wide = 3 * hidden
    pairs = 2 * sentences
    steps = segments * height
    rows = segments * pairs
    loads = [
        pltpu.make_async_copy(
            in_hbm.at[:, pl.ds(pl.multiple_of(core * wide, 128), wide)], in_ref, sems.at[0]
        ),
        pltpu.make_async_copy(rec_hbm.at[core], rec_ref, sems.at[1]),
    ]
    for load in loads:
        load.start()
    ids = row_ids(steps)
    step, lane = ids // height, ids % height
    segment = jnp.where(core == 0, step, segments - 1 - step)
    real = lane < pairs
    order = jnp.where(
        real, (lane // sentences) * (segments * sentences) + segment * sentences + lane % sentences, -1
    )
    to_steps = one_hot(steps, rows, order)
    order_2 = jnp.where(real, lane * segments + segment, -1)
    length = row_lengths(lens_ref, pairs, lane)
    live = real & (segment < (length + STRIDE - 1) // STRIDE)
    alive = jnp.broadcast_to(live.astype(F32), (steps, 128))
    stepped = dot(to_steps, high_ref[...]).astype(BF16)
    loads[0].wait()
    gates_ref[...] = dot(stepped, in_ref[...]) + in_bias_ref[...]
    emit_ref[...] = alive
    loads[1].wait()
    rec_bias = rec_bias_ref[...]

    def ahead(index, state):
        at = pl.ds(pl.multiple_of(index * height, height), height)
        q = dot(state.astype(BF16), rec_ref[...]) + rec_bias
        gates = gates_ref[at, :]
        alive = emit_ref[at, 0:1] > 0.0
        reset = sigmoid(gates[:, :hidden] + q[:, :hidden])
        update = sigmoid(gates[:, hidden : 2 * hidden] + q[:, hidden : 2 * hidden])
        q_n = q[:, 2 * hidden :]
        fresh = jnp.tanh(gates[:, 2 * hidden :] + reset * q_n)
        keep = jnp.where(alive, update, 1.0)
        move = jnp.where(alive, 1.0 - update, 0.0)
        after = move * fresh + keep * state
        prior_ref[at, :] = state
        slope = move * (1.0 - fresh * fresh)
        slope_r = slope * reset
        coef_ref[at, :hidden] = slope_r * q_n * (1.0 - reset)
        coef_ref[at, hidden : 2 * hidden] = (state - fresh) * update * move
        coef_ref[at, 2 * hidden : wide] = slope_r
        coef_ref[at, wide : wide + hidden] = slope
        coef_ref[at, wide + hidden :] = keep
        gates_ref[at, :hidden] = jnp.where(alive, after, 0.0)
        return after

    lax.fori_loop(0, segments, ahead, jnp.zeros((height, hidden), F32), unroll=2)
    pick = one_hot(steps, rows, order_2)
    states_ref[...] = dot_tn(pick, gates_ref[:, :hidden].astype(BF16)).astype(BF16)
    gates_ref[:, :hidden] = dot(pick, cot_ref[...]) * alive[:, 0:1]
    rec_t_ref[...] = rec_ref[...].T

    def back(index, carried):
        at = pl.ds(pl.multiple_of((segments - 1 - index) * height, height), height)
        total = carried + gates_ref[at, :hidden]
        d_r = total * coef_ref[at, :hidden]
        d_z = total * coef_ref[at, hidden : 2 * hidden]
        d_q = total * coef_ref[at, 2 * hidden : wide]
        d_n = total * coef_ref[at, wide : wide + hidden]
        kept = total * coef_ref[at, wide + hidden :]
        coef_ref[at, :hidden] = d_r
        coef_ref[at, hidden : 2 * hidden] = d_z
        coef_ref[at, 2 * hidden : wide] = d_q
        coef_ref[at, wide : wide + hidden] = d_n
        low = jnp.concatenate([d_r, d_z, d_q], axis=1).astype(BF16)
        return kept + dot(low, rec_t_ref[...])

    lax.fori_loop(0, segments, back, jnp.zeros((height, hidden), F32), unroll=2)
    recur = coef_ref[:, :wide].astype(BF16)
    fresh = coef_ref[:, wide : wide + hidden].astype(BF16)
    prior = prior_ref[...].astype(BF16)
    sums = jnp.sum(recur.astype(F32), axis=0, keepdims=True)
    sums_n = jnp.sum(fresh.astype(F32), axis=0, keepdims=True)
    tiles = wide // TILE
    bias_ref[...] = jnp.zeros_like(bias_ref)
    for tile in range(tiles):
        cols = slice(tile * TILE, (tile + 1) * TILE)
        rec_part_ref[tile * hidden : (tile + 1) * hidden, :] = dot_tn(prior, recur[:, cols]).astype(BF16)
        if tile * TILE < 2 * hidden:
            bias_ref[tile : tile + 1, :] = sums[:, cols]
        else:
            bias_ref[tile : tile + 1, :] = sums_n[:, tile * TILE - 2 * hidden : (tile + 1) * TILE - 2 * hidden]
        bias_ref[tiles + tile : tiles + tile + 1, :] = sums[:, cols]
    rec_part_ref[tiles * hidden :, :] = bias_ref[...].astype(BF16)
    dgates_ref[:, : 2 * hidden] = dot_tn(to_steps, recur[:, : 2 * hidden]).astype(BF16)
    dgates_ref[:, 2 * hidden :] = dot_tn(to_steps, fresh).astype(BF16)


class Place:
    def __init__(self, dps, groups):
        self.chips, self.groups = dps // 2, groups
        self.dp, self.seq = lax.axis_index("dp"), lax.axis_index("seq")
        self.chip, self.core = self.dp // 2, self.dp % 2
        self.partner = (self.chip * 2 + 1 - self.core, self.seq)
        half = groups // 2
        low = self.seq < half
        self.inner = (self.dp, jnp.where(low, self.seq + 1, self.seq - 1))
        self.outer = (self.dp, jnp.clip(jnp.where(low, self.seq - 1, self.seq + 1), 0, groups - 1))
        self.has_outer = (self.seq > 0) & (self.seq < groups - 1)
        self.depth = jnp.where(low, half - 1 - self.seq, self.seq - half)
        self.middle = self.depth == 0

    def peer_chip(self, hop):
        return (self.chip + hop) % self.chips

    def peer(self, hop):
        return (self.peer_chip(hop) * 2 + self.core, self.seq)

    def peers(self):
        return [self.peer(hop) for hop in range(1, self.chips)]

    def along_place(self, hop):
        return (self.seq + hop) % self.groups

    def along(self):
        return [(self.dp, self.along_place(hop)) for hop in range(1, self.groups)]


def greet(devices):
    barrier = pltpu.get_barrier_semaphore()
    for device in devices:
        pl.semaphore_signal(barrier, inc=1, device_id=device, device_id_type=MESH)
    pl.semaphore_wait(barrier, len(devices))


def remote(src, dst, send, recv, device):
    return pltpu.make_async_remote_copy(
        src_ref=src, dst_ref=dst, send_sem=send, recv_sem=recv, device_id=device, device_id_type=MESH
    )


def exact(start, size, unit):
    return pl.ds(pl.multiple_of(start, unit), size)


def back_kernel(
    sizes, lens_ref, dgates_ref, c1_ref, c2_ref, c3_ref, slope_ref, cross_ref, taps_ref, in_hbm, hwy_hbm,
    in_box_ref, hwy_box_ref, conv_part_ref, chars_box_ref,
    in_ref, hwy_ref, other_ref, pair_ref, gates_t_ref, dpre_ref, pre_t_ref, dy_ref, dconv_ref, bias_ref, chars_ref,
    sems, swap_sems, in_sems, hwy_sems, chars_sems,
):
    sentences, span, segments, channels, embed, filters, dps, groups = sizes
    rows = sentences * segments
    tiles = channels // TILE
    wide = dgates_ref.shape[2]
    here = Place(dps, groups)
    loads = []
    for tile in range(tiles):
        at = pl.ds(tile * TILE, TILE)
        loads.append(pltpu.make_async_copy(in_hbm.at[at], in_ref.at[at], sems.at[0, tile]))
    for tile in range(tiles):
        at = pl.ds(tile * TILE, TILE)
        loads.append(pltpu.make_async_copy(hwy_hbm.at[at], hwy_ref.at[at], sems.at[1, tile]))
    for load in loads:
        load.start()
    greet([here.partner] + here.peers() + here.along())
    swap = remote(dgates_ref.at[1 - here.core], other_ref, swap_sems.at[0], swap_sems.at[1], here.partner)
    swap.start()
    ids = row_ids(rows)
    segment, sentence = ids // sentences, ids % sentences
    length = row_lengths(lens_ref, sentences, sentence)
    count = jnp.clip(length - STRIDE * segment, 0, STRIDE).astype(F32)
    scale = 1.0 / jnp.maximum(count, 1.0)
    bias_ref[...] = jnp.zeros_like(bias_ref)
    first = here.core == 0
    swap.wait()
    mine, other = dgates_ref[here.core], other_ref[...]
    for side, block in enumerate((jnp.where(first, mine, other), jnp.where(first, other, mine))):
        pair_ref[:, side * wide : (side + 1) * wide] = block
        gates_t_ref[side * wide : (side + 1) * wide, :] = block.T

    def spread(source, box, sends):
        share = box.shape[1]
        copies = []
        for hop in range(1, here.chips):
            at = exact(here.peer_chip(hop) * share, share, 16)
            copies.append(
                remote(source.at[at], box.at[here.chip], sends.at[0, hop], sends.at[1, hop], here.peer(hop))
            )
            copies[-1].start()
        box[here.chip] = source[exact(here.chip * share, share, 16), :]
        return copies

    copies = spread(gates_t_ref, in_box_ref, in_sems)
    for tile in range(tiles):
        cols = slice(tile * TILE, (tile + 1) * TILE)
        cols_2 = slice(channels + tile * TILE, channels + (tile + 1) * TILE)
        loads[tile].wait()
        dy = dot_nt(pair_ref[...], in_ref[cols, :])
        d_1 = (dy * c1_ref[:, cols]).astype(BF16)
        d_2 = (dy * c2_ref[:, cols]).astype(BF16)
        dpre_ref[:, cols] = d_1
        dpre_ref[:, cols_2] = d_2
        pre_t_ref[cols, :] = d_1.T
        pre_t_ref[cols_2, :] = d_2.T
        bias_ref[tiles + tile : tiles + tile + 1, :] = jnp.sum(d_1.astype(F32), axis=0, keepdims=True)
        bias_ref[2 * tiles + tile : 2 * tiles + tile + 1, :] = jnp.sum(d_2.astype(F32), axis=0, keepdims=True)
        dy_ref[:, cols] = dy * c3_ref[:, cols]
    copies += spread(pre_t_ref, hwy_box_ref, hwy_sems)
    for tile in range(tiles):
        cols = slice(tile * TILE, (tile + 1) * TILE)
        loads[tiles + tile].wait()
        dy = (dy_ref[:, cols] + dot_nt(dpre_ref[...], hwy_ref[cols, :])) * scale
        sums = jnp.zeros((1, TILE), F32)
        for place in range(STRIDE):
            alive = (segment * STRIDE + place < length).astype(F32)
            part = (dy * alive * slope_ref[place, :, cols].astype(F32)).astype(BF16)
            dconv_ref[place * rows : (place + 1) * rows, cols] = part
            sums = sums + jnp.sum(part.astype(F32), axis=0, keepdims=True)
        bias_ref[tile : tile + 1, :] = sums
    spans = tile_taps(filters)
    sums = {}
    for begin_tap in range(0, NWID, 2):
        begin = min(tile for tile, (low, high) in enumerate(spans) if low < begin_tap + 2 and high > begin_tap)
        part = dot_nt(
            dconv_ref[:, begin * TILE :],
            taps_ref[begin_tap * embed : (begin_tap + 2) * embed, begin * TILE :],
        )
        for tap in (begin_tap, begin_tap + 1):
            for place in range(STRIDE):
                spot = place + tap - LEAD
                key = (spot // STRIDE, spot % STRIDE)
                piece = part[
                    place * rows : (place + 1) * rows, (tap - begin_tap) * embed : (tap - begin_tap + 1) * embed
                ]
                sums[key] = sums[key] + piece if key in sums else piece
    total = jnp.zeros((sentences * span, embed), F32)
    out_ids = row_ids(sentences * span)
    out_sentence, out_time = out_ids // span, out_ids % span
    for place in range(STRIDE):
        plane = jnp.zeros((rows, embed), F32)
        for hop in (-1, 0, 1):
            if (hop, place) in sums:
                plane = plane + shift_rows(sums[hop, place], hop * sentences)
        plane = jnp.where(segment * STRIDE + place < length, plane, 0.0).astype(BF16)
        target = jnp.where(
            out_time % STRIDE == place, (out_time // STRIDE) * sentences + out_sentence, -1
        )
        total = total + dot(one_hot(sentences * span, rows, target), plane)
    for index in range(sentences):
        chars_ref[index] = total[index * span : (index + 1) * span].astype(BF16)
    share = span // groups
    for hop in range(1, groups):
        at = exact(here.along_place(hop) * share, share, 16)
        copies.append(
            remote(
                chars_ref.at[:, at], chars_box_ref.at[here.seq], chars_sems.at[0, hop], chars_sems.at[1, hop],
                (here.dp, here.along_place(hop)),
            )
        )
        copies[-1].start()
    chars_box_ref[here.seq] = chars_ref[:, exact(here.seq * share, share, 16), :]
    at = 0
    for tile, (low, high) in enumerate(spans):
        cols = slice(tile * TILE, (tile + 1) * TILE)
        size = (high - low) * embed
        conv_part_ref[at : at + size, :] = dot(
            cross_ref[low * embed : high * embed, :], dconv_ref[:, cols]
        ).astype(BF16)
        at += size
    conv_part_ref[at:, :] = bias_ref[...].astype(BF16)
    for copy in copies:
        copy.wait()


def sum_kernel(
    sizes, in_box_ref, hwy_box_ref, high_ref, pool_ref, conv_ref, rec_ref,
    in_out, hwy_out, conv_out, rec_out,
    in_full, hwy_full, in_got, hwy_got, in_outer, hwy_outer, in_inner, hwy_inner,
    conv_got, conv_half, conv_box, conv_low, conv_outer, conv_inner, rec_box, rec_low, rec_outer, rec_inner,
    in_sems, hwy_sems, conv_swap, conv_sems, rec_sems, small_sems,
):
    dps, groups = sizes
    here = Place(dps, groups)
    tiles = in_full.shape[0]
    greet([here.partner] + here.peers() + here.along())
    half = conv_half.shape[0]
    conv_copy = remote(
        conv_ref.at[exact((1 - here.core) * half, half, 16)], conv_got, conv_swap.at[0], conv_swap.at[1], here.partner
    )
    conv_copy.start()

    def spread(source, box, sends):
        share = box.shape[1]
        copies = []
        for hop in range(1, here.chips):
            at = exact(here.peer_chip(hop) * share, share, 16)
            copies.append(
                remote(source.at[at], box.at[hop - 1], sends.at[0, hop], sends.at[1, hop], here.peer(hop))
            )
            copies[-1].start()
        return copies

    rec_copies = spread(rec_ref, rec_box, rec_sems)

    def multiply(box_ref, rows_ref, full, got, sems, tile):
        share = got.shape[1]
        cols = slice(tile * TILE, (tile + 1) * TILE)
        total = dot(box_ref[0], rows_ref[0, :, cols])
        for chip in range(1, here.chips):
            total = total + dot(box_ref[chip], rows_ref[chip, :, cols])
        full[tile] = total.astype(BF16)
        copy = remote(
            full.at[tile, exact((1 - here.core) * share, share, 16)], got.at[tile],
            sems.at[0, tile], sems.at[1, tile], here.partner,
        )
        copy.start()
        return copy

    in_copies = [multiply(in_box_ref, high_ref, in_full, in_got, in_sems, tile) for tile in range(tiles)]
    hwy_copies = [multiply(hwy_box_ref, pool_ref, hwy_full, hwy_got, hwy_sems, tile) for tile in range(tiles)]

    conv_copy.wait_recv()
    mine = conv_ref[exact(here.core * half, half, 16), :]
    conv_half[...] = (mine.astype(F32) + conv_got[...].astype(F32)).astype(BF16)
    conv_copies = spread(conv_half, conv_box, conv_sems)

    def tile_sum(full, got, copies, tile):
        def found():
            copies[tile].wait_recv()
            share = got.shape[1]
            mine = full[tile, exact(here.core * share, share, 16), :]
            return mine.astype(F32) + got[tile].astype(F32)

        return found

    def box_sum(source, box, copies):
        def found():
            share = box.shape[1]
            total = source[exact(here.chip * share, share, 16), :].astype(F32)
            for hop, copy in enumerate(copies):
                copy.wait_recv()
                total = total + box[hop].astype(F32)
            return total

        return found

    def line_item(found, low, from_outer, from_inner, sem, keep=None):
        out_to_in = remote(low, from_outer, sem(2), sem(3), here.inner)
        across = remote(low, from_inner, sem(2), sem(4), here.inner)
        in_to_out = remote(low, from_inner, sem(5), sem(4), here.outer)

        def inward():
            low[...] = found().astype(BF16)

            @pl.when(here.has_outer)
            def _():
                out_to_in.wait_recv()
                low[...] = (low[...].astype(F32) + from_outer[...].astype(F32)).astype(BF16)

            @pl.when(here.middle)
            def _():
                across.start()

            @pl.when(jnp.logical_not(here.middle))
            def _():
                out_to_in.start()

        def outward():
            across.wait()

            @pl.when(here.middle)
            def _():
                low[...] = (low[...].astype(F32) + from_inner[...].astype(F32)).astype(BF16)

            @pl.when(jnp.logical_not(here.middle))
            def _():
                low[...] = from_inner[...]

            @pl.when(here.has_outer)
            def _():
                in_to_out.start()

            if keep is not None:
                keep()

        def finish():
            @pl.when(here.has_outer)
            def _():
                in_to_out.wait_send()

        return inward, outward, finish

    onward = []
    waits = []

    def share_out(out, low, sems):
        base = here.core * (out.shape[0] // 2)
        share = low.shape[0]
        at = exact(base + here.chip * share, share, 16)
        copies = [remote(low, out.at[at], sems.at[0, 0], sems.at[1, 0], here.partner)]
        for hop in range(1, here.chips):
            copies.append(remote(low, out.at[at], sems.at[0, hop], sems.at[1, hop], here.peer(hop)))
            source = (here.chip + here.chips - hop) % here.chips
            place = exact(base + source * share, share, 16)
            send_on = remote(out.at[place], out.at[place], sems.at[2, hop], sems.at[3, hop], here.partner)
            onward.append((copies[hop], send_on))
            waits.append(send_on.wait)
        waits.extend(copy.wait_send for copy in copies)
        waits.append(copies[0].wait_recv)

        def keep():
            out[at, :] = low[...]
            for copy in copies:
                copy.start()

        return keep

    def tile_items(full, got, copies, out, outer, inner, sems):
        return [
            line_item(
                tile_sum(full, got, copies, tile), out.at[tile], outer.at[tile], inner.at[tile],
                lambda index, tile=tile: sems.at[index, tile],
            )
            for tile in range(tiles)
        ]

    items = tile_items(in_full, in_got, in_copies, in_out, in_outer, in_inner, in_sems)
    items.append(
        line_item(
            box_sum(rec_ref, rec_box, rec_copies), rec_low, rec_outer, rec_inner,
            lambda index: small_sems.at[0, index], share_out(rec_out, rec_low, rec_sems.at[2:]),
        )
    )
    hwy_items = tile_items(hwy_full, hwy_got, hwy_copies, hwy_out, hwy_outer, hwy_inner, hwy_sems)
    items += hwy_items[:3]
    items.append(
        line_item(
            box_sum(conv_half, conv_box, conv_copies), conv_low, conv_outer, conv_inner,
            lambda index: small_sems.at[1, index], share_out(conv_out, conv_low, conv_sems.at[2:]),
        )
    )
    items += hwy_items[3:]
    depths = groups // 2
    for index in range(len(items) + 1 + 4 * (depths - 1)):
        if index < len(items):
            items[index][0]()
        for depth in range(depths):
            ready = index - 1 - 4 * depth
            if 0 <= ready < len(items):
                pl.when(here.depth == depth)(items[ready][1])
    for copy, send_on in onward:
        copy.wait_recv()
        send_on.start()
    for item in items:
        item[2]()
    for copy in in_copies + hwy_copies + [conv_copy] + rec_copies + conv_copies:
        copy.wait_send()
    for wait in waits:
        wait()


def finish_kernel(
    sizes, in_ref, hwy_ref, conv_ref, rec_ref,
    in_out, hwy_out, conv_out, rec_out, conv_bias_out, hwy_bias_out, in_bias_out, rec_bias_out,
):
    embed, filters, hidden = sizes
    tiles = in_ref.shape[0]
    for tile in range(tiles):
        at = slice(tile * TILE, (tile + 1) * TILE)
        in_out[at, :] = in_ref[tile].astype(F32).T
        hwy_out[at, :] = hwy_ref[tile].astype(F32).T
    spans = tile_taps(filters)
    starts = [0]
    for low, high in spans:
        starts.append(starts[-1] + (high - low) * embed)
    for width in range(1, NWID + 1):
        lead, first = (width - 1) // 2, width * (width - 1) // 2
        for tap in range(width):
            spot = LEAD - lead + tap
            pieces = []
            begin, end = (width - 1) * filters, width * filters
            while begin < end:
                tile = begin // TILE
                stop = min(end, (tile + 1) * TILE)
                row = starts[tile] + (spot - spans[tile][0]) * embed
                piece = conv_ref[row : row + embed, :].astype(F32)
                pieces.append(piece[:, begin - tile * TILE : stop - tile * TILE])
                begin = stop
            conv_out[first + tap] = pieces[0] if len(pieces) == 1 else jnp.concatenate(pieces, axis=1)
    rest = conv_ref[starts[-1] :, :].astype(F32)
    for tile in range(tiles):
        at = slice(tile * TILE, (tile + 1) * TILE)
        conv_bias_out[:, at] = rest[tile : tile + 1]
    for tile in range(2 * tiles):
        hwy_bias_out[:, tile * TILE : (tile + 1) * TILE] = rest[tiles + tile : tiles + tile + 1]
    half = rec_ref.shape[0] // 2
    rec_tiles = 3 * hidden // TILE
    for side in range(2):
        for tile in range(rec_tiles):
            row = side * half + tile * hidden
            at = slice(tile * TILE, (tile + 1) * TILE)
            rec_out[side, :, at] = rec_ref[row : row + hidden, :].astype(F32)
        row = side * half + rec_tiles * hidden
        rest = rec_ref[row : row + 16, :].astype(F32)
        for tile in range(rec_tiles):
            at = slice(tile * TILE, (tile + 1) * TILE)
            in_bias_out[side : side + 1, at] = rest[tile : tile + 1]
            rec_bias_out[side : side + 1, at] = rest[rec_tiles + tile : rec_tiles + tile + 1]


VMEM = pl.BlockSpec(memory_space=pltpu.VMEM)
SMEM = pl.BlockSpec(memory_space=pltpu.SMEM)
ANY = pl.BlockSpec(memory_space=pl.ANY)


def params(**more):
    return pltpu.CompilerParams(vmem_limit_bytes=VMEM_LIMIT, **more)


def shape(*dims, dtype=F32):
    return jax.ShapeDtypeStruct(dims, dtype)


def local(
    char_embeds, lengths, conv_weight, conv_bias, hwy_weight, hwy_bias, gru_in_weight, gru_in_bias,
    gru_rec_weight, gru_rec_bias, out_grad,
):
    groups = lax.axis_size("seq")
    dps = lax.axis_size("dp")
    seq_place, dp_place = lax.axis_index("seq"), lax.axis_index("dp")
    core = dp_place % 2
    sentences = char_embeds.shape[0] // groups
    span = char_embeds.shape[1] * groups
    segments = span // STRIDE
    embed, filters = conv_weight.shape[1:]
    channels = NWID * filters
    hidden = gru_rec_weight.shape[1]
    wide = 3 * hidden
    rows = sentences * segments
    height = max(8, 2 * sentences)
    pair = [(i, i ^ 1) for i in range(dps)]

    def joined(own):
        other = lax.ppermute(own, "dp", pair)
        return jnp.where(core == 0, jnp.stack([own, other]), jnp.stack([other, own]))

    chars = lax.all_to_all(char_embeds, "seq", 0, 1, tiled=True).reshape(sentences * span, embed)
    lens = lax.dynamic_slice(lengths, (seq_place * sentences,), (sentences,))
    lens_pair = joined(lens).reshape(-1)
    cot = lax.all_to_all(out_grad, "seq", 0, 1, tiled=True)
    kept = lax.dynamic_slice_in_dim(cot, core * hidden, hidden, 2)
    given = lax.ppermute(lax.dynamic_slice_in_dim(cot, (1 - core) * hidden, hidden, 2), "dp", pair)
    cot = jnp.where(core == 0, jnp.stack([kept, given]), jnp.stack([given, kept]))
    cot = cot.reshape(2 * rows, hidden)
    sizes = (sentences, span, segments, channels, embed, filters)
    pooled, high, slope, cross, c1, c2, c3, taps = pl.pallas_call(
        functools.partial(ahead_kernel, sizes),
        name="ahead",
        out_shape=[
            shape(rows, channels, dtype=BF16),
            shape(rows, channels, dtype=BF16),
            shape(STRIDE, rows, channels, dtype=BF16),
            shape(NWID * embed, STRIDE * rows, dtype=BF16),
            shape(rows, channels),
            shape(rows, channels),
            shape(rows, channels),
            shape(NWID * embed, channels, dtype=BF16),
        ],
        in_specs=[SMEM, VMEM, VMEM, VMEM, ANY, VMEM],
        out_specs=[VMEM] * 8,
        scratch_shapes=[
            pltpu.VMEM((channels, 2 * channels), BF16),
            pltpu.VMEM((STRIDE, rows, NWID * embed), BF16),
            pltpu.SemaphoreType.DMA,
        ],
        compiler_params=params(),
    )(lens, chars, conv_weight, conv_bias.astype(F32)[None], hwy_weight[0], hwy_bias.astype(F32))
    same_core = [[chip * 2 + which for chip in range(dps // 2)] for which in range(2)]
    high_all = lax.all_gather(high, "dp", axis_index_groups=same_core)
    pooled_all = lax.all_gather(pooled, "dp", axis_index_groups=same_core)
    high_pair = joined(high).reshape(2 * rows, channels)
    in_bias = lax.dynamic_slice(gru_in_bias.astype(F32)[None], (0, core * wide), (1, wide))
    rec_bias = lax.dynamic_slice(gru_rec_bias.astype(F32), (core, 0), (1, wide))
    steps = segments * height
    chips = dps // 2
    pad = 16 * chips
    rec_rows = wide // TILE * hidden + pad
    states, dgates, rec_part = pl.pallas_call(
        functools.partial(gru_kernel, (sentences, segments, hidden, height)),
        name="gru",
        out_shape=[
            shape(2 * rows, hidden, dtype=BF16),
            shape(2 * rows, wide, dtype=BF16),
            shape(rec_rows, TILE, dtype=BF16),
        ],
        in_specs=[SMEM, SMEM, VMEM, VMEM, ANY, VMEM, ANY, VMEM],
        out_specs=[VMEM] * 3,
        scratch_shapes=[
            pltpu.VMEM((channels, wide), BF16),
            pltpu.VMEM((hidden, wide), BF16),
            pltpu.VMEM((wide, hidden), BF16),
            pltpu.VMEM((steps, wide), F32),
            pltpu.VMEM((steps, 5 * hidden), F32),
            pltpu.VMEM((steps, hidden), F32),
            pltpu.VMEM((steps, 128), F32),
            pltpu.VMEM((pad, TILE), F32),
            pltpu.SemaphoreType.DMA((2,)),
        ],
        compiler_params=params(),
    )(core[None].astype(jnp.int32), lens_pair, high_pair, cot, gru_in_weight, in_bias, gru_rec_weight, rec_bias)

    def swapped(pair_rows):
        blocks = pair_rows.reshape((2, rows) + pair_rows.shape[1:])
        kept = lax.dynamic_index_in_dim(blocks, core, 0, False)
        given = lax.ppermute(lax.dynamic_index_in_dim(blocks, 1 - core, 0, False), "dp", pair)
        return jnp.where(
            core == 0, jnp.concatenate([kept, given], 1), jnp.concatenate([given, kept], 1)
        )

    encoded = swapped(states).reshape(sentences, segments, 2 * hidden)
    encoded = lax.all_to_all(encoded, "seq", 1, 0, tiled=True)
    tiles = channels // TILE
    in_share, hwy_share = 2 * wide // dps, 2 * channels // dps
    spans = tile_taps(filters)
    conv_rows = (sum(high - low for low, high in spans) + 1) * embed
    in_box, hwy_box, conv_part, chars_box = pl.pallas_call(
        functools.partial(back_kernel, sizes + (dps, groups)),
        name="back",
        out_shape=[
            shape(chips, 2 * in_share, rows, dtype=BF16),
            shape(chips, 2 * hwy_share, rows, dtype=BF16),
            shape(conv_rows, TILE, dtype=BF16),
            shape(groups, sentences, span // groups, embed, dtype=BF16),
        ],
        in_specs=[SMEM, VMEM, VMEM, VMEM, VMEM, VMEM, VMEM, VMEM, ANY, ANY],
        out_specs=[VMEM] * 4,
        scratch_shapes=[
            pltpu.VMEM((channels, 2 * wide), BF16),
            pltpu.VMEM((channels, 2 * channels), BF16),
            pltpu.VMEM((rows, wide), BF16),
            pltpu.VMEM((rows, 2 * wide), BF16),
            pltpu.VMEM((2 * wide, rows), BF16),
            pltpu.VMEM((rows, 2 * channels), BF16),
            pltpu.VMEM((2 * channels, rows), BF16),
            pltpu.VMEM((rows, channels), F32),
            pltpu.VMEM((STRIDE * rows, channels), BF16),
            pltpu.VMEM((embed, TILE), F32),
            pltpu.VMEM((sentences, span, embed), BF16),
            pltpu.SemaphoreType.DMA((2, tiles)),
            pltpu.SemaphoreType.DMA((2,)),
            pltpu.SemaphoreType.DMA((2, chips)),
            pltpu.SemaphoreType.DMA((2, chips)),
            pltpu.SemaphoreType.DMA((2, groups)),
        ],
        compiler_params=params(collective_id=1, has_side_effects=True),
    )(lens, dgates.reshape(2, rows, wide), c1, c2, c3, slope, cross, taps, gru_in_weight, hwy_weight[0])

    def slots(lead, share):
        return pltpu.VMEM((lead, share, TILE), BF16)

    conv_share, rec_share = conv_rows // dps, rec_rows // chips
    in_sum, hwy_sum, conv_sum, rec_sum = pl.pallas_call(
        functools.partial(sum_kernel, (dps, groups)),
        name="sums",
        out_shape=[
            shape(tiles, in_share, TILE, dtype=BF16),
            shape(tiles, hwy_share, TILE, dtype=BF16),
            shape(conv_rows, TILE, dtype=BF16),
            shape(2 * rec_rows, TILE, dtype=BF16),
        ],
        in_specs=[VMEM] * 6,
        out_specs=[VMEM] * 4,
        scratch_shapes=[
            slots(tiles, 2 * in_share), slots(tiles, 2 * hwy_share),
            slots(tiles, in_share), slots(tiles, hwy_share),
            slots(tiles, in_share), slots(tiles, hwy_share),
            slots(tiles, in_share), slots(tiles, hwy_share),
            pltpu.VMEM((conv_rows // 2, TILE), BF16),
            pltpu.VMEM((conv_rows // 2, TILE), BF16),
            slots(chips - 1, conv_share),
            pltpu.VMEM((conv_share, TILE), BF16),
            pltpu.VMEM((conv_share, TILE), BF16),
            pltpu.VMEM((conv_share, TILE), BF16),
            slots(chips - 1, rec_share),
            pltpu.VMEM((rec_share, TILE), BF16),
            pltpu.VMEM((rec_share, TILE), BF16),
            pltpu.VMEM((rec_share, TILE), BF16),
            pltpu.SemaphoreType.DMA((6, tiles)),
            pltpu.SemaphoreType.DMA((6, tiles)),
            pltpu.SemaphoreType.DMA((2,)),
            pltpu.SemaphoreType.DMA((6, chips)),
            pltpu.SemaphoreType.DMA((6, chips)),
            pltpu.SemaphoreType.DMA((2, 6)),
        ],
        compiler_params=params(collective_id=2, has_side_effects=True),
    )(in_box, hwy_box, high_all, pooled_all, conv_part, rec_part)
    in_grad, hwy_grad, conv_grad, rec_grad, conv_bias_grad, hwy_bias_grad, in_bias_grad, rec_bias_grad = pl.pallas_call(
        functools.partial(finish_kernel, (embed, filters, hidden)),
        name="finish",
        out_shape=[
            shape(channels, in_share),
            shape(channels, hwy_share),
            shape(*conv_weight.shape),
            shape(2, hidden, wide),
            shape(1, channels),
            shape(1, 2 * channels),
            shape(2, wide),
            shape(2, wide),
        ],
        in_specs=[VMEM] * 4,
        out_specs=[VMEM] * 8,
        compiler_params=params(),
    )(in_sum, hwy_sum, conv_sum, rec_sum)
    dchars = chars_box.reshape(groups * sentences, span // groups, embed).astype(F32)
    return (
        encoded, dchars, conv_grad, conv_bias_grad.reshape(-1), hwy_grad[None], hwy_bias_grad, in_grad,
        in_bias_grad.reshape(-1), rec_grad, rec_bias_grad,
    )


def solution(mesh):
    whole = P()
    split = P("dp", "seq", None)
    return jax.shard_map(
        local,
        mesh=mesh,
        in_specs=(split, P("dp")) + (whole,) * 8 + (split,),
        out_specs=(split, split, whole, whole, P(None, None, "dp"), whole, P(None, "dp"), whole, whole, whole),
        check_vma=False,
    )
```

```python
import functools
import math

import jax
import jax.numpy as jnp
from jax import lax
from jax.experimental import pallas as pl
from jax.experimental.pallas import tpu as pltpu
from jax.sharding import PartitionSpec as P

MESH = pl.DeviceIdType.MESH
NWID = 8
STRIDE = 5
LEAD = (NWID - 1) // 2
TILE = 256
SMALL_PARTS = 3
F32 = jnp.float32
BF16 = jnp.bfloat16
VMEM_LIMIT = 61 * 2**20


def tile_taps(filters):
    found = []
    for tile in range(NWID * filters // TILE):
        first_width = tile * TILE // filters + 1
        last_width = (tile * TILE + TILE - 1) // filters + 1
        low, high = NWID, 0
        for width in range(first_width, last_width + 1):
            lead = (width - 1) // 2
            low, high = min(low, LEAD - lead), max(high, LEAD - lead + width)
        found.append((low, high))
    return found


def lay_taps(weight_ref, taps_ref):
    _, filters, embed = weight_ref.shape
    taps_ref[...] = jnp.zeros_like(taps_ref)
    for width in range(1, NWID + 1):
        for tap in range(width):
            spot = LEAD - (width - 1) // 2 + tap
            taps_ref[(width - 1) * filters : width * filters, spot * embed : (spot + 1) * embed] = weight_ref[
                width * (width - 1) // 2 + tap
            ]


def sigmoid(value):
    return 0.5 * jnp.tanh(0.5 * value) + 0.5


def dot(left, right):
    return jnp.dot(left, right, preferred_element_type=F32)


def dot_nt(left, right):
    return lax.dot_general(left, right, (((1,), (1,)), ((), ())), preferred_element_type=F32)


def dot_tn(left, right):
    return lax.dot_general(left, right, (((0,), (0,)), ((), ())), preferred_element_type=F32)


def one_hot(rows, columns, target):
    places = lax.broadcasted_iota(jnp.int32, (rows, columns), 1)
    return jnp.where(places == target, 1.0, 0.0).astype(BF16)


def row_ids(rows):
    return lax.broadcasted_iota(jnp.int32, (rows, 1), 0)


def shift_rows(value, count):
    if count == 0:
        return value
    rows = value.shape[0]
    ids = row_ids(rows)
    moved = pltpu.roll(value, count % rows, axis=0)
    keep = ids >= count if count > 0 else ids < rows + count
    return jnp.where(keep, moved, 0.0)


class Place:
    def __init__(self, dps, groups):
        self.chips, self.groups = dps // 2, groups
        self.dp, self.seq = lax.axis_index("dp"), lax.axis_index("seq")
        self.chip, self.core = self.dp // 2, self.dp % 2
        self.partner = (self.chip * 2 + 1 - self.core, self.seq)
        half = groups // 2
        low = self.seq < half
        self.inner = (self.dp, jnp.where(low, self.seq + 1, self.seq - 1))
        self.outer = (self.dp, jnp.clip(jnp.where(low, self.seq - 1, self.seq + 1), 0, groups - 1))
        self.has_outer = (self.seq > 0) & (self.seq < groups - 1)
        self.depth = jnp.where(low, half - 1 - self.seq, self.seq - half)
        self.middle = self.depth == 0

    def peer_chip(self, hop):
        return (self.chip + hop) % self.chips

    def peer(self, hop):
        return (self.peer_chip(hop) * 2 + self.core, self.seq)

    def peers(self):
        return [self.peer(hop) for hop in range(1, self.chips)]

    def column(self):
        found = []
        for hop in range(self.groups):
            for flip in range(2):
                if hop or flip:
                    found.append((hop, flip, (self.chip * 2 + (self.core + flip) % 2, self.along_place(hop))))
        return found

    def grid(self, axis, hop):
        side = math.isqrt(self.chips)
        high, low = self.chip // side, self.chip % side
        if axis == 0:
            return (high + hop) % side * side + low
        return high * side + (low + hop) % side

    def along_place(self, hop):
        return (self.seq + hop) % self.groups

    def along(self):
        return [(self.dp, self.along_place(hop)) for hop in range(1, self.groups)]


def greet(devices):
    barrier = pltpu.get_barrier_semaphore()
    for device in devices:
        pl.semaphore_signal(barrier, inc=1, device_id=device, device_id_type=MESH)
    pl.semaphore_wait(barrier, len(devices))


def remote(src, dst, send, recv, device):
    return pltpu.make_async_remote_copy(
        src_ref=src, dst_ref=dst, send_sem=send, recv_sem=recv, device_id=device, device_id_type=MESH
    )


def exact(start, size, unit):
    return pl.ds(pl.multiple_of(start, unit), size)


def row_lengths(lens, which):
    found = jnp.zeros(which.shape, F32)
    for place, value in enumerate(lens):
        found = jnp.where(which == place, value, found)
    return found.astype(jnp.int32)


def own_lengths(lens_ref, first, count):
    spots = lax.broadcasted_iota(jnp.int32, (1, lens_ref.shape[1]), 1)
    return [
        jnp.sum(jnp.where(spots == first + place, lens_ref[0:1, :], 0.0), axis=1, keepdims=True)
        for place in range(count)
    ]


def head_kernel(
    sizes, lens_ref, chars_hbm, weight_ref, conv_bias_ref, hwy_hbm, hwy_bias_ref, cot_hbm, in_hbm, in_bias_ref,
    rec_hbm, rec_bias_ref,
    states_out, pool_all, high_all, slope_hbm, factor_hbm, cross_ref, taps_ref, pair_ref, rec_part_ref,
    lens_other, chars_box, hwy_slots, stack_ref, slope_slots, factor_slots, pooled_ref, high_ref, other_ref,
    in_ref, rec_ref, gates_ref, coef_ref, prior_ref, emit_ref, cot_box, states_ref, given_ref, bias_ref,
    hwy_sems, slope_sems, factor_sems, load_sems, swap_sems, chars_sems, cot_sems, states_sems, pool_sems, high_sems,
):
    sentences, span, segments, channels, embed, filters, hidden, height, dps, groups = sizes
    rows = sentences * segments
    tiles = channels // TILE
    wide = 3 * hidden
    here = Place(dps, groups)
    waits = []

    def columns(tile):
        return [(hwy_hbm.at[:, pl.ds(side * channels + tile * TILE, TILE)], side) for side in range(2)]

    hwy_loads = {}

    def hwy_start(tile):
        if tile < tiles:
            slot = tile % hwy_slots.shape[0]
            hwy_loads[tile] = [
                pltpu.make_async_copy(source, hwy_slots.at[slot, side], hwy_sems.at[slot, side])
                for source, side in columns(tile)
            ]
            for load in hwy_loads[tile]:
                load.start()

    for tile in range(hwy_slots.shape[0]):
        hwy_start(tile)
    loads = [
        pltpu.make_async_copy(in_hbm.at[:, exact(here.core * wide, wide, 128)], in_ref, load_sems.at[0]),
        pltpu.make_async_copy(rec_hbm.at[here.core], rec_ref, load_sems.at[1]),
    ]
    greet([device for _, _, device in here.column()] + here.peers())
    swap_lens = remote(lens_ref, lens_other, swap_sems.at[0], swap_sems.at[1], here.partner)
    swap_lens.start()
    share = span // groups
    chars_copies = []
    for hop in range(1, groups):
        chars_copies.append(
            remote(
                chars_hbm.at[exact(here.along_place(hop) * sentences, sentences, 1)], chars_box.at[here.seq],
                chars_sems.at[0, hop], chars_sems.at[1, hop], (here.dp, here.along_place(hop)),
            )
        )
    chars_copies.append(
        pltpu.make_async_copy(
            chars_hbm.at[exact(here.seq * sentences, sentences, 1)], chars_box.at[here.seq], chars_sems.at[0, 0]
        )
    )
    for copy in chars_copies:
        copy.start()
    cot_copies = []
    for hop, flip, device in here.column():
        side = (here.core + flip) % 2
        cot_copies.append(
            remote(
                cot_hbm.at[
                    exact(here.along_place(hop) * sentences, sentences, 1), :, exact(side * hidden, hidden, 128)
                ],
                cot_box.at[here.core, here.seq], cot_sems.at[0, 2 * hop + flip], cot_sems.at[1, 2 * hop + flip], device,
            )
        )
    cot_copies.append(
        pltpu.make_async_copy(
            cot_hbm.at[exact(here.seq * sentences, sentences, 1), :, exact(here.core * hidden, hidden, 128)],
            cot_box.at[here.core, here.seq], cot_sems.at[0, 0],
        )
    )
    for copy in cot_copies:
        copy.start()
    for load in loads:
        load.start()
    lay_taps(weight_ref, taps_ref)
    ids = row_ids(rows)
    segment, sentence = ids // sentences, ids % sentences
    lens = own_lengths(lens_ref, here.seq * sentences, sentences)
    length = row_lengths(lens, sentence)
    live = []
    planes = {}
    for copy in chars_copies:
        copy.wait()
    chars = chars_box[...].reshape(sentences * span, embed)
    for place in range(STRIDE):
        time = segment * STRIDE + place
        alive = time < length
        live.append(alive.astype(F32))
        target = jnp.where(alive, (time // share * sentences + sentence) * share + time % share, -1)
        plane = dot(one_hot(rows, sentences * span, target), chars)
        for hop in (-1, 0, 1):
            planes[hop, place] = shift_rows(plane, -hop * sentences).astype(BF16)
    for place in range(STRIDE):
        for tap in range(NWID):
            spot = place + tap - LEAD
            part = planes[spot // STRIDE, spot % STRIDE]
            stack_ref[place, :, tap * embed : (tap + 1) * embed] = part
            cross_ref[tap * embed : (tap + 1) * embed, place * rows : (place + 1) * rows] = part.T
    count = jnp.clip(length - STRIDE * segment, 0, STRIDE).astype(F32)
    scale = 1.0 / jnp.maximum(count, 1.0)

    def stored(slots, out, sems, tile, copies):
        slot = tile % slots.shape[0]
        if tile >= slots.shape[0]:
            copies[tile - slots.shape[0]].wait()
        copies.append(pltpu.make_async_copy(slots.at[slot], out.at[tile], sems.at[slot]))
        return slots.at[slot]

    slope_copies, factor_copies = [], []
    for tile, (low, high) in enumerate(tile_taps(filters)):
        cols = slice(tile * TILE, (tile + 1) * TILE)
        total = jnp.zeros((rows, TILE), F32)
        slot = stored(slope_slots, slope_hbm, slope_sems, tile, slope_copies)
        for place in range(STRIDE):
            pre = dot_nt(
                stack_ref[place, :, low * embed : high * embed],
                taps_ref[cols, low * embed : high * embed],
            ) + conv_bias_ref[:, cols]
            gate = sigmoid(pre)
            act = pre * gate
            total = total + act * live[place]
            slot[place] = (gate + act * (1.0 - gate)).astype(BF16)
        slope_copies[tile].start()
        pooled_ref[:, cols] = (total * scale).astype(BF16)

    def gather(source, out, sems):
        side = math.isqrt(here.chips)
        half = rows // 2
        stay = pltpu.make_async_copy(source, out.at[here.chip], sems.at[0, 0])
        firsts, seconds, onwards = [], [], []
        flag = 1
        for axis in range(2):
            at = pl.ds(axis * half, half)
            for hop in range(1, side):
                chip = here.grid(axis, hop)
                firsts.append(
                    remote(
                        source.at[at], out.at[here.chip, at], sems.at[0, flag], sems.at[1, flag],
                        (chip * 2 + here.core, here.seq),
                    )
                )
                came = here.grid(axis, side - hop)
                flag += 1
                for hop_2 in range(1, side):
                    chip = here.grid(1 - axis, hop_2)
                    onwards.append(
                        (
                            firsts[-1],
                            remote(
                                out.at[came, at], out.at[came, at], sems.at[0, flag], sems.at[1, flag],
                                (chip * 2 + here.core, here.seq),
                            ),
                        )
                    )
                    flag += 1
            for hop in range(1, side):
                chip = here.grid(1 - axis, hop)
                seconds.append(
                    remote(
                        source.at[at], out.at[here.chip, at], sems.at[0, flag], sems.at[1, flag],
                        (chip * 2 + here.core, here.seq),
                    )
                )
                flag += 1
        for copy in [stay] + firsts + seconds:
            copy.start()
        waits.extend([stay.wait] + [copy.wait_send for copy in firsts] + [copy.wait for copy in seconds])
        return onwards

    pool_onwards = gather(pooled_ref, pool_all, pool_sems)
    for tile in range(tiles):
        cols = slice(tile * TILE, (tile + 1) * TILE)
        cols_2 = slice(channels + tile * TILE, channels + (tile + 1) * TILE)
        for load in hwy_loads[tile]:
            load.wait()
        slot = tile % hwy_slots.shape[0]
        pre_1 = dot(pooled_ref[...], hwy_slots[slot, 0]) + hwy_bias_ref[:, cols]
        pre_2 = dot(pooled_ref[...], hwy_slots[slot, 1]) + hwy_bias_ref[:, cols_2]
        hwy_start(tile + hwy_slots.shape[0])
        layer_in = pooled_ref[:, cols].astype(F32)
        gate, inner = sigmoid(pre_2), sigmoid(pre_1)
        act = pre_1 * inner
        off = 1.0 - gate
        high_ref[:, cols] = (gate * act + off * layer_in).astype(BF16)
        factor = stored(factor_slots, factor_hbm, factor_sems, tile, factor_copies)
        factor[0] = gate * (inner + act * (1.0 - inner))
        factor[1] = (act - layer_in) * gate * off
        factor[2] = off
        factor_copies[tile].start()
    swap = remote(high_ref, other_ref, swap_sems.at[2], swap_sems.at[3], here.partner)
    swap.start()
    high_onwards = gather(high_ref, high_all, high_sems)
    for copies, slots in ((slope_copies, slope_slots), (factor_copies, factor_slots)):
        for copy in copies[-slots.shape[0] :]:
            copy.wait()

    steps = segments * height
    ids = row_ids(steps)
    step, lane = ids // height, ids % height
    segment = jnp.where(here.core == 0, step, segments - 1 - step)
    whose, sentence = lane // sentences, lane % sentences
    real = lane < 2 * sentences
    order = segment * sentences + sentence
    mine = real & (whose == here.core)
    theirs = real & (whose != here.core)
    take_own = one_hot(steps, rows, jnp.where(mine, order, -1))
    take_other = one_hot(steps, rows, jnp.where(theirs, order, -1))
    part = segments // groups
    order_2 = ((whose * groups + segment // part) * sentences + sentence) * part + segment % part
    pick = one_hot(steps, 2 * rows, jnp.where(real, order_2, -1))
    swap_lens.wait()
    lens_2 = own_lengths(lens_other, here.seq * sentences, sentences)
    length = jnp.where(mine, row_lengths(lens, sentence), row_lengths(lens_2, sentence))
    live = real & (segment < (length + STRIDE - 1) // STRIDE)
    emit_ref[...] = jnp.broadcast_to(live.astype(F32), (steps, 128))
    own_part = dot(take_own, high_ref[...])
    swap.wait()
    stepped = (own_part + dot(take_other, other_ref[...])).astype(BF16)
    loads[0].wait()
    gates_ref[...] = dot(stepped, in_ref[...]) + in_bias_ref[pl.ds(here.core, 1), :]
    loads[1].wait()
    rec_bias = rec_bias_ref[pl.ds(here.core, 1), :]

    def ahead(index, state):
        at = pl.ds(pl.multiple_of(index * height, height), height)
        q = dot(state.astype(BF16), rec_ref[...]) + rec_bias
        gates = gates_ref[at, :]
        alive = emit_ref[at, 0:1] > 0.0
        reset = sigmoid(gates[:, :hidden] + q[:, :hidden])
        update = sigmoid(gates[:, hidden : 2 * hidden] + q[:, hidden : 2 * hidden])
        q_n = q[:, 2 * hidden :]
        fresh = jnp.tanh(gates[:, 2 * hidden :] + reset * q_n)
        keep = jnp.where(alive, update, 1.0)
        move = jnp.where(alive, 1.0 - update, 0.0)
        after = move * fresh + keep * state
        prior_ref[at, :] = state
        slope = move * (1.0 - fresh * fresh)
        slope_r = slope * reset
        coef_ref[at, :hidden] = slope_r * q_n * (1.0 - reset)
        coef_ref[at, hidden : 2 * hidden] = (state - fresh) * update * move
        coef_ref[at, 2 * hidden : wide] = slope_r
        coef_ref[at, wide : wide + hidden] = slope
        coef_ref[at, wide + hidden :] = keep
        gates_ref[at, :hidden] = jnp.where(alive, after, 0.0)
        return after

    lax.fori_loop(0, segments, ahead, jnp.zeros((height, hidden), F32), unroll=2)
    for came, onward in pool_onwards + high_onwards:
        came.wait_recv()
        onward.start()
        waits.append(onward.wait)
    states = dot_tn(pick, gates_ref[:, :hidden].astype(BF16)).astype(BF16)
    block = rows // groups
    for whose in range(2):
        for place in range(groups):
            at = (whose * groups + place) * block
            states_ref[whose, place] = states[at : at + block].reshape(sentences, part, hidden)
    seat = (exact(here.seq * sentences, sentences, 1), slice(None), exact(here.core * hidden, hidden, 128))
    for hop, flip, device in here.column():
        copy = remote(
            states_ref.at[(here.core + flip) % 2, here.along_place(hop)], states_out.at[seat],
            states_sems.at[0, 2 * hop + flip], states_sems.at[1, 2 * hop + flip], device,
        )
        copy.start()
        waits.append(copy.wait)
    stay = pltpu.make_async_copy(states_ref.at[here.core, here.seq], states_out.at[seat], states_sems.at[0, 0])
    stay.start()
    waits.append(stay.wait)
    for copy in cot_copies:
        copy.wait()
    cot = cot_box[...].reshape(2 * rows, hidden)
    gates_ref[:, :hidden] = dot(pick, cot) * emit_ref[:, 0:1]
    turned = (slice(0, wide), slice(0, hidden))
    in_ref[turned] = rec_ref[...].T

    def back(index, carried):
        at = pl.ds(pl.multiple_of((segments - 1 - index) * height, height), height)
        total = carried + gates_ref[at, :hidden]
        d_r = total * coef_ref[at, :hidden]
        d_z = total * coef_ref[at, hidden : 2 * hidden]
        d_q = total * coef_ref[at, 2 * hidden : wide]
        d_n = total * coef_ref[at, wide : wide + hidden]
        kept = total * coef_ref[at, wide + hidden :]
        coef_ref[at, :hidden] = d_r
        coef_ref[at, hidden : 2 * hidden] = d_z
        coef_ref[at, 2 * hidden : wide] = d_q
        coef_ref[at, wide : wide + hidden] = d_n
        low = jnp.concatenate([d_r, d_z, d_q], axis=1).astype(BF16)
        return kept + dot(low, in_ref[turned])

    lax.fori_loop(0, segments, back, jnp.zeros((height, hidden), F32), unroll=2)
    recur = coef_ref[:, :wide].astype(BF16)
    fresh = coef_ref[:, wide : wide + hidden].astype(BF16)
    given_ref[:, : 2 * hidden] = dot_tn(take_other, recur[:, : 2 * hidden]).astype(BF16)
    given_ref[:, 2 * hidden :] = dot_tn(take_other, fresh).astype(BF16)
    seat = (slice(None), exact(here.core * wide, wide, 128))
    give = remote(given_ref, pair_ref.at[seat], swap_sems.at[4], swap_sems.at[5], here.partner)
    give.start()
    waits.append(give.wait)
    pair_ref[:, exact(here.core * wide, 2 * hidden, 128)] = dot_tn(take_own, recur[:, : 2 * hidden]).astype(BF16)
    pair_ref[:, exact(here.core * wide + 2 * hidden, hidden, 128)] = dot_tn(take_own, fresh).astype(BF16)
    prior = prior_ref[...].astype(BF16)
    sums = jnp.sum(recur.astype(F32), axis=0, keepdims=True)
    sums_n = jnp.sum(fresh.astype(F32), axis=0, keepdims=True)
    rec_tiles = wide // TILE
    bias_ref[...] = jnp.zeros_like(bias_ref)
    for tile in range(rec_tiles):
        cols = slice(tile * TILE, (tile + 1) * TILE)
        rec_part_ref[tile * hidden : (tile + 1) * hidden, :] = dot_tn(prior, recur[:, cols]).astype(BF16)
        if tile * TILE < 2 * hidden:
            bias_ref[tile : tile + 1, :] = sums[:, cols]
        else:
            bias_ref[tile : tile + 1, :] = sums_n[:, tile * TILE - 2 * hidden : (tile + 1) * TILE - 2 * hidden]
        bias_ref[rec_tiles + tile : rec_tiles + tile + 1, :] = sums[:, cols]
    rec_part_ref[rec_tiles * hidden :, :] = bias_ref[...].astype(BF16)
    for wait in waits:
        wait()


class Ring:
    def __init__(self, slots, sems, loads):
        self.slots, self.sems, self.loads = slots, sems, loads
        self.depth = slots.shape[0]
        self.copies = {}

    def start(self, index):
        if index < len(self.loads):
            source, place = self.loads[index]
            slot = index % self.depth
            self.copies[index] = pltpu.make_async_copy(source, place(self.slots.at[slot]), self.sems.at[slot])
            self.copies[index].start()

    def begin(self):
        for index in range(self.depth):
            self.start(index)

    def take(self, index):
        self.copies[index].wait()
        return self.slots.at[index % self.depth]

    def done(self, index):
        self.start(index + self.depth)


def tail_kernel(
    sizes, lens_ref, pair_hbm, factor_hbm, slope_hbm, cross_hbm, taps_hbm, in_hbm, hwy_hbm, high_hbm, pool_hbm, rec_hbm,
    in_low, hwy_low, conv_out, rec_out, chars_box,
    weight_slots, factor_slots, slope_slots, rows_slots, full_slots,
    pair_ref, gates_t_ref, dpre_ref, pre_t_ref, dy_ref, dconv_ref, bias_ref, chars_ref, cross_ref, taps_ref,
    in_box, hwy_box, in_got, hwy_got, in_outer, hwy_outer, in_inner, hwy_inner,
    conv_part, conv_got, conv_half, conv_box, conv_low, conv_outer, conv_inner, rec_box, rec_low, rec_outer, rec_inner,
    weight_sems, factor_sems, slope_sems, rows_sems, load_sems, in_spread, hwy_spread, chars_sems,
    in_sems, hwy_sems, conv_swap, conv_sems, rec_sems, conv_line, rec_line, conv_share, rec_share,
):
    sentences, span, segments, channels, embed, filters, dps, groups = sizes
    rows = sentences * segments
    tiles = channels // TILE
    wide = pair_hbm.shape[1] // 2
    here = Place(dps, groups)

    def tile_at(tile):
        return pl.ds(tile * TILE, TILE)

    weights = Ring(
        weight_slots, weight_sems,
        [(in_hbm.at[tile_at(tile)], lambda slot: slot.at[:, pl.ds(0, 2 * wide)]) for tile in range(tiles)]
        + [(hwy_hbm.at[tile_at(tile)], lambda slot: slot) for tile in range(tiles)],
    )
    factors = Ring(factor_slots, factor_sems, [(factor_hbm.at[tile], lambda slot: slot) for tile in range(tiles)])
    slopes = Ring(slope_slots, slope_sems, [(slope_hbm.at[tile], lambda slot: slot) for tile in range(tiles)])
    gathered = Ring(
        rows_slots, rows_sems,
        [(source.at[:, :, tile_at(tile)], lambda slot: slot) for source in (high_hbm, pool_hbm) for tile in range(tiles)],
    )
    pair_load = pltpu.make_async_copy(pair_hbm, pair_ref, load_sems.at[0])
    pair_load.start()
    weights.begin()
    factors.begin()
    slopes.begin()
    taps_load = pltpu.make_async_copy(taps_hbm, taps_ref, load_sems.at[1])
    cross_load = pltpu.make_async_copy(cross_hbm, cross_ref, load_sems.at[2])
    greet([here.partner] + here.peers() + here.along())
    taps_load.start()
    cross_load.start()
    rec_load = pltpu.make_async_copy(
        rec_hbm.at[exact(here.chip * rec_low.shape[0], rec_low.shape[0], 16)], rec_low, load_sems.at[3]
    )
    rec_load.start()
    gathered.begin()
    ids = row_ids(rows)
    segment, sentence = ids // sentences, ids % sentences
    length = row_lengths(own_lengths(lens_ref, here.seq * sentences, sentences), sentence)
    count = jnp.clip(length - STRIDE * segment, 0, STRIDE).astype(F32)
    scale = 1.0 / jnp.maximum(count, 1.0)
    bias_ref[...] = jnp.zeros_like(bias_ref)
    pair_load.wait()
    sent = []
    waits = []
    for side in range(2):
        gates_t_ref[side * wide : (side + 1) * wide, :] = pair_ref[:, side * wide : (side + 1) * wide].T

    def spread(source, box, sends):
        share = box.shape[1]
        copies = []
        for hop in range(1, here.chips):
            at = exact(here.peer_chip(hop) * share, share, 16)
            copies.append(
                remote(source.at[at], box.at[hop - 1], sends.at[0, hop], sends.at[1, hop], here.peer(hop))
            )
            copies[-1].start()
        sent.extend(copies)
        return copies

    in_spread_copies = spread(gates_t_ref, in_box, in_spread)
    for tile in range(tiles):
        cols = slice(tile * TILE, (tile + 1) * TILE)
        cols_2 = slice(channels + tile * TILE, channels + (tile + 1) * TILE)
        weight = weights.take(tile)
        dy = dot_nt(pair_ref[...], weight[:, : 2 * wide])
        weights.done(tile)
        factor = factors.take(tile)
        d_1 = (dy * factor[0]).astype(BF16)
        d_2 = (dy * factor[1]).astype(BF16)
        dy_ref[:, cols] = dy * factor[2]
        factors.done(tile)
        dpre_ref[:, cols] = d_1
        dpre_ref[:, cols_2] = d_2
        pre_t_ref[cols, :] = d_1.T
        pre_t_ref[cols_2, :] = d_2.T
        bias_ref[tiles + tile : tiles + tile + 1, :] = jnp.sum(d_1.astype(F32), axis=0, keepdims=True)
        bias_ref[2 * tiles + tile : 2 * tiles + tile + 1, :] = jnp.sum(d_2.astype(F32), axis=0, keepdims=True)
    hwy_spread_copies = spread(pre_t_ref, hwy_box, hwy_spread)
    rec_copies = spread(rec_hbm, rec_box, rec_sems)
    for tile in range(tiles):
        cols = slice(tile * TILE, (tile + 1) * TILE)
        weight = weights.take(tiles + tile)
        dy = (dy_ref[:, cols] + dot_nt(dpre_ref[...], weight[...])) * scale
        weights.done(tiles + tile)
        slope = slopes.take(tile)
        sums = jnp.zeros((1, TILE), F32)
        for place in range(STRIDE):
            alive = (segment * STRIDE + place < length).astype(F32)
            part = (dy * alive * slope[place].astype(F32)).astype(BF16)
            dconv_ref[place * rows : (place + 1) * rows, cols] = part
            sums = sums + jnp.sum(part.astype(F32), axis=0, keepdims=True)
        slopes.done(tile)
        bias_ref[tile : tile + 1, :] = sums
    spans = tile_taps(filters)
    starts = [0]
    for low, high in spans:
        starts.append(starts[-1] + (high - low) * embed)
    sums = {}
    half = conv_half.shape[0]
    conv_copy = remote(
        conv_part.at[exact((1 - here.core) * half, half, 16)], conv_got, conv_swap.at[0], conv_swap.at[1], here.partner
    )
    conv_copies = []

    def chars_part(begin_tap):
        begin = min(tile for tile, (low, high) in enumerate(spans) if low < begin_tap + 2 and high > begin_tap)
        part = dot(
            dconv_ref[:, begin * TILE :],
            taps_ref[begin * TILE :, begin_tap * embed : (begin_tap + 2) * embed],
        )
        for tap in (begin_tap, begin_tap + 1):
            for place in range(STRIDE):
                spot = place + tap - LEAD
                key = (spot // STRIDE, spot % STRIDE)
                piece = part[
                    place * rows : (place + 1) * rows, (tap - begin_tap) * embed : (tap - begin_tap + 1) * embed
                ]
                sums[key] = sums[key] + piece if key in sums else piece

    def chars_end():
        total = jnp.zeros((sentences * span, embed), F32)
        out_ids = row_ids(sentences * span)
        out_sentence, out_time = out_ids // span, out_ids % span
        for place in range(STRIDE):
            plane = jnp.zeros((rows, embed), F32)
            for hop in (-1, 0, 1):
                if (hop, place) in sums:
                    plane = plane + shift_rows(sums[hop, place], hop * sentences)
            plane = jnp.where(segment * STRIDE + place < length, plane, 0.0).astype(BF16)
            target = jnp.where(
                out_time % STRIDE == place, (out_time // STRIDE) * sentences + out_sentence, -1
            )
            total = total + dot(one_hot(sentences * span, rows, target), plane)
        for index in range(sentences):
            chars_ref[index] = total[index * span : (index + 1) * span].astype(BF16)
        share = span // groups
        for hop in range(1, groups):
            at = exact(here.along_place(hop) * share, share, 16)
            copy = remote(
                chars_ref.at[:, at], chars_box.at[here.seq], chars_sems.at[0, hop], chars_sems.at[1, hop],
                (here.dp, here.along_place(hop)),
            )
            copy.start()
            waits.append(copy.wait)
        chars_box[here.seq] = chars_ref[:, exact(here.seq * share, share, 16), :]

    def taps_part(tile):
        low, high = spans[tile]
        conv_part[starts[tile] : starts[tile + 1], :] = dot(
            cross_ref[low * embed : high * embed, :], dconv_ref[:, tile * TILE : (tile + 1) * TILE]
        ).astype(BF16)

    def taps_end():
        conv_part[starts[-1] :, :] = bias_ref[...].astype(BF16)
        conv_copy.start()
        sent.append(conv_copy)

    def conv_send():
        conv_copy.wait_recv()
        mine = conv_part[exact(here.core * half, half, 16), :]
        conv_half[...] = (mine.astype(F32) + conv_got[...].astype(F32)).astype(BF16)
        conv_copies.extend(spread(conv_half, conv_box, conv_sems))
        share = conv_low.shape[0]
        conv_low[...] = conv_half[exact(here.chip * share, share, 16), :]

    tasks = [cross_load.wait]
    tasks += [functools.partial(taps_part, tile) for tile in range(tiles)]
    tasks += [taps_end, taps_load.wait]
    tasks += [functools.partial(chars_part, begin_tap) for begin_tap in range(0, NWID, 2)]
    tasks += [conv_send, chars_end]

    def multiply(box, source, low, got, sems, tile, turn, earlier):
        share = got.shape[1]
        full = full_slots.at[turn % full_slots.shape[0], pl.ds(0, 2 * share)]
        if turn >= full_slots.shape[0]:
            earlier[turn - full_slots.shape[0]].wait_send()
        block = gathered.take(turn)
        total = dot(source[exact(here.chip * 2 * share, 2 * share, 16), :], block[here.chip])
        for hop in range(1, here.chips):
            chip = (here.chip + here.chips - hop) % here.chips
            total = total + dot(box[hop - 1], block[chip])
        gathered.done(turn)
        full[...] = total.astype(BF16)
        low[tile] = full[exact(here.core * share, share, 16), :]
        copy = remote(
            full.at[exact((1 - here.core) * share, share, 16)], got.at[tile],
            sems.at[0, tile], sems.at[1, tile], here.partner,
        )
        copy.start()
        earlier.append(copy)

    halves = []
    for copy in in_spread_copies:
        copy.wait_recv()
    for tile in range(tiles):
        multiply(in_box, gates_t_ref, in_low, in_got, in_sems, tile, tile, halves)

    def line_item(found, low, from_outer, from_inner, sem, keep=None):
        out_to_in = remote(low, from_outer, sem(2), sem(3), here.inner)
        across = remote(low, from_inner, sem(2), sem(4), here.inner)
        in_to_out = remote(low, from_inner, sem(5), sem(4), here.outer)

        def inward():
            low[...] = found().astype(BF16)

            @pl.when(here.has_outer)
            def _():
                out_to_in.wait_recv()
                low[...] = (low[...].astype(F32) + from_outer[...].astype(F32)).astype(BF16)

            @pl.when(here.middle)
            def _():
                across.start()

            @pl.when(jnp.logical_not(here.middle))
            def _():
                out_to_in.start()

        def outward():
            across.wait()

            @pl.when(here.middle)
            def _():
                low[...] = (low[...].astype(F32) + from_inner[...].astype(F32)).astype(BF16)

            @pl.when(jnp.logical_not(here.middle))
            def _():
                low[...] = from_inner[...]

            @pl.when(here.has_outer)
            def _():
                in_to_out.start()

            if keep is not None:
                keep()

        def finish():
            @pl.when(here.has_outer)
            def _():
                in_to_out.wait_send()

        return inward, outward, finish

    onward = []

    def share_out(out, low, begin, size, sems):
        base = here.core * (out.shape[0] // 2) + begin
        share = low.shape[0]
        piece = low.at[pl.ds(begin, size)]
        at = exact(base + here.chip * share, size, 16)
        stay = pltpu.make_async_copy(piece, out.at[at], sems.at[2, 0])
        copies = [remote(piece, out.at[at], sems.at[0, 0], sems.at[1, 0], here.partner)]
        for hop in range(1, here.chips):
            copies.append(remote(piece, out.at[at], sems.at[0, hop], sems.at[1, hop], here.peer(hop)))
            source = (here.chip + here.chips - hop) % here.chips
            place = exact(base + source * share, size, 16)
            send_on = remote(out.at[place], out.at[place], sems.at[2, hop], sems.at[3, hop], here.partner)
            onward.append((copies[hop], send_on))
            waits.append(send_on.wait)
        waits.extend(copy.wait_send for copy in copies)
        waits.append(copies[0].wait_recv)
        waits.append(stay.wait)

        def keep():
            stay.start()
            for copy in copies:
                copy.start()

        return keep

    def tile_items(low, got, turns, outer, inner, sems):
        def found(tile):
            halves[turns + tile].wait_recv()
            return low[tile].astype(F32) + got[tile].astype(F32)

        return [
            line_item(
                functools.partial(found, tile), low.at[tile], outer.at[tile], inner.at[tile],
                lambda index, tile=tile: sems.at[index, tile],
            )
            for tile in range(tiles)
        ]

    def small_items(low, box, copies, outer, inner, line_sems, share_sems, out, ready):
        found_items = []
        size = low.shape[0] // 16
        cuts = [size * part // SMALL_PARTS * 16 for part in range(SMALL_PARTS + 1)]

        def found(part):
            if part == 0:
                ready()
                for copy in copies:
                    copy.wait_recv()
            at = slice(cuts[part], cuts[part + 1])
            total = low[at, :].astype(F32)
            for hop in range(here.chips - 1):
                total = total + box[hop, at, :].astype(F32)
            return total

        for part in range(SMALL_PARTS):
            at = pl.ds(cuts[part], cuts[part + 1] - cuts[part])
            found_items.append(
                line_item(
                    functools.partial(found, part), low.at[at], outer.at[at], inner.at[at],
                    lambda index, part=part: line_sems.at[part, index],
                    share_out(out, low, cuts[part], cuts[part + 1] - cuts[part], share_sems.at[part]),
                )
            )
        return found_items

    def later():
        for copy in hwy_spread_copies:
            copy.wait_recv()
        for tile in range(tiles):
            multiply(hwy_box, pre_t_ref, hwy_low, hwy_got, hwy_sems, tile, tiles + tile, halves)

    items = tile_items(in_low, in_got, 0, in_outer, in_inner, in_sems)
    hwy_items = tile_items(hwy_low, hwy_got, tiles, hwy_outer, hwy_inner, hwy_sems)
    rec_items = small_items(
        rec_low, rec_box, rec_copies, rec_outer, rec_inner, rec_line, rec_share, rec_out, rec_load.wait
    )
    conv_items = small_items(
        conv_low, conv_box, conv_copies, conv_outer, conv_inner, conv_line, conv_share, conv_out, lambda: None
    )
    items += hwy_items[:2] + rec_items + hwy_items[2:3] + conv_items + hwy_items[3:]
    depths = groups // 2
    for index in range(len(items) + 1 + 4 * (depths - 1)):
        if index == tiles:
            later()
        if index < len(items):
            items[index][0]()
        for task in tasks[2 * index : 2 * index + 2]:
            task()
        for depth in range(depths):
            ready = index - 1 - 4 * depth
            if 0 <= ready < len(items):
                pl.when(here.depth == depth)(items[ready][1])
    for copy, send_on in onward:
        copy.wait_recv()
        send_on.start()
    for item in items:
        item[2]()
    for copy in sent:
        copy.wait_send()
    for copy in halves[-full_slots.shape[0] :]:
        copy.wait_send()
    for wait in waits:
        wait()


def finish_kernel(
    sizes, in_ref, hwy_ref, conv_ref, rec_ref,
    in_out, hwy_out, conv_out, rec_out, conv_bias_out, hwy_bias_out, in_bias_out, rec_bias_out,
):
    embed, filters, hidden = sizes
    tiles = in_ref.shape[0]
    for tile in range(tiles):
        at = slice(tile * TILE, (tile + 1) * TILE)
        in_out[at, :] = in_ref[tile].astype(F32).T
        hwy_out[:, at] = hwy_ref[tile].astype(F32)
    spans = tile_taps(filters)
    starts = [0]
    for low, high in spans:
        starts.append(starts[-1] + (high - low) * embed)
    for width in range(1, NWID + 1):
        lead, first = (width - 1) // 2, width * (width - 1) // 2
        for tap in range(width):
            spot = LEAD - lead + tap
            begin, end = (width - 1) * filters, width * filters
            while begin < end:
                tile = begin // TILE
                stop = min(end, (tile + 1) * TILE)
                row = starts[tile] + (spot - spans[tile][0]) * embed
                piece = conv_ref[row : row + embed, :].astype(F32).T
                at = slice(begin - (width - 1) * filters, stop - (width - 1) * filters)
                conv_out[first + tap, at, :] = piece[begin - tile * TILE : stop - tile * TILE]
                begin = stop
    rest = conv_ref[starts[-1] :, :].astype(F32)
    for tile in range(tiles):
        at = slice(tile * TILE, (tile + 1) * TILE)
        conv_bias_out[:, at] = rest[tile : tile + 1]
    for tile in range(2 * tiles):
        hwy_bias_out[:, tile * TILE : (tile + 1) * TILE] = rest[tiles + tile : tiles + tile + 1]
    half = rec_ref.shape[0] // 2
    rec_tiles = 3 * hidden // TILE
    for side in range(2):
        for tile in range(rec_tiles):
            row = side * half + tile * hidden
            at = slice(tile * TILE, (tile + 1) * TILE)
            rec_out[side, :, at] = rec_ref[row : row + hidden, :].astype(F32)
        row = side * half + rec_tiles * hidden
        rest = rec_ref[row : row + 16, :].astype(F32)
        for tile in range(rec_tiles):
            at = slice(tile * TILE, (tile + 1) * TILE)
            in_bias_out[side : side + 1, at] = rest[tile : tile + 1]
            rec_bias_out[side : side + 1, at] = rest[rec_tiles + tile : rec_tiles + tile + 1]


VMEM = pl.BlockSpec(memory_space=pltpu.VMEM)
SMEM = pl.BlockSpec(memory_space=pltpu.SMEM)
ANY = pl.BlockSpec(memory_space=pl.ANY)


def params(**more):
    return pltpu.CompilerParams(vmem_limit_bytes=VMEM_LIMIT, **more)


def shape(*dims, dtype=F32):
    return jax.ShapeDtypeStruct(dims, dtype)


def block(*dims, dtype=BF16):
    return pltpu.VMEM(dims, dtype)


def flags(*dims):
    return pltpu.SemaphoreType.DMA(dims)


def head_call(sizes, hidden, dps, groups, given):
    sentences, span, segments, channels, embed, filters = sizes
    wide, rows, chips, tiles = 3 * hidden, sentences * segments, dps // 2, channels // TILE
    height = max(8, 2 * sentences)
    steps, part = segments * height, segments // groups
    rec_rows = wide // TILE * hidden + 16 * chips
    side = math.isqrt(chips)
    copies = 1 + 2 * (side - 1) * (side + 1)
    return pl.pallas_call(
        functools.partial(head_kernel, sizes + (hidden, height, dps, groups)),
        name="head",
        out_shape=[
            shape(groups * sentences, part, 2 * hidden, dtype=BF16),
            shape(chips, rows, channels, dtype=BF16),
            shape(chips, rows, channels, dtype=BF16),
            shape(tiles, STRIDE, rows, TILE, dtype=BF16),
            shape(tiles, 3, rows, TILE),
            shape(NWID * embed, STRIDE * rows, dtype=BF16),
            shape(channels, NWID * embed, dtype=BF16),
            shape(rows, 2 * wide, dtype=BF16),
            shape(rec_rows, TILE, dtype=BF16),
        ],
        in_specs=[VMEM, ANY, VMEM, VMEM, ANY, VMEM, ANY, ANY, VMEM, ANY, VMEM],
        out_specs=[VMEM, ANY, ANY, ANY, ANY, VMEM, VMEM, VMEM, VMEM],
        scratch_shapes=[
            block(8, 128, dtype=F32),
            block(groups, sentences, span // groups, embed),
            block(2, 2, channels, TILE),
            block(STRIDE, rows, NWID * embed),
            block(2, STRIDE, rows, TILE),
            block(2, 3, rows, TILE, dtype=F32),
            block(rows, channels),
            block(rows, channels),
            block(rows, channels),
            block(channels, wide),
            block(hidden, wide),
            block(steps, wide, dtype=F32),
            block(steps, 5 * hidden, dtype=F32),
            block(steps, hidden, dtype=F32),
            block(steps, 128, dtype=F32),
            block(2, groups, sentences, part, hidden),
            block(2, groups, sentences, part, hidden),
            block(rows, wide),
            block(16 * chips, TILE, dtype=F32),
            flags(2, 2), flags(2), flags(2), flags(2), flags(6), flags(2, groups), flags(2, 2 * groups),
            flags(2, 2 * groups), flags(2, copies), flags(2, copies),
        ],
        compiler_params=params(collective_id=2, has_side_effects=True),
    )(*given)


def tail_call(sizes, hidden, dps, groups, given):
    sentences, span, segments, channels, embed, filters = sizes
    wide, rows, chips = 3 * hidden, sentences * segments, dps // 2
    rec_rows = wide // TILE * hidden + 16 * chips
    tiles = channels // TILE
    in_share, hwy_share = 2 * wide // dps, 2 * channels // dps
    spans = tile_taps(filters)
    conv_rows = (sum(high - low for low, high in spans) + 1) * embed

    def slots(lead, share):
        return pltpu.VMEM((lead, share, TILE), BF16)

    conv_share, rec_share = conv_rows // dps, rec_rows // chips
    return pl.pallas_call(
        functools.partial(tail_kernel, sizes + (dps, groups)),
        name="tail",
        out_shape=[
            shape(tiles, in_share, TILE, dtype=BF16),
            shape(tiles, hwy_share, TILE, dtype=BF16),
            shape(conv_rows, TILE, dtype=BF16),
            shape(2 * rec_rows, TILE, dtype=BF16),
            shape(groups, sentences, span // groups, embed, dtype=BF16),
        ],
        in_specs=[VMEM] + [ANY] * 10,
        out_specs=[VMEM, VMEM, ANY, ANY, VMEM],
        scratch_shapes=[
            block(3, TILE, 2 * channels),
            block(2, 3, rows, TILE, dtype=F32),
            block(2, STRIDE, rows, TILE),
            block(2, chips, rows, TILE),
            slots(3, 2 * hwy_share),
            block(rows, 2 * wide),
            block(2 * wide, rows),
            block(rows, 2 * channels),
            block(2 * channels, rows),
            block(rows, channels, dtype=F32),
            block(STRIDE * rows, channels),
            block(embed, TILE, dtype=F32),
            block(sentences, span, embed),
            block(NWID * embed, STRIDE * rows),
            block(channels, NWID * embed),
            block(chips - 1, 2 * in_share, rows),
            block(chips - 1, 2 * hwy_share, rows),
            slots(tiles, in_share), slots(tiles, hwy_share),
            slots(tiles, in_share), slots(tiles, hwy_share),
            slots(tiles, in_share), slots(tiles, hwy_share),
            block(conv_rows, TILE),
            block(conv_rows // 2, TILE),
            block(conv_rows // 2, TILE),
            slots(chips - 1, conv_share),
            block(conv_share, TILE),
            block(conv_share, TILE),
            block(conv_share, TILE),
            slots(chips - 1, rec_share),
            block(rec_share, TILE),
            block(rec_share, TILE),
            block(rec_share, TILE),
            flags(3), flags(2), flags(2), flags(2), flags(4),
            flags(2, chips), flags(2, chips), flags(2, groups),
            flags(6, tiles), flags(6, tiles), flags(2), flags(2, chips), flags(2, chips),
            flags(SMALL_PARTS, 6), flags(SMALL_PARTS, 6), flags(SMALL_PARTS, 4, chips), flags(SMALL_PARTS, 4, chips),
        ],
        compiler_params=params(collective_id=1, has_side_effects=True),
    )(
        *given
    )


def local(
    char_embeds, lengths, conv_weight, conv_bias, hwy_weight, hwy_bias, gru_in_weight, gru_in_bias,
    gru_rec_weight, gru_rec_bias, out_grad,
):
    groups = lax.axis_size("seq")
    dps = lax.axis_size("dp")
    sentences = char_embeds.shape[0] // groups
    span = char_embeds.shape[1] * groups
    segments = span // STRIDE
    embed, filters = conv_weight.shape[1:]
    channels = NWID * filters
    hidden = gru_rec_weight.shape[1]
    wide = 3 * hidden
    lens = jnp.pad(lengths.astype(F32)[None], ((0, 7), (0, 128 - lengths.shape[0])))
    sizes = (sentences, span, segments, channels, embed, filters)
    encoded, pool_all, high_all, slope, factor, cross, taps, pair, rec_part = head_call(
        sizes, hidden, dps, groups,
        (
            lens, char_embeds, conv_weight.transpose(0, 2, 1), conv_bias.astype(F32)[None], hwy_weight[0],
            hwy_bias.astype(F32), out_grad, gru_in_weight, gru_in_bias.astype(F32).reshape(2, wide), gru_rec_weight,
            gru_rec_bias.astype(F32),
        ),
    )
    in_sum, hwy_sum, conv_sum, rec_sum, chars_box = tail_call(
        sizes, hidden, dps, groups,
        (
            lens, pair, factor, slope, cross, taps, gru_in_weight, hwy_weight[0], high_all, pool_all, rec_part,
        ),
    )
    in_share, hwy_share = 2 * wide // dps, 2 * channels // dps
    in_grad, hwy_grad, conv_grad, rec_grad, conv_bias_grad, hwy_bias_grad, in_bias_grad, rec_bias_grad = pl.pallas_call(
        functools.partial(finish_kernel, (embed, filters, hidden)),
        name="finish",
        out_shape=[
            shape(channels, in_share),
            shape(hwy_share, channels),
            shape(NWID * (NWID + 1) // 2, filters, embed),
            shape(2, hidden, wide),
            shape(1, channels),
            shape(1, 2 * channels),
            shape(2, wide),
            shape(2, wide),
        ],
        in_specs=[VMEM] * 4,
        out_specs=[VMEM] * 8,
        compiler_params=params(),
    )(in_sum, hwy_sum, conv_sum, rec_sum)
    dchars = chars_box.reshape(groups * sentences, span // groups, embed).astype(F32)
    return (
        encoded, dchars, conv_grad.transpose(0, 2, 1), conv_bias_grad.reshape(-1), hwy_grad.T[None], hwy_bias_grad, in_grad,
        in_bias_grad.reshape(-1), rec_grad, rec_bias_grad,
    )


def solution(mesh):
    whole = P()
    split = P("dp", "seq", None)
    return jax.shard_map(
        local,
        mesh=mesh,
        in_specs=(split, P("dp")) + (whole,) * 8 + (split,),
        out_specs=(split, split, whole, whole, P(None, None, "dp"), whole, P(None, "dp"), whole, whole, whole),
        check_vma=False,
    )
```

```python
import functools
import math

import jax
import jax.numpy as jnp
from jax import lax
from jax.experimental import pallas as pl
from jax.experimental.pallas import tpu as pltpu
from jax.sharding import PartitionSpec as P

MESH = pl.DeviceIdType.MESH
NWID = 8
STRIDE = 5
LEAD = (NWID - 1) // 2
TILE = 256
LENS = 128
SMALL_PARTS = 3
IN_CHUNKS = 3
HWY_CHUNKS = 4
HALVES = 2
ENDING = 4
F32 = jnp.float32
BF16 = jnp.bfloat16
VMEM_LIMIT = 61 * 2**20


def tile_taps(filters):
    found = []
    for tile in range(NWID * filters // TILE):
        first_width = tile * TILE // filters + 1
        last_width = (tile * TILE + TILE - 1) // filters + 1
        low, high = NWID, 0
        for width in range(first_width, last_width + 1):
            lead = (width - 1) // 2
            low, high = min(low, LEAD - lead), max(high, LEAD - lead + width)
        found.append((low, high))
    return found


def chunk_of(share, most):
    units = share // 16
    return share // max(count for count in range(1, most + 1) if units % count == 0)


def chunk_pieces(first, last, share, chunk):
    pieces = []
    while first < last:
        chip, rest = divmod(first, 2 * share)
        core, rest = divmod(rest, share)
        turn, rest = divmod(rest, chunk)
        size = min(last - first, chunk - rest)
        pieces.append((first, size, chip * 2 * share + turn * 2 * chunk + core * chunk + rest))
        first += size
    return pieces


def lay_taps(weight_ref, taps_ref):
    _, filters, embed = weight_ref.shape
    taps_ref[...] = jnp.zeros_like(taps_ref)
    for width in range(1, NWID + 1):
        for tap in range(width):
            spot = LEAD - (width - 1) // 2 + tap
            taps_ref[(width - 1) * filters : width * filters, spot * embed : (spot + 1) * embed] = weight_ref[
                width * (width - 1) // 2 + tap
            ]


def sigmoid(value):
    return 0.5 * jnp.tanh(0.5 * value) + 0.5


def dot(left, right):
    return jnp.dot(left, right, preferred_element_type=F32)


def dot_nt(left, right):
    return lax.dot_general(left, right, (((1,), (1,)), ((), ())), preferred_element_type=F32)


def dot_tn(left, right):
    return lax.dot_general(left, right, (((0,), (0,)), ((), ())), preferred_element_type=F32)


def one_hot(rows, columns, target):
    places = lax.broadcasted_iota(jnp.int32, (rows, columns), 1)
    return jnp.where(places == target, 1.0, 0.0).astype(BF16)


def row_ids(rows):
    return lax.broadcasted_iota(jnp.int32, (rows, 1), 0)


def shift_rows(value, count):
    if count == 0:
        return value
    rows = value.shape[0]
    ids = row_ids(rows)
    moved = pltpu.roll(value, count % rows, axis=0)
    keep = ids >= count if count > 0 else ids < rows + count
    return jnp.where(keep, moved, 0.0)


class Place:
    def __init__(self, dps, groups):
        self.chips, self.groups = dps // 2, groups
        self.dp, self.seq = lax.axis_index("dp"), lax.axis_index("seq")
        self.chip, self.core = self.dp // 2, self.dp % 2
        self.partner = (self.chip * 2 + 1 - self.core, self.seq)
        half = groups // 2
        low = self.seq < half
        self.inner = (self.dp, jnp.where(low, self.seq + 1, self.seq - 1))
        self.outer = (self.dp, jnp.clip(jnp.where(low, self.seq - 1, self.seq + 1), 0, groups - 1))
        self.has_outer = (self.seq > 0) & (self.seq < groups - 1)
        self.depth = jnp.where(low, half - 1 - self.seq, self.seq - half)
        self.middle = self.depth == 0

    def peer_chip(self, hop):
        return (self.chip + hop) % self.chips

    def peer(self, hop):
        return (self.peer_chip(hop) * 2 + self.core, self.seq)

    def peers(self):
        return [self.peer(hop) for hop in range(1, self.chips)]

    def column(self):
        found = []
        for hop in range(self.groups):
            for flip in range(2):
                if hop or flip:
                    found.append((hop, flip, (self.chip * 2 + (self.core + flip) % 2, self.along_place(hop))))
        return found

    def grid(self, axis, hop):
        side = math.isqrt(self.chips)
        high, low = self.chip // side, self.chip % side
        if axis == 0:
            return (high + hop) % side * side + low
        return high * side + (low + hop) % side

    def along_place(self, hop):
        return (self.seq + hop) % self.groups

    def along(self):
        return [(self.dp, self.along_place(hop)) for hop in range(1, self.groups)]


def greet(devices):
    barrier = pltpu.get_barrier_semaphore()
    for device in devices:
        pl.semaphore_signal(barrier, inc=1, device_id=device, device_id_type=MESH)
    pl.semaphore_wait(barrier, len(devices))


def remote(src, dst, send, recv, device):
    return pltpu.make_async_remote_copy(
        src_ref=src, dst_ref=dst, send_sem=send, recv_sem=recv, device_id=device, device_id_type=MESH
    )


def exact(start, size, unit):
    return pl.ds(pl.multiple_of(start, unit), size)


def row_lengths(lens, which):
    found = jnp.zeros(which.shape, F32)
    for place, value in enumerate(lens):
        found = jnp.where(which == place, value, found)
    return found.astype(jnp.int32)


def own_lengths(lens_ref, first, count):
    spots = lax.broadcasted_iota(jnp.int32, (1, LENS), 1)
    return [
        jnp.sum(jnp.where(spots == first + place, lens_ref[:, 0:LENS], 0.0), axis=1, keepdims=True)
        for place in range(count)
    ]


def head_kernel(
    sizes, row_ref, chars_hbm, weight_ref, hwy_hbm, cot_hbm, in_hbm, rec_hbm,
    states_out, pool_all, high_all, slope_hbm, factor_hbm, cross_hbm, taps_hbm, pair_hbm, turned_hbm, rec_part_ref,
    cross_ref, taps_ref, keep_ref,
    lens_other, chars_box, hwy_slots, stack_ref, slope_slots, factor_slots, pooled_ref, high_ref, other_ref,
    in_ref, rec_ref, gates_ref, coef_ref, prior_ref, emit_ref, cot_box, states_ref, given_ref, bias_ref,
    hwy_sems, slope_sems, factor_sems, load_sems, swap_sems, chars_sems, cot_sems, states_sems, pool_sems, high_sems,
):
    sentences, span, segments, channels, embed, filters, hidden, height, dps, groups = sizes
    rows = sentences * segments
    tiles = channels // TILE
    wide = 3 * hidden
    here = Place(dps, groups)
    waits = []
    lens_ref = row_ref.at[:, pl.ds(0, LENS)]
    conv_bias_ref = row_ref.at[:, pl.ds(LENS, channels)]
    hwy_bias_ref = row_ref.at[:, pl.ds(LENS + channels, 2 * channels)]
    in_first = LENS + 3 * channels
    in_bias = row_ref[:, exact(in_first + here.core * wide, wide, 128)]
    rec_bias = row_ref[:, exact(in_first + (2 + here.core) * wide, wide, 128)]

    def columns(tile):
        return [(hwy_hbm.at[:, pl.ds(side * channels + tile * TILE, TILE)], side) for side in range(2)]

    hwy_loads = {}

    def hwy_start(tile):
        if tile < tiles:
            slot = tile % hwy_slots.shape[0]
            hwy_loads[tile] = [
                pltpu.make_async_copy(source, hwy_slots.at[slot, side], hwy_sems.at[slot, side])
                for source, side in columns(tile)
            ]
            for load in hwy_loads[tile]:
                load.start()

    for tile in range(hwy_slots.shape[0]):
        hwy_start(tile)
    loads = [
        pltpu.make_async_copy(in_hbm.at[:, exact(here.core * wide, wide, 128)], in_ref, load_sems.at[0]),
        pltpu.make_async_copy(rec_hbm.at[here.core], rec_ref, load_sems.at[1]),
    ]
    greet([device for _, _, device in here.column()] + here.peers())
    swap_lens = remote(lens_ref, lens_other, swap_sems.at[0], swap_sems.at[1], here.partner)
    swap_lens.start()
    share = span // groups
    chars_copies = []
    for hop in range(1, groups):
        chars_copies.append(
            remote(
                chars_hbm.at[exact(here.along_place(hop) * sentences, sentences, 1)], chars_box.at[here.seq],
                chars_sems.at[0, hop], chars_sems.at[1, hop], (here.dp, here.along_place(hop)),
            )
        )
    chars_copies.append(
        pltpu.make_async_copy(
            chars_hbm.at[exact(here.seq * sentences, sentences, 1)], chars_box.at[here.seq], chars_sems.at[0, 0]
        )
    )
    for copy in chars_copies:
        copy.start()
    cot_copies = []
    for hop, flip, device in here.column():
        side = (here.core + flip) % 2
        cot_copies.append(
            remote(
                cot_hbm.at[
                    exact(here.along_place(hop) * sentences, sentences, 1), :, exact(side * hidden, hidden, 128)
                ],
                cot_box.at[here.core, here.seq], cot_sems.at[0, 2 * hop + flip], cot_sems.at[1, 2 * hop + flip], device,
            )
        )
    cot_copies.append(
        pltpu.make_async_copy(
            cot_hbm.at[exact(here.seq * sentences, sentences, 1), :, exact(here.core * hidden, hidden, 128)],
            cot_box.at[here.core, here.seq], cot_sems.at[0, 0],
        )
    )
    for copy in cot_copies:
        copy.start()
    for load in loads:
        load.start()
    lay_taps(weight_ref, taps_ref)
    ids = row_ids(rows)
    segment, sentence = ids // sentences, ids % sentences
    lens = own_lengths(lens_ref, here.seq * sentences, sentences)
    length = row_lengths(lens, sentence)
    live = []
    planes = {}
    for copy in chars_copies:
        copy.wait()
    chars = chars_box[...].reshape(sentences * span, embed)
    for place in range(STRIDE):
        time = segment * STRIDE + place
        alive = time < length
        live.append(alive.astype(F32))
        target = jnp.where(alive, (time // share * sentences + sentence) * share + time % share, -1)
        plane = dot(one_hot(rows, sentences * span, target), chars)
        for hop in (-1, 0, 1):
            planes[hop, place] = shift_rows(plane, -hop * sentences).astype(BF16)
    turned = {key: plane.T for key, plane in planes.items()}
    for place in range(STRIDE):
        for tap in range(NWID):
            spot = place + tap - LEAD
            key = (spot // STRIDE, spot % STRIDE)
            stack_ref[place, :, tap * embed : (tap + 1) * embed] = planes[key]
            cross_ref[tap * embed : (tap + 1) * embed, place * rows : (place + 1) * rows] = turned[key]
    count = jnp.clip(length - STRIDE * segment, 0, STRIDE).astype(F32)
    scale = 1.0 / jnp.maximum(count, 1.0)

    for source, out, flag in ((cross_ref, cross_hbm, 2), (taps_ref, taps_hbm, 3)):
        copy = pltpu.make_async_copy(source, out, load_sems.at[flag])
        copy.start()
        waits.append(copy.wait)

    def stored(slots, out, sems, tile, copies):
        slot = tile % slots.shape[0]
        if tile >= slots.shape[0]:
            copies[tile - slots.shape[0]].wait()
        copies.append(pltpu.make_async_copy(slots.at[slot], out.at[tile], sems.at[slot]))
        return slots.at[slot]

    slope_copies, factor_copies = [], []
    for tile, (low, high) in enumerate(tile_taps(filters)):
        cols = slice(tile * TILE, (tile + 1) * TILE)
        total = jnp.zeros((rows, TILE), F32)
        slot = stored(slope_slots, slope_hbm, slope_sems, tile, slope_copies)
        for place in range(STRIDE):
            pre = dot_nt(
                stack_ref[place, :, low * embed : high * embed],
                taps_ref[cols, low * embed : high * embed],
            ) + conv_bias_ref[:, cols]
            gate = sigmoid(pre)
            act = pre * gate
            total = total + act * live[place]
            slot[place] = (gate + act * (1.0 - gate)).astype(BF16)
        slope_copies[tile].start()
        pooled_ref[:, cols] = (total * scale).astype(BF16)

    def gather(source, out, sems):
        side = math.isqrt(here.chips)
        half = rows // 2
        stay = pltpu.make_async_copy(source, out.at[here.chip], sems.at[0, 0])
        firsts, seconds, onwards = [], [], []
        flag = 1
        for axis in range(2):
            at = pl.ds(axis * half, half)
            for hop in range(1, side):
                chip = here.grid(axis, hop)
                firsts.append(
                    remote(
                        source.at[at], out.at[here.chip, at], sems.at[0, flag], sems.at[1, flag],
                        (chip * 2 + here.core, here.seq),
                    )
                )
                came = here.grid(axis, side - hop)
                flag += 1
                for hop_2 in range(1, side):
                    chip = here.grid(1 - axis, hop_2)
                    onwards.append(
                        (
                            firsts[-1],
                            remote(
                                out.at[came, at], out.at[came, at], sems.at[0, flag], sems.at[1, flag],
                                (chip * 2 + here.core, here.seq),
                            ),
                        )
                    )
                    flag += 1
            for hop in range(1, side):
                chip = here.grid(1 - axis, hop)
                seconds.append(
                    remote(
                        source.at[at], out.at[here.chip, at], sems.at[0, flag], sems.at[1, flag],
                        (chip * 2 + here.core, here.seq),
                    )
                )
                flag += 1
        for copy in [stay] + firsts + seconds:
            copy.start()
        waits.extend([stay.wait] + [copy.wait_send for copy in firsts] + [copy.wait for copy in seconds])
        return onwards

    pool_onwards = gather(pooled_ref, pool_all, pool_sems)
    for tile in range(tiles):
        cols = slice(tile * TILE, (tile + 1) * TILE)
        cols_2 = slice(channels + tile * TILE, channels + (tile + 1) * TILE)
        for load in hwy_loads[tile]:
            load.wait()
        slot = tile % hwy_slots.shape[0]
        pre_1 = dot(pooled_ref[...], hwy_slots[slot, 0]) + hwy_bias_ref[:, cols]
        pre_2 = dot(pooled_ref[...], hwy_slots[slot, 1]) + hwy_bias_ref[:, cols_2]
        hwy_start(tile + hwy_slots.shape[0])
        layer_in = pooled_ref[:, cols].astype(F32)
        gate, inner = sigmoid(pre_2), sigmoid(pre_1)
        act = pre_1 * inner
        off = 1.0 - gate
        high_ref[:, cols] = (gate * act + off * layer_in).astype(BF16)
        factor = stored(factor_slots, factor_hbm, factor_sems, tile, factor_copies)
        factor[0] = gate * (inner + act * (1.0 - inner))
        factor[1] = (act - layer_in) * gate * off
        factor[2] = off
        factor_copies[tile].start()
    swap = remote(high_ref, other_ref, swap_sems.at[2], swap_sems.at[3], here.partner)
    swap.start()
    high_onwards = gather(high_ref, high_all, high_sems)
    for copies, slots in ((slope_copies, slope_slots), (factor_copies, factor_slots)):
        for copy in copies[-slots.shape[0] :]:
            copy.wait()

    steps = segments * height
    ids = row_ids(steps)
    step, lane = ids // height, ids % height
    segment = jnp.where(here.core == 0, step, segments - 1 - step)
    whose, sentence = lane // sentences, lane % sentences
    real = lane < 2 * sentences
    order = segment * sentences + sentence
    mine = real & (whose == here.core)
    theirs = real & (whose != here.core)
    take_own = one_hot(steps, rows, jnp.where(mine, order, -1))
    take_other = one_hot(steps, rows, jnp.where(theirs, order, -1))
    part = segments // groups
    order_2 = ((whose * groups + segment // part) * sentences + sentence) * part + segment % part
    pick = one_hot(steps, 2 * rows, jnp.where(real, order_2, -1))
    swap_lens.wait()
    lens_2 = own_lengths(lens_other, here.seq * sentences, sentences)
    length = jnp.where(mine, row_lengths(lens, sentence), row_lengths(lens_2, sentence))
    live = real & (segment < (length + STRIDE - 1) // STRIDE)
    emit_ref[...] = jnp.broadcast_to(live.astype(F32), (steps, 128))
    own_part = dot(take_own, high_ref[...])
    swap.wait()
    stepped = (own_part + dot(take_other, other_ref[...])).astype(BF16)
    loads[0].wait()
    gates_ref[...] = dot(stepped, in_ref[...]) + in_bias
    loads[1].wait()

    def ahead(index, state):
        at = pl.ds(pl.multiple_of(index * height, height), height)
        q = dot(state.astype(BF16), rec_ref[...]) + rec_bias
        gates = gates_ref[at, :]
        alive = emit_ref[at, 0:1] > 0.0
        reset = sigmoid(gates[:, :hidden] + q[:, :hidden])
        update = sigmoid(gates[:, hidden : 2 * hidden] + q[:, hidden : 2 * hidden])
        q_n = q[:, 2 * hidden :]
        fresh = jnp.tanh(gates[:, 2 * hidden :] + reset * q_n)
        keep = jnp.where(alive, update, 1.0)
        move = jnp.where(alive, 1.0 - update, 0.0)
        after = move * fresh + keep * state
        prior_ref[at, :] = state
        slope = move * (1.0 - fresh * fresh)
        slope_r = slope * reset
        coef_ref[at, :hidden] = slope_r * q_n * (1.0 - reset)
        coef_ref[at, hidden : 2 * hidden] = (state - fresh) * update * move
        coef_ref[at, 2 * hidden : wide] = slope_r
        coef_ref[at, wide : wide + hidden] = slope
        coef_ref[at, wide + hidden :] = keep
        gates_ref[at, :hidden] = jnp.where(alive, after, 0.0)
        return after

    lax.fori_loop(0, segments, ahead, jnp.zeros((height, hidden), F32), unroll=2)
    for came, onward in pool_onwards + high_onwards:
        came.wait_recv()
        onward.start()
        waits.append(onward.wait)
    states = dot_tn(pick, gates_ref[:, :hidden].astype(BF16)).astype(BF16)
    block = rows // groups
    for whose in range(2):
        for place in range(groups):
            at = (whose * groups + place) * block
            states_ref[whose, place] = states[at : at + block].reshape(sentences, part, hidden)
    seat = (exact(here.seq * sentences, sentences, 1), slice(None), exact(here.core * hidden, hidden, 128))
    for hop, flip, device in here.column():
        copy = remote(
            states_ref.at[(here.core + flip) % 2, here.along_place(hop)], states_out.at[seat],
            states_sems.at[0, 2 * hop + flip], states_sems.at[1, 2 * hop + flip], device,
        )
        copy.start()
        waits.append(copy.wait)
    stay = pltpu.make_async_copy(states_ref.at[here.core, here.seq], states_out.at[seat], states_sems.at[0, 0])
    stay.start()
    waits.append(stay.wait)
    for copy in cot_copies:
        copy.wait()
    cot = cot_box[...].reshape(2 * rows, hidden)
    gates_ref[:, :hidden] = dot(pick, cot) * emit_ref[:, 0:1]
    turned = (slice(0, wide), slice(0, hidden))
    in_ref[turned] = rec_ref[...].T

    def back(index, carried):
        at = pl.ds(pl.multiple_of((segments - 1 - index) * height, height), height)
        total = carried + gates_ref[at, :hidden]
        d_r = total * coef_ref[at, :hidden]
        d_z = total * coef_ref[at, hidden : 2 * hidden]
        d_q = total * coef_ref[at, 2 * hidden : wide]
        d_n = total * coef_ref[at, wide : wide + hidden]
        kept = total * coef_ref[at, wide + hidden :]
        coef_ref[at, :hidden] = d_r
        coef_ref[at, hidden : 2 * hidden] = d_z
        coef_ref[at, 2 * hidden : wide] = d_q
        coef_ref[at, wide : wide + hidden] = d_n
        low = jnp.concatenate([d_r, d_z, d_q], axis=1).astype(BF16)
        return kept + dot(low, in_ref[turned])

    lax.fori_loop(0, segments, back, jnp.zeros((height, hidden), F32), unroll=2)
    recur = coef_ref[:, :wide].astype(BF16)
    fresh = coef_ref[:, wide : wide + hidden].astype(BF16)
    share = 2 * wide // dps
    chunk = chunk_of(share, IN_CHUNKS)
    seat = (slice(None), exact(here.core * wide, wide, 128))
    seat_t = exact(here.core * wide, wide, 16)
    given_t_ref = in_ref.at[pl.ds(0, wide), pl.ds(hidden, rows)]
    keep_t_ref = in_ref.at[pl.ds(0, wide), pl.ds(hidden + rows, rows)]
    for take, ref, ref_t in ((take_other, given_ref, given_t_ref), (take_own, keep_ref, keep_t_ref)):
        ref[:, : 2 * hidden] = dot_tn(take, recur[:, : 2 * hidden]).astype(BF16)
        ref[:, 2 * hidden :] = dot_tn(take, fresh).astype(BF16)
        for row, size, place in chunk_pieces(0, wide, share, chunk):
            ref_t[place : place + size, :] = ref[:, row : row + size].T
        if ref is given_ref:
            copies = [
                remote(ref, pair_hbm.at[seat], swap_sems.at[4], swap_sems.at[5], here.partner),
                remote(ref_t, turned_hbm.at[seat_t], swap_sems.at[6], swap_sems.at[7], here.partner),
            ]
        else:
            copies = [
                pltpu.make_async_copy(ref, pair_hbm.at[seat], load_sems.at[4]),
                pltpu.make_async_copy(ref_t, turned_hbm.at[seat_t], load_sems.at[5]),
            ]
        for copy in copies:
            copy.start()
            waits.append(copy.wait)
    prior = prior_ref[...].astype(BF16)
    sums = jnp.sum(recur.astype(F32), axis=0, keepdims=True)
    sums_n = jnp.sum(fresh.astype(F32), axis=0, keepdims=True)
    rec_tiles = wide // TILE
    bias_ref[...] = jnp.zeros_like(bias_ref)
    for tile in range(rec_tiles):
        cols = slice(tile * TILE, (tile + 1) * TILE)
        rec_part_ref[tile * hidden : (tile + 1) * hidden, :] = dot_tn(prior, recur[:, cols]).astype(BF16)
        if tile * TILE < 2 * hidden:
            bias_ref[tile : tile + 1, :] = sums[:, cols]
        else:
            bias_ref[tile : tile + 1, :] = sums_n[:, tile * TILE - 2 * hidden : (tile + 1) * TILE - 2 * hidden]
        bias_ref[rec_tiles + tile : rec_tiles + tile + 1, :] = sums[:, cols]
    rec_part_ref[rec_tiles * hidden :, :] = bias_ref[...].astype(BF16)
    for wait in waits:
        wait()


class Ring:
    def __init__(self, slots, sems, loads):
        self.slots, self.sems, self.loads = slots, sems, loads
        self.depth = slots.shape[0]
        self.copies = {}

    def start(self, index):
        if index < len(self.loads):
            source, place = self.loads[index]
            slot = index % self.depth
            self.copies[index] = pltpu.make_async_copy(source, place(self.slots.at[slot]), self.sems.at[slot])
            self.copies[index].start()

    def begin(self):
        for index in range(self.depth):
            self.start(index)

    def take(self, index):
        self.copies[index].wait()
        return self.slots.at[index % self.depth]

    def done(self, index):
        self.start(index + self.depth)


def tail_kernel(
    sizes, lens_ref, pair_hbm, turned_hbm, factor_hbm, slope_hbm, cross_hbm, taps_hbm, in_hbm, hwy_hbm, high_hbm, pool_hbm, rec_hbm,
    in_low, hwy_low, conv_out, rec_out, chars_box,
    weight_slots, factor_slots, slope_slots, rows_ref, full_slots,
    pair_ref, gates_own, dpre_ref, pre_t_ref, dy_ref, dconv_ref, bias_ref, chars_ref, cross_ref, taps_ref,
    in_box, hwy_box, in_got, hwy_got, in_outer, hwy_outer, in_inner, hwy_inner,
    conv_part, conv_got, conv_half, conv_box, conv_low, conv_outer, conv_inner, rec_box, rec_low, rec_outer, rec_inner,
    weight_sems, factor_sems, slope_sems, load_sems, in_spread, hwy_spread, chars_sems,
    in_sems, hwy_sems, conv_swap, conv_sems, rec_sems, conv_line, rec_line, conv_share, rec_share,
):
    sentences, span, segments, channels, embed, filters, dps, groups = sizes
    rows = sentences * segments
    tiles = channels // TILE
    wide = pair_hbm.shape[1] // 2
    here = Place(dps, groups)

    def tile_at(tile):
        return pl.ds(tile * TILE, TILE)

    weights = Ring(
        weight_slots, weight_sems,
        [(in_hbm.at[tile_at(tile)], lambda slot: slot.at[:, pl.ds(0, 2 * wide)]) for tile in range(tiles)]
        + [(hwy_hbm.at[tile_at(tile)], lambda slot: slot) for tile in range(tiles)],
    )
    factors = Ring(factor_slots, factor_sems, [(factor_hbm.at[tile], lambda slot: slot) for tile in range(tiles)])
    slopes = Ring(slope_slots, slope_sems, [(slope_hbm.at[tile], lambda slot: slot) for tile in range(tiles)])
    pair_load = pltpu.make_async_copy(pair_hbm, pair_ref, load_sems.at[0])
    pair_load.start()
    weights.begin()
    factors.begin()
    slopes.begin()
    taps_load = pltpu.make_async_copy(taps_hbm, taps_ref, load_sems.at[1])
    cross_load = pltpu.make_async_copy(cross_hbm, cross_ref, load_sems.at[2])
    in_share, hwy_share = in_got.shape[0] * in_got.shape[1], hwy_got.shape[0] * hwy_got.shape[1]
    own_load = pltpu.make_async_copy(
        turned_hbm.at[exact(here.chip * 2 * in_share, 2 * in_share, 16)], gates_own, load_sems.at[4]
    )
    own_load.start()
    rows_load = pltpu.make_async_copy(high_hbm, rows_ref, load_sems.at[5])
    rows_load_2 = pltpu.make_async_copy(pool_hbm, rows_ref, load_sems.at[5])
    rows_load.start()
    greet([here.partner] + here.peers() + here.along())
    taps_load.start()
    cross_load.start()
    rec_load = pltpu.make_async_copy(
        rec_hbm.at[exact(here.chip * rec_low.shape[0], rec_low.shape[0], 16)], rec_low, load_sems.at[3]
    )
    rec_load.start()
    ids = row_ids(rows)
    segment, sentence = ids // sentences, ids % sentences
    length = row_lengths(own_lengths(lens_ref, here.seq * sentences, sentences), sentence)
    count = jnp.clip(length - STRIDE * segment, 0, STRIDE).astype(F32)
    scale = 1.0 / jnp.maximum(count, 1.0)
    bias_ref[...] = jnp.zeros_like(bias_ref)
    sent = []
    waits = []

    def spread(source, box, sends):
        share = box.shape[1]
        copies = []
        for hop in range(1, here.chips):
            at = exact(here.peer_chip(hop) * share, share, 16)
            copies.append(
                remote(source.at[at], box.at[hop - 1], sends.at[0, hop], sends.at[1, hop], here.peer(hop))
            )
            copies[-1].start()
        sent.extend(copies)
        return copies

    def chunk_spread(source, box, sends, share, chunk):
        lists = []
        for turn in range(share // chunk):
            lists.append([])
            for hop in range(1, here.chips):
                at = exact(here.peer_chip(hop) * 2 * share + turn * 2 * chunk, 2 * chunk, 16)
                lists[-1].append(
                    remote(
                        source.at[at], box.at[hop - 1, pl.ds(turn * 2 * chunk, 2 * chunk)],
                        sends.at[0, turn, hop], sends.at[1, turn, hop], here.peer(hop),
                    )
                )
                lists[-1][-1].start()
            sent.extend(lists[-1])
        return lists

    in_chunk, hwy_chunk = in_got.shape[1], hwy_got.shape[1]
    in_lists = chunk_spread(turned_hbm, in_box, in_spread, in_share, in_chunk)
    rec_copies = spread(rec_hbm, rec_box, rec_sems)
    pair_load.wait()
    for tile in range(tiles):
        cols = slice(tile * TILE, (tile + 1) * TILE)
        cols_2 = slice(channels + tile * TILE, channels + (tile + 1) * TILE)
        weight = weights.take(tile)
        dy = dot_nt(pair_ref[...], weight[:, : 2 * wide])
        weights.done(tile)
        factor = factors.take(tile)
        d_1 = (dy * factor[0]).astype(BF16)
        d_2 = (dy * factor[1]).astype(BF16)
        dy_ref[:, cols] = dy * factor[2]
        factors.done(tile)
        dpre_ref[:, cols] = d_1
        dpre_ref[:, cols_2] = d_2
        for at, turned in ((cols, d_1.T), (cols_2, d_2.T)):
            for row, size, place in chunk_pieces(at.start, at.stop, hwy_share, hwy_chunk):
                pre_t_ref[place : place + size, :] = turned[row - at.start : row - at.start + size]
        bias_ref[tiles + tile : tiles + tile + 1, :] = jnp.sum(d_1.astype(F32), axis=0, keepdims=True)
        bias_ref[2 * tiles + tile : 2 * tiles + tile + 1, :] = jnp.sum(d_2.astype(F32), axis=0, keepdims=True)
    hwy_lists = chunk_spread(pre_t_ref, hwy_box, hwy_spread, hwy_share, hwy_chunk)

    def conv_back(tile):
        cols = slice(tile * TILE, (tile + 1) * TILE)
        weight = weights.take(tiles + tile)
        dy = (dy_ref[:, cols] + dot_nt(dpre_ref[...], weight[...])) * scale
        weights.done(tiles + tile)
        slope = slopes.take(tile)
        sums = jnp.zeros((1, TILE), F32)
        for place in range(STRIDE):
            alive = (segment * STRIDE + place < length).astype(F32)
            part = (dy * alive * slope[place].astype(F32)).astype(BF16)
            dconv_ref[place * rows : (place + 1) * rows, cols] = part
            sums = sums + jnp.sum(part.astype(F32), axis=0, keepdims=True)
        slopes.done(tile)
        bias_ref[tile : tile + 1, :] = sums

    spans = tile_taps(filters)
    starts = [0]
    for low, high in spans:
        starts.append(starts[-1] + (high - low) * embed)
    sums = {}
    half = conv_half.shape[0]
    conv_copy = remote(
        conv_part.at[exact((1 - here.core) * half, half, 16)], conv_got, conv_swap.at[0], conv_swap.at[1], here.partner
    )
    conv_copies = []

    def chars_part(begin_tap):
        begin = min(tile for tile, (low, high) in enumerate(spans) if low < begin_tap + 2 and high > begin_tap)
        part = dot(
            dconv_ref[:, begin * TILE :],
            taps_ref[begin * TILE :, begin_tap * embed : (begin_tap + 2) * embed],
        )
        for tap in (begin_tap, begin_tap + 1):
            for place in range(STRIDE):
                spot = place + tap - LEAD
                key = (spot // STRIDE, spot % STRIDE)
                piece = part[
                    place * rows : (place + 1) * rows, (tap - begin_tap) * embed : (tap - begin_tap + 1) * embed
                ]
                sums[key] = sums[key] + piece if key in sums else piece

    def chars_end():
        total = jnp.zeros((sentences * span, embed), F32)
        out_ids = row_ids(sentences * span)
        out_sentence, out_time = out_ids // span, out_ids % span
        for place in range(STRIDE):
            plane = jnp.zeros((rows, embed), F32)
            for hop in (-1, 0, 1):
                if (hop, place) in sums:
                    plane = plane + shift_rows(sums[hop, place], hop * sentences)
            plane = jnp.where(segment * STRIDE + place < length, plane, 0.0).astype(BF16)
            target = jnp.where(
                out_time % STRIDE == place, (out_time // STRIDE) * sentences + out_sentence, -1
            )
            total = total + dot(one_hot(sentences * span, rows, target), plane)
        for index in range(sentences):
            chars_ref[index] = total[index * span : (index + 1) * span].astype(BF16)

    def chars_send():
        share = span // groups
        for hop in range(1, groups):
            at = exact(here.along_place(hop) * share, share, 16)
            copy = remote(
                chars_ref.at[:, at], chars_box.at[here.seq], chars_sems.at[0, hop], chars_sems.at[1, hop],
                (here.dp, here.along_place(hop)),
            )
            copy.start()
            waits.append(copy.wait)
        chars_box[here.seq] = chars_ref[:, exact(here.seq * share, share, 16), :]

    def taps_part(tile):
        low, high = spans[tile]
        conv_part[starts[tile] : starts[tile + 1], :] = dot(
            cross_ref[low * embed : high * embed, :], dconv_ref[:, tile * TILE : (tile + 1) * TILE]
        ).astype(BF16)

    def taps_end():
        conv_part[starts[-1] :, :] = bias_ref[...].astype(BF16)
        conv_copy.start()
        sent.append(conv_copy)

    def conv_send():
        conv_copy.wait_recv()
        mine = conv_part[exact(here.core * half, half, 16), :]
        conv_half[...] = (mine.astype(F32) + conv_got[...].astype(F32)).astype(BF16)
        conv_copies.extend(spread(conv_half, conv_box, conv_sems))
        share = conv_low.shape[0]
        conv_low[...] = conv_half[exact(here.chip * share, share, 16), :]

    tasks = [cross_load.wait]
    tasks += [functools.partial(taps_part, tile) for tile in range(tiles)]
    tasks += [taps_end, taps_load.wait]
    tasks += [functools.partial(chars_part, begin_tap) for begin_tap in range(0, NWID, 2)]
    tasks += [conv_send, chars_end]

    halves = []

    def multiply(box, own, own_first, lists, low, got, sems, turn):
        chunk = got.shape[1]
        index = len(halves)
        full = full_slots.at[index % full_slots.shape[0], pl.ds(0, 2 * chunk)]
        if index >= full_slots.shape[0]:
            halves[index - full_slots.shape[0]].wait_send()
        for copy in lists[turn]:
            copy.wait_recv()
        at = pl.ds(turn * 2 * chunk, 2 * chunk)
        for tile in range(tiles):
            cols = slice(tile * TILE, (tile + 1) * TILE)
            total = dot(own[exact(own_first + turn * 2 * chunk, 2 * chunk, 16), :], rows_ref[here.chip, :, cols])
            for hop in range(1, here.chips):
                chip = (here.chip + here.chips - hop) % here.chips
                total = total + dot(box[hop - 1, at, :], rows_ref[chip, :, cols])
            full[:, cols] = total.astype(BF16)
        low[turn] = full[exact(here.core * chunk, chunk, 16), :]
        copy = remote(
            full.at[exact((1 - here.core) * chunk, chunk, 16)], got.at[turn],
            sems.at[turn, 0, 0], sems.at[turn, 0, 1], here.partner,
        )
        copy.start()
        halves.append(copy)

    def line_item(found, low, from_outer, from_inner, sem, keep=None):
        out_to_in = remote(low, from_outer, sem(2), sem(3), here.inner)
        across = remote(low, from_inner, sem(2), sem(4), here.inner)
        in_to_out = remote(low, from_inner, sem(5), sem(4), here.outer)

        def inward():
            low[...] = found().astype(BF16)

            @pl.when(here.has_outer)
            def _():
                out_to_in.wait_recv()
                low[...] = (low[...].astype(F32) + from_outer[...].astype(F32)).astype(BF16)

            @pl.when(here.middle)
            def _():
                across.start()

            @pl.when(jnp.logical_not(here.middle))
            def _():
                out_to_in.start()

        def outward():
            across.wait()

            @pl.when(here.middle)
            def _():
                low[...] = (low[...].astype(F32) + from_inner[...].astype(F32)).astype(BF16)

            @pl.when(jnp.logical_not(here.middle))
            def _():
                low[...] = from_inner[...]

            @pl.when(here.has_outer)
            def _():
                in_to_out.start()

            if keep is not None:
                keep()

        def finish():
            @pl.when(here.has_outer)
            def _():
                in_to_out.wait_send()

        return inward, outward, finish

    onward = []

    def share_out(out, low, begin, size, sems):
        base = here.core * (out.shape[0] // 2) + begin
        share = low.shape[0]
        piece = low.at[pl.ds(begin, size)]
        at = exact(base + here.chip * share, size, 16)
        stay = pltpu.make_async_copy(piece, out.at[at], sems.at[2, 0])
        copies = [remote(piece, out.at[at], sems.at[0, 0], sems.at[1, 0], here.partner)]
        for hop in range(1, here.chips):
            copies.append(remote(piece, out.at[at], sems.at[0, hop], sems.at[1, hop], here.peer(hop)))
            source = (here.chip + here.chips - hop) % here.chips
            place = exact(base + source * share, size, 16)
            send_on = remote(out.at[place], out.at[place], sems.at[2, hop], sems.at[3, hop], here.partner)
            onward.append((copies[hop], send_on))
            waits.append(send_on.wait)
        waits.extend(copy.wait_send for copy in copies)
        waits.append(copies[0].wait_recv)
        waits.append(stay.wait)

        def keep():
            stay.start()
            for copy in copies:
                copy.start()

        return keep

    def chunk_items(low, got, first, outer, inner, sems, ending):
        turns = low.shape[0]
        found_lists = []

        def found(turn, part, at):
            if part == 0:
                halves[first + turn].wait_recv()
            return low[turn, :, at].astype(F32) + got[turn, :, at].astype(F32)

        for turn in range(turns):
            count = ENDING if ending and turn == turns - 1 else HALVES
            cuts = [-(-tiles * part // count) * TILE if count > 2 else part * channels // count for part in range(count + 1)]
            found_lists.append([])
            for part, (begin, end) in enumerate(zip(cuts, cuts[1:])):
                at = (turn, slice(None), pl.ds(begin, end - begin))
                found_lists[-1].append(
                    line_item(
                        functools.partial(found, turn, part, slice(begin, end)), low.at[at], outer.at[at], inner.at[at],
                        lambda index, turn=turn, part=part: sems.at[turn, 1 + part, index],
                    )
                )
        return found_lists

    def small_items(low, box, copies, outer, inner, line_sems, share_sems, out, ready):
        found_items = []
        size = low.shape[0] // 16
        cuts = [size * part // SMALL_PARTS * 16 for part in range(SMALL_PARTS + 1)]

        def found(part):
            if part == 0:
                ready()
                for copy in copies:
                    copy.wait_recv()
            at = slice(cuts[part], cuts[part + 1])
            total = low[at, :].astype(F32)
            for hop in range(here.chips - 1):
                total = total + box[hop, at, :].astype(F32)
            return total

        for part in range(SMALL_PARTS):
            at = pl.ds(cuts[part], cuts[part + 1] - cuts[part])
            found_items.append(
                line_item(
                    functools.partial(found, part), low.at[at], outer.at[at], inner.at[at],
                    lambda index, part=part: line_sems.at[part, index],
                    share_out(out, low, cuts[part], cuts[part + 1] - cuts[part], share_sems.at[part]),
                )
            )
        return found_items

    in_items = chunk_items(in_low, in_got, 0, in_outer, in_inner, in_sems, False)
    hwy_items = chunk_items(hwy_low, hwy_got, in_low.shape[0], hwy_outer, hwy_inner, hwy_sems, True)
    rec_items = small_items(
        rec_low, rec_box, rec_copies, rec_outer, rec_inner, rec_line, rec_share, rec_out, rec_load.wait
    )
    conv_items = small_items(
        conv_low, conv_box, conv_copies, conv_outer, conv_inner, conv_line, conv_share, conv_out, lambda: None
    )

    def in_multiply(turn):
        if turn == 0:
            own_load.wait()
            rows_load.wait()
        multiply(in_box, gates_own, 0, in_lists, in_low, in_got, in_sems, turn)
        if turn + 1 == in_low.shape[0]:
            rows_load_2.start()

    def hwy_multiply(turn):
        if turn == 0:
            rows_load_2.wait()
        multiply(hwy_box, pre_t_ref, here.chip * 2 * hwy_share, hwy_lists, hwy_low, hwy_got, hwy_sems, turn)

    tasks = [functools.partial(conv_back, tile) for tile in range(tiles)] + tasks
    items = []
    plan = []

    def add(new):
        plan.extend(new)

    for turn in range(in_low.shape[0]):
        add([functools.partial(in_multiply, turn), 1])
        for item in in_items[turn]:
            add([1, item, 1])
    for item in rec_items:
        add([2, item])
    last = hwy_low.shape[0] - 1
    for turn in range(last):
        add([functools.partial(hwy_multiply, turn), 1])
        for item in hwy_items[turn]:
            add([1, item])
    add([functools.partial(hwy_multiply, last), len(tasks)])
    for item in conv_items + hwy_items[last]:
        add([item])
    add([chars_send])
    depths = groups // 2

    def outwards(index):
        for depth in range(depths):
            ready = index - 2 - 8 * depth
            if 0 <= ready < len(items):
                pl.when(here.depth == depth)(items[ready][1])

    for step in plan:
        if isinstance(step, int):
            for task in tasks[:step]:
                task()
            del tasks[:step]
        elif isinstance(step, tuple):
            items.append(step)
            step[0]()
            outwards(len(items) - 1)
        else:
            step()
    for extra in range(2 + 8 * (depths - 1)):
        outwards(len(items) + extra)
    for copy, send_on in onward:
        copy.wait_recv()
        send_on.start()
    for item in items:
        item[2]()
    for copy in sent:
        copy.wait_send()
    for copy in halves[-full_slots.shape[0] :]:
        copy.wait_send()
    for wait in waits:
        wait()


def finish_kernel(
    sizes, in_hbm, hwy_hbm, conv_hbm, rec_hbm, chars_hbm,
    in_out, hwy_out, conv_out, rec_out, chars_out, conv_bias_out, hwy_bias_out, in_bias_out, rec_bias_out,
    in_ref, hwy_ref, conv_ref, rec_ref, chars_ref, in_full, hwy_full, conv_full, rec_full, chars_full,
    load_sems, store_sems,
):
    embed, filters, hidden = sizes
    tiles = in_ref.shape[2] // TILE
    half = rec_ref.shape[0] // 2
    loads = [
        pltpu.make_async_copy(rec_hbm.at[pl.ds(side * half, half)], rec_ref.at[pl.ds(side * half, half)], load_sems.at[side])
        for side in range(2)
    ]
    for place, (source, ref) in enumerate(((hwy_hbm, hwy_ref), (conv_hbm, conv_ref), (in_hbm, in_ref), (chars_hbm, chars_ref))):
        loads.append(pltpu.make_async_copy(source, ref, load_sems.at[2 + place]))
    for load in loads:
        load.start()
    stores = []

    def store(source, out):
        stores.append(pltpu.make_async_copy(source, out, store_sems.at[len(stores)]))
        stores[-1].start()

    rec_tiles = 3 * hidden // TILE
    for side in range(2):
        loads[side].wait()
        for tile in range(rec_tiles):
            row = side * half + tile * hidden
            at = slice(tile * TILE, (tile + 1) * TILE)
            rec_full[side, :, at] = rec_ref[row : row + hidden, :].astype(F32)
        store(rec_full.at[side], rec_out.at[side])
        row = side * half + rec_tiles * hidden
        rest = rec_ref[row : row + 16, :].astype(F32)
        for tile in range(rec_tiles):
            at = slice(tile * TILE, (tile + 1) * TILE)
            in_bias_out[side : side + 1, at] = rest[tile : tile + 1]
            rec_bias_out[side : side + 1, at] = rest[rec_tiles + tile : rec_tiles + tile + 1]
    loads[2].wait()
    hwy_full[...] = hwy_ref[...].astype(F32).reshape(hwy_full.shape)
    store(hwy_full, hwy_out)
    loads[3].wait()
    spans = tile_taps(filters)
    starts = [0]
    for low, high in spans:
        starts.append(starts[-1] + (high - low) * embed)
    for width in range(1, NWID + 1):
        lead, first = (width - 1) // 2, width * (width - 1) // 2
        for tap in range(width):
            spot = LEAD - lead + tap
            begin, end = (width - 1) * filters, width * filters
            while begin < end:
                tile = begin // TILE
                stop = min(end, (tile + 1) * TILE)
                row = starts[tile] + (spot - spans[tile][0]) * embed
                piece = conv_ref[row : row + embed, :].astype(F32).T
                at = slice(begin - (width - 1) * filters, stop - (width - 1) * filters)
                conv_full[first + tap, at, :] = piece[begin - tile * TILE : stop - tile * TILE]
                begin = stop
    store(conv_full, conv_out)
    rest = conv_ref[starts[-1] :, :].astype(F32)
    for tile in range(tiles):
        at = slice(tile * TILE, (tile + 1) * TILE)
        conv_bias_out[:, at] = rest[tile : tile + 1]
    for tile in range(2 * tiles):
        hwy_bias_out[:, tile * TILE : (tile + 1) * TILE] = rest[tiles + tile : tiles + tile + 1]
    loads[4].wait()
    for turn in range(in_ref.shape[0]):
        at = slice(turn * in_ref.shape[1], (turn + 1) * in_ref.shape[1])
        in_full[:, at] = in_ref[turn].astype(F32).T
    store(in_full, in_out)
    loads[5].wait()
    chars_full[...] = chars_ref[...].astype(F32).reshape(chars_full.shape)
    store(chars_full, chars_out)
    for copy in stores:
        copy.wait()


VMEM = pl.BlockSpec(memory_space=pltpu.VMEM)
SMEM = pl.BlockSpec(memory_space=pltpu.SMEM)
ANY = pl.BlockSpec(memory_space=pl.ANY)


def params(**more):
    return pltpu.CompilerParams(vmem_limit_bytes=VMEM_LIMIT, **more)


def shape(*dims, dtype=F32):
    return jax.ShapeDtypeStruct(dims, dtype)


def block(*dims, dtype=BF16):
    return pltpu.VMEM(dims, dtype)


def flags(*dims):
    return pltpu.SemaphoreType.DMA(dims)


def head_call(sizes, hidden, dps, groups, given):
    sentences, span, segments, channels, embed, filters = sizes
    wide, rows, chips, tiles = 3 * hidden, sentences * segments, dps // 2, channels // TILE
    height = max(8, 2 * sentences)
    steps, part = segments * height, segments // groups
    rec_rows = wide // TILE * hidden + 16 * chips
    side = math.isqrt(chips)
    copies = 1 + 2 * (side - 1) * (side + 1)
    return pl.pallas_call(
        functools.partial(head_kernel, sizes + (hidden, height, dps, groups)),
        name="head",
        out_shape=[
            shape(groups * sentences, part, 2 * hidden, dtype=BF16),
            shape(chips, rows, channels, dtype=BF16),
            shape(chips, rows, channels, dtype=BF16),
            shape(tiles, STRIDE, rows, TILE, dtype=BF16),
            shape(tiles, 3, rows, TILE),
            shape(NWID * embed, STRIDE * rows, dtype=BF16),
            shape(channels, NWID * embed, dtype=BF16),
            shape(rows, 2 * wide, dtype=BF16),
            shape(2 * wide, rows, dtype=BF16),
            shape(rec_rows, TILE, dtype=BF16),
        ],
        in_specs=[VMEM, ANY, VMEM, ANY, ANY, ANY, ANY],
        out_specs=[VMEM] + [ANY] * 8 + [VMEM],
        scratch_shapes=[
            block(NWID * embed, STRIDE * rows),
            block(channels, NWID * embed),
            block(rows, wide),
            block(1, LENS, dtype=F32),
            block(groups, sentences, span // groups, embed),
            block(2, 2, channels, TILE),
            block(STRIDE, rows, NWID * embed),
            block(2, STRIDE, rows, TILE),
            block(2, 3, rows, TILE, dtype=F32),
            block(rows, channels),
            block(rows, channels),
            block(rows, channels),
            block(channels, wide),
            block(hidden, wide),
            block(steps, wide, dtype=F32),
            block(steps, 5 * hidden, dtype=F32),
            block(steps, hidden, dtype=F32),
            block(steps, 128, dtype=F32),
            block(2, groups, sentences, part, hidden),
            block(2, groups, sentences, part, hidden),
            block(rows, wide),
            block(16 * chips, TILE, dtype=F32),
            flags(2, 2), flags(2), flags(2), flags(6), flags(8), flags(2, groups), flags(2, 2 * groups),
            flags(2, 2 * groups), flags(2, copies), flags(2, copies),
        ],
        compiler_params=params(collective_id=2, has_side_effects=True),
    )(*given)


def tail_call(sizes, hidden, dps, groups, given):
    sentences, span, segments, channels, embed, filters = sizes
    wide, rows, chips = 3 * hidden, sentences * segments, dps // 2
    rec_rows = wide // TILE * hidden + 16 * chips
    tiles = channels // TILE
    in_share, hwy_share = 2 * wide // dps, 2 * channels // dps
    spans = tile_taps(filters)
    conv_rows = (sum(high - low for low, high in spans) + 1) * embed

    def slots(lead, share):
        return pltpu.VMEM((lead, share, TILE), BF16)

    in_chunk, hwy_chunk = chunk_of(in_share, IN_CHUNKS), chunk_of(hwy_share, HWY_CHUNKS)
    in_turns, hwy_turns = in_share // in_chunk, hwy_share // hwy_chunk
    conv_share, rec_share = conv_rows // dps, rec_rows // chips
    return pl.pallas_call(
        functools.partial(tail_kernel, sizes + (dps, groups)),
        name="tail",
        out_shape=[
            shape(in_turns, in_chunk, channels, dtype=BF16),
            shape(hwy_turns, hwy_chunk, channels, dtype=BF16),
            shape(conv_rows, TILE, dtype=BF16),
            shape(2 * rec_rows, TILE, dtype=BF16),
            shape(groups, sentences, span // groups, embed, dtype=BF16),
        ],
        in_specs=[VMEM] + [ANY] * 11,
        out_specs=[VMEM, VMEM, ANY, ANY, VMEM],
        scratch_shapes=[
            block(3 if chips <= 8 else 2, TILE, 2 * channels),
            block(2, 3, rows, TILE, dtype=F32),
            block(2, STRIDE, rows, TILE),
            block(chips, rows, channels),
            block(2, 2 * max(in_chunk, hwy_chunk), channels),
            block(rows, 2 * wide),
            block(2 * in_share, rows),
            block(rows, 2 * channels),
            block(2 * channels, rows),
            block(rows, channels, dtype=F32),
            block(STRIDE * rows, channels),
            block(embed, TILE, dtype=F32),
            block(sentences, span, embed),
            block(NWID * embed, STRIDE * rows),
            block(channels, NWID * embed),
            block(chips - 1, 2 * in_share, rows),
            block(chips - 1, 2 * hwy_share, rows),
            block(in_turns, in_chunk, channels), block(hwy_turns, hwy_chunk, channels),
            block(in_turns, in_chunk, channels), block(hwy_turns, hwy_chunk, channels),
            block(in_turns, in_chunk, channels), block(hwy_turns, hwy_chunk, channels),
            block(conv_rows, TILE),
            block(conv_rows // 2, TILE),
            block(conv_rows // 2, TILE),
            slots(chips - 1, conv_share),
            block(conv_share, TILE),
            block(conv_share, TILE),
            block(conv_share, TILE),
            slots(chips - 1, rec_share),
            block(rec_share, TILE),
            block(rec_share, TILE),
            block(rec_share, TILE),
            flags(3), flags(2), flags(2), flags(6),
            flags(2, in_turns, chips), flags(2, hwy_turns, chips), flags(2, groups),
            flags(in_turns, 1 + HALVES, 6), flags(hwy_turns, 1 + ENDING, 6), flags(2), flags(2, chips), flags(2, chips),
            flags(SMALL_PARTS, 6), flags(SMALL_PARTS, 6), flags(SMALL_PARTS, 4, chips), flags(SMALL_PARTS, 4, chips),
        ],
        compiler_params=params(collective_id=1, has_side_effects=True),
    )(
        *given
    )


def local(
    char_embeds, lengths, conv_weight, conv_bias, hwy_weight, hwy_bias, gru_in_weight, gru_in_bias,
    gru_rec_weight, gru_rec_bias, out_grad,
):
    groups = lax.axis_size("seq")
    dps = lax.axis_size("dp")
    sentences = char_embeds.shape[0] // groups
    span = char_embeds.shape[1] * groups
    segments = span // STRIDE
    embed, filters = conv_weight.shape[1:]
    channels = NWID * filters
    hidden = gru_rec_weight.shape[1]
    wide = 3 * hidden
    row = jnp.concatenate(
        [jnp.pad(lengths.astype(F32), (0, LENS - lengths.shape[0]))]
        + [bias.astype(F32).reshape(-1) for bias in (conv_bias, hwy_bias, gru_in_bias, gru_rec_bias)]
    )[None]
    sizes = (sentences, span, segments, channels, embed, filters)
    encoded, pool_all, high_all, slope, factor, cross, taps, pair, turned, rec_part = head_call(
        sizes, hidden, dps, groups,
        (
            row, char_embeds, conv_weight.transpose(0, 2, 1), hwy_weight[0], out_grad, gru_in_weight, gru_rec_weight,
        ),
    )
    in_sum, hwy_sum, conv_sum, rec_sum, chars_box = tail_call(
        sizes, hidden, dps, groups,
        (
            row, pair, turned, factor, slope, cross, taps, gru_in_weight, hwy_weight[0], high_all, pool_all, rec_part,
        ),
    )
    in_share, hwy_share = 2 * wide // dps, 2 * channels // dps
    whole = [
        (channels, in_share),
        (hwy_share, channels),
        (NWID * (NWID + 1) // 2, filters, embed),
        (2, hidden, wide),
        (groups * sentences, span // groups, embed),
    ]
    in_grad, hwy_grad, conv_grad, rec_grad, dchars, conv_bias_grad, hwy_bias_grad, in_bias_grad, rec_bias_grad = pl.pallas_call(
        functools.partial(finish_kernel, (embed, filters, hidden)),
        name="finish",
        out_shape=[shape(*dims) for dims in whole]
        + [shape(1, channels), shape(1, 2 * channels), shape(2, wide), shape(2, wide)],
        in_specs=[ANY] * 5,
        out_specs=[ANY] * 5 + [VMEM] * 4,
        scratch_shapes=[
            block(*part.shape) for part in (in_sum, hwy_sum, conv_sum, rec_sum, chars_box)
        ]
        + [block(*dims, dtype=F32) for dims in whole]
        + [flags(6), flags(6)],
        compiler_params=params(),
    )(in_sum, hwy_sum, conv_sum, rec_sum, chars_box)
    return (
        encoded, dchars, conv_grad.transpose(0, 2, 1), conv_bias_grad.reshape(-1), hwy_grad.T[None], hwy_bias_grad, in_grad,
        in_bias_grad.reshape(-1), rec_grad, rec_bias_grad,
    )


def solution(mesh):
    whole = P()
    split = P("dp", "seq", None)
    return jax.shard_map(
        local,
        mesh=mesh,
        in_specs=(split, P("dp")) + (whole,) * 8 + (split,),
        out_specs=(split, split, whole, whole, P(None, None, "dp"), whole, P(None, "dp"), whole, whole, whole),
        check_vma=False,
    )
```

```python
import functools
import math

import jax
import jax.numpy as jnp
from jax import lax
from jax.experimental import pallas as pl
from jax.experimental.pallas import tpu as pltpu
from jax.sharding import PartitionSpec as P

MESH = pl.DeviceIdType.MESH
NWID = 8
STRIDE = 5
LEAD = (NWID - 1) // 2
TILE = 256
LENS = 128
SMALL_PARTS = 3
IN_CHUNKS = 3
HWY_CHUNKS = 4
HALVES = 2
ENDING = 4
LAG = 6
F32 = jnp.float32
BF16 = jnp.bfloat16
VMEM_LIMIT = 61 * 2**20


def tile_taps(filters):
    found = []
    for tile in range(NWID * filters // TILE):
        first_width = tile * TILE // filters + 1
        last_width = (tile * TILE + TILE - 1) // filters + 1
        low, high = NWID, 0
        for width in range(first_width, last_width + 1):
            lead = (width - 1) // 2
            low, high = min(low, LEAD - lead), max(high, LEAD - lead + width)
        found.append((low, high))
    return found


def chunk_of(share, most):
    units = share // 16
    return share // max(count for count in range(1, most + 1) if units % count == 0)


def chunk_pieces(first, last, share, chunk):
    pieces = []
    while first < last:
        chip, rest = divmod(first, 2 * share)
        core, rest = divmod(rest, share)
        turn, rest = divmod(rest, chunk)
        size = min(last - first, chunk - rest)
        pieces.append((first, size, chip * 2 * share + turn * 2 * chunk + core * chunk + rest))
        first += size
    return pieces


def lay_taps(weight_ref, taps_ref):
    _, filters, embed = weight_ref.shape
    taps_ref[...] = jnp.zeros_like(taps_ref)
    for width in range(1, NWID + 1):
        for tap in range(width):
            spot = LEAD - (width - 1) // 2 + tap
            taps_ref[(width - 1) * filters : width * filters, spot * embed : (spot + 1) * embed] = weight_ref[
                width * (width - 1) // 2 + tap
            ]


def sigmoid(value):
    return 0.5 * jnp.tanh(0.5 * value) + 0.5


def dot(left, right):
    return jnp.dot(left, right, preferred_element_type=F32)


def dot_nt(left, right):
    return lax.dot_general(left, right, (((1,), (1,)), ((), ())), preferred_element_type=F32)


def dot_tn(left, right):
    return lax.dot_general(left, right, (((0,), (0,)), ((), ())), preferred_element_type=F32)


def one_hot(rows, columns, target):
    places = lax.broadcasted_iota(jnp.int32, (rows, columns), 1)
    return jnp.where(places == target, 1.0, 0.0).astype(BF16)


def row_ids(rows):
    return lax.broadcasted_iota(jnp.int32, (rows, 1), 0)


def shift_rows(value, count):
    if count == 0:
        return value
    rows = value.shape[0]
    ids = row_ids(rows)
    moved = pltpu.roll(value, count % rows, axis=0)
    keep = ids >= count if count > 0 else ids < rows + count
    return jnp.where(keep, moved, 0.0)


class Place:
    def __init__(self, dps, groups):
        self.chips, self.groups = dps // 2, groups
        self.dp, self.seq = lax.axis_index("dp"), lax.axis_index("seq")
        self.chip, self.core = self.dp // 2, self.dp % 2
        self.partner = (self.chip * 2 + 1 - self.core, self.seq)
        half = groups // 2
        low = self.seq < half
        self.inner = (self.dp, jnp.where(low, self.seq + 1, self.seq - 1))
        self.outer = (self.dp, jnp.clip(jnp.where(low, self.seq - 1, self.seq + 1), 0, groups - 1))
        self.has_outer = (self.seq > 0) & (self.seq < groups - 1)
        self.depth = jnp.where(low, half - 1 - self.seq, self.seq - half)
        self.middle = self.depth == 0

    def peer_chip(self, hop):
        return (self.chip + hop) % self.chips

    def peer(self, hop):
        return (self.peer_chip(hop) * 2 + self.core, self.seq)

    def peers(self):
        return [self.peer(hop) for hop in range(1, self.chips)]

    def column(self):
        found = []
        for hop in range(self.groups):
            for flip in range(2):
                if hop or flip:
                    found.append((hop, flip, (self.chip * 2 + (self.core + flip) % 2, self.along_place(hop))))
        return found

    def grid(self, axis, hop):
        side = math.isqrt(self.chips)
        high, low = self.chip // side, self.chip % side
        if axis == 0:
            return (high + hop) % side * side + low
        return high * side + (low + hop) % side

    def along_place(self, hop):
        return (self.seq + hop) % self.groups

    def along(self):
        return [(self.dp, self.along_place(hop)) for hop in range(1, self.groups)]


def greet(devices):
    barrier = pltpu.get_barrier_semaphore()
    for device in devices:
        pl.semaphore_signal(barrier, inc=1, device_id=device, device_id_type=MESH)
    pl.semaphore_wait(barrier, len(devices))


def remote(src, dst, send, recv, device):
    return pltpu.make_async_remote_copy(
        src_ref=src, dst_ref=dst, send_sem=send, recv_sem=recv, device_id=device, device_id_type=MESH
    )


def exact(start, size, unit):
    return pl.ds(pl.multiple_of(start, unit), size)


def row_lengths(lens, which):
    found = jnp.zeros(which.shape, F32)
    for place, value in enumerate(lens):
        found = jnp.where(which == place, value, found)
    return found.astype(jnp.int32)


def own_lengths(lens_ref, first, count):
    return [jnp.full((1, 1), lens_ref[first + place].astype(F32)) for place in range(count)]


def row_values(row_ref, count):
    return [row_ref[:, place : place + 1] for place in range(count)]


def head_kernel(
    sizes, lens_ref, conv_bias_ref, hwy_bias_ref, in_bias_ref, rec_bias_ref, chars_hbm, weight_hbm, hwy_hbm, cot_hbm, in_hbm, rec_hbm,
    states_out, pool_all, high_all, slope_hbm, factor_hbm, cross_hbm, taps_hbm, pair_hbm, turned_hbm, rec_part_ref,
    weight_ref, cross_ref, taps_ref, keep_ref,
    lens_row, lens_other, chars_box, hwy_slots, stack_ref, slope_slots, factor_slots, pooled_ref, high_ref, other_ref,
    in_ref, rec_ref, gates_ref, coef_ref, prior_ref, emit_ref, cot_box, states_ref, given_ref, bias_ref,
    hwy_sems, slope_sems, factor_sems, load_sems, swap_sems, chars_sems, cot_sems, states_sems, pool_sems, high_sems,
):
    sentences, span, segments, channels, embed, filters, hidden, height, dps, groups = sizes
    rows = sentences * segments
    tiles = channels // TILE
    wide = 3 * hidden
    here = Place(dps, groups)
    waits = []
    in_bias = in_bias_ref[exact(here.core * wide, wide, 128)].astype(F32).reshape(1, wide)
    rec_bias = rec_bias_ref[...].astype(F32)
    rec_bias = jnp.where(here.core == 0, rec_bias[0:1], rec_bias[1:2])
    lens = own_lengths(lens_ref, here.seq * sentences, sentences)
    spots = lax.broadcasted_iota(jnp.int32, (1, LENS), 1)
    line = jnp.zeros((1, LENS), F32)
    for place, value in enumerate(lens):
        line = jnp.where(spots == place, value, line)
    lens_row[...] = line

    def columns(tile):
        return [(hwy_hbm.at[:, pl.ds(side * channels + tile * TILE, TILE)], side) for side in range(2)]

    hwy_loads = {}

    def hwy_start(tile):
        if tile < tiles:
            slot = tile % hwy_slots.shape[0]
            hwy_loads[tile] = [
                pltpu.make_async_copy(source, hwy_slots.at[slot, side], hwy_sems.at[slot, side])
                for source, side in columns(tile)
            ]
            for load in hwy_loads[tile]:
                load.start()

    loads = [
        pltpu.make_async_copy(in_hbm.at[:, exact(here.core * wide, wide, 128)], in_ref, load_sems.at[0]),
        pltpu.make_async_copy(rec_hbm.at[here.core], rec_ref, load_sems.at[1]),
    ]
    weight_load = pltpu.make_async_copy(weight_hbm, weight_ref, load_sems.at[6])
    weight_load.start()
    greet([device for _, _, device in here.column()] + here.peers())
    swap_lens = remote(lens_row, lens_other, swap_sems.at[0], swap_sems.at[1], here.partner)
    swap_lens.start()
    share = span // groups
    chars_copies = []
    for hop in range(1, groups):
        chars_copies.append(
            remote(
                chars_hbm.at[exact(here.along_place(hop) * sentences, sentences, 1)], chars_box.at[here.seq],
                chars_sems.at[0, hop], chars_sems.at[1, hop], (here.dp, here.along_place(hop)),
            )
        )
    chars_copies.append(
        pltpu.make_async_copy(
            chars_hbm.at[exact(here.seq * sentences, sentences, 1)], chars_box.at[here.seq], chars_sems.at[0, 0]
        )
    )
    for copy in chars_copies:
        copy.start()
    cot_copies = []
    for hop, flip, device in here.column():
        side = (here.core + flip) % 2
        cot_copies.append(
            remote(
                cot_hbm.at[
                    exact(here.along_place(hop) * sentences, sentences, 1), :, exact(side * hidden, hidden, 128)
                ],
                cot_box.at[here.core, here.seq], cot_sems.at[0, 2 * hop + flip], cot_sems.at[1, 2 * hop + flip], device,
            )
        )
    cot_copies.append(
        pltpu.make_async_copy(
            cot_hbm.at[exact(here.seq * sentences, sentences, 1), :, exact(here.core * hidden, hidden, 128)],
            cot_box.at[here.core, here.seq], cot_sems.at[0, 0],
        )
    )
    for tile in range(hwy_slots.shape[0]):
        hwy_start(tile)
    for load in loads:
        load.start()
    weight_load.wait()
    lay_taps(weight_ref, taps_ref)
    ids = row_ids(rows)
    segment, sentence = ids // sentences, ids % sentences
    length = row_lengths(lens, sentence)
    steps = segments * height
    step_ids = row_ids(steps)
    step, lane = step_ids // height, step_ids % height
    step_segment = jnp.where(here.core == 0, step, segments - 1 - step)
    whose, step_sentence = lane // sentences, lane % sentences
    real = lane < 2 * sentences
    order = step_segment * sentences + step_sentence
    mine = real & (whose == here.core)
    theirs = real & (whose != here.core)
    take_own = one_hot(steps, rows, jnp.where(mine, order, -1))
    take_other = one_hot(steps, rows, jnp.where(theirs, order, -1))
    part = segments // groups
    order_2 = ((whose * groups + step_segment // part) * sentences + step_sentence) * part + step_segment % part
    pick = one_hot(steps, 2 * rows, jnp.where(real, order_2, -1))
    live = []
    planes = {}
    for copy in chars_copies:
        copy.wait()
    for copy in cot_copies:
        copy.start()
    chars = chars_box[...].reshape(sentences * span, embed)
    for place in range(STRIDE):
        time = segment * STRIDE + place
        alive = time < length
        live.append(alive.astype(F32))
        target = jnp.where(alive, (time // share * sentences + sentence) * share + time % share, -1)
        plane = dot(one_hot(rows, sentences * span, target), chars)
        for hop in (-1, 0, 1):
            planes[hop, place] = shift_rows(plane, -hop * sentences).astype(BF16)
    turned = {key: plane.T for key, plane in planes.items()}
    for place in range(STRIDE):
        for tap in range(NWID):
            spot = place + tap - LEAD
            key = (spot // STRIDE, spot % STRIDE)
            stack_ref[place, :, tap * embed : (tap + 1) * embed] = planes[key]
            cross_ref[tap * embed : (tap + 1) * embed, place * rows : (place + 1) * rows] = turned[key]
    count = jnp.clip(length - STRIDE * segment, 0, STRIDE).astype(F32)
    scale = 1.0 / jnp.maximum(count, 1.0)

    for source, out, flag in ((cross_ref, cross_hbm, 2), (taps_ref, taps_hbm, 3)):
        copy = pltpu.make_async_copy(source, out, load_sems.at[flag])
        copy.start()
        waits.append(copy.wait)

    def stored(slots, out, sems, tile, copies):
        slot = tile % slots.shape[0]
        if tile >= slots.shape[0]:
            copies[tile - slots.shape[0]].wait()
        copies.append(pltpu.make_async_copy(slots.at[slot], out.at[tile], sems.at[slot]))
        return slots.at[slot]

    slope_copies, factor_copies = [], []
    for tile, (low, high) in enumerate(tile_taps(filters)):
        cols = slice(tile * TILE, (tile + 1) * TILE)
        total = jnp.zeros((rows, TILE), F32)
        conv_bias = conv_bias_ref[pl.ds(tile * TILE, TILE)].astype(F32).reshape(1, TILE)
        slot = stored(slope_slots, slope_hbm, slope_sems, tile, slope_copies)
        for place in range(STRIDE):
            pre = dot_nt(
                stack_ref[place, :, low * embed : high * embed],
                taps_ref[cols, low * embed : high * embed],
            ) + conv_bias
            gate = sigmoid(pre)
            act = pre * gate
            total = total + act * live[place]
            slot[place] = (gate + act * (1.0 - gate)).astype(BF16)
        slope_copies[tile].start()
        pooled_ref[:, cols] = (total * scale).astype(BF16)

    def gather(source, out, sems):
        side = math.isqrt(here.chips)
        half = rows // 2
        stay = pltpu.make_async_copy(source, out.at[here.chip], sems.at[0, 0])
        firsts, seconds, onwards = [], [], []
        flag = 1
        for axis in range(2):
            at = pl.ds(axis * half, half)
            for hop in range(1, side):
                chip = here.grid(axis, hop)
                firsts.append(
                    remote(
                        source.at[at], out.at[here.chip, at], sems.at[0, flag], sems.at[1, flag],
                        (chip * 2 + here.core, here.seq),
                    )
                )
                came = here.grid(axis, side - hop)
                flag += 1
                for hop_2 in range(1, side):
                    chip = here.grid(1 - axis, hop_2)
                    onwards.append(
                        (
                            firsts[-1],
                            remote(
                                out.at[came, at], out.at[came, at], sems.at[0, flag], sems.at[1, flag],
                                (chip * 2 + here.core, here.seq),
                            ),
                        )
                    )
                    flag += 1
            for hop in range(1, side):
                chip = here.grid(1 - axis, hop)
                seconds.append(
                    remote(
                        source.at[at], out.at[here.chip, at], sems.at[0, flag], sems.at[1, flag],
                        (chip * 2 + here.core, here.seq),
                    )
                )
                flag += 1
        for copy in [stay] + firsts + seconds:
            copy.start()
        waits.extend([stay.wait] + [copy.wait_send for copy in firsts] + [copy.wait for copy in seconds])
        return onwards

    pool_onwards = gather(pooled_ref, pool_all, pool_sems)
    for tile in range(tiles):
        cols = slice(tile * TILE, (tile + 1) * TILE)
        cols_2 = slice(channels + tile * TILE, channels + (tile + 1) * TILE)
        for load in hwy_loads[tile]:
            load.wait()
        slot = tile % hwy_slots.shape[0]
        pre_1 = dot(pooled_ref[...], hwy_slots[slot, 0]) + hwy_bias_ref[:, cols].astype(F32)
        pre_2 = dot(pooled_ref[...], hwy_slots[slot, 1]) + hwy_bias_ref[:, cols_2].astype(F32)
        hwy_start(tile + hwy_slots.shape[0])
        layer_in = pooled_ref[:, cols].astype(F32)
        gate, inner = sigmoid(pre_2), sigmoid(pre_1)
        act = pre_1 * inner
        off = 1.0 - gate
        high_ref[:, cols] = (gate * act + off * layer_in).astype(BF16)
        factor = stored(factor_slots, factor_hbm, factor_sems, tile, factor_copies)
        factor[0] = gate * (inner + act * (1.0 - inner))
        factor[1] = (act - layer_in) * gate * off
        factor[2] = off
        factor_copies[tile].start()
    swap = remote(high_ref, other_ref, swap_sems.at[2], swap_sems.at[3], here.partner)
    swap.start()
    high_onwards = gather(high_ref, high_all, high_sems)
    for copies, slots in ((slope_copies, slope_slots), (factor_copies, factor_slots)):
        waits.extend(copy.wait for copy in copies[-slots.shape[0] :])

    swap_lens.wait()
    lens_2 = row_values(lens_other, sentences)
    length = jnp.where(mine, row_lengths(lens, step_sentence), row_lengths(lens_2, step_sentence))
    live = real & (step_segment < (length + STRIDE - 1) // STRIDE)
    emit_ref[...] = jnp.broadcast_to(live.astype(F32), (steps, 128))
    own_part = dot(take_own, high_ref[...])
    swap.wait()
    stepped = (own_part + dot(take_other, other_ref[...])).astype(BF16)
    loads[0].wait()
    gates_ref[...] = dot(stepped, in_ref[...]) + in_bias
    loads[1].wait()

    def ahead(index, state):
        at = pl.ds(pl.multiple_of(index * height, height), height)
        q = dot(state.astype(BF16), rec_ref[...]) + rec_bias
        gates = gates_ref[at, :]
        alive = emit_ref[at, 0:1] > 0.0
        reset = sigmoid(gates[:, :hidden] + q[:, :hidden])
        update = sigmoid(gates[:, hidden : 2 * hidden] + q[:, hidden : 2 * hidden])
        q_n = q[:, 2 * hidden :]
        fresh = jnp.tanh(gates[:, 2 * hidden :] + reset * q_n)
        keep = jnp.where(alive, update, 1.0)
        move = jnp.where(alive, 1.0 - update, 0.0)
        after = move * fresh + keep * state
        prior_ref[at, :] = state
        slope = move * (1.0 - fresh * fresh)
        slope_r = slope * reset
        coef_ref[at, :hidden] = slope_r * q_n * (1.0 - reset)
        coef_ref[at, hidden : 2 * hidden] = (state - fresh) * update * move
        coef_ref[at, 2 * hidden : wide] = slope_r
        coef_ref[at, wide : wide + hidden] = slope
        coef_ref[at, wide + hidden :] = keep
        gates_ref[at, :hidden] = jnp.where(alive, after, 0.0)
        return after

    lax.fori_loop(0, segments, ahead, jnp.zeros((height, hidden), F32), unroll=4)
    for came, onward in pool_onwards + high_onwards:
        came.wait_recv()
        onward.start()
        waits.append(onward.wait)
    states = dot_tn(pick, gates_ref[:, :hidden].astype(BF16)).astype(BF16)
    block = rows // groups
    for whose in range(2):
        for place in range(groups):
            at = (whose * groups + place) * block
            states_ref[whose, place] = states[at : at + block].reshape(sentences, part, hidden)
    seat = (exact(here.seq * sentences, sentences, 1), slice(None), exact(here.core * hidden, hidden, 128))
    for hop, flip, device in here.column():
        copy = remote(
            states_ref.at[(here.core + flip) % 2, here.along_place(hop)], states_out.at[seat],
            states_sems.at[0, 2 * hop + flip], states_sems.at[1, 2 * hop + flip], device,
        )
        copy.start()
        waits.append(copy.wait)
    stay = pltpu.make_async_copy(states_ref.at[here.core, here.seq], states_out.at[seat], states_sems.at[0, 0])
    stay.start()
    waits.append(stay.wait)
    for copy in cot_copies:
        copy.wait()
    cot = cot_box[...].reshape(2 * rows, hidden)
    gates_ref[:, :hidden] = dot(pick, cot) * emit_ref[:, 0:1]
    turned = (slice(0, wide), slice(0, hidden))
    in_ref[turned] = rec_ref[...].T

    def back(index, carried):
        at = pl.ds(pl.multiple_of((segments - 1 - index) * height, height), height)
        total = carried + gates_ref[at, :hidden]
        d_r = total * coef_ref[at, :hidden]
        d_z = total * coef_ref[at, hidden : 2 * hidden]
        d_q = total * coef_ref[at, 2 * hidden : wide]
        d_n = total * coef_ref[at, wide : wide + hidden]
        kept = total * coef_ref[at, wide + hidden :]
        coef_ref[at, :hidden] = d_r
        coef_ref[at, hidden : 2 * hidden] = d_z
        coef_ref[at, 2 * hidden : wide] = d_q
        coef_ref[at, wide : wide + hidden] = d_n
        low = jnp.concatenate([d_r, d_z, d_q], axis=1).astype(BF16)
        return kept + dot(low, in_ref[turned])

    lax.fori_loop(0, segments, back, jnp.zeros((height, hidden), F32), unroll=4)
    recur = coef_ref[:, :wide].astype(BF16)
    fresh = coef_ref[:, wide : wide + hidden].astype(BF16)
    share = 2 * wide // dps
    chunk = chunk_of(share, IN_CHUNKS)
    seat = (slice(None), exact(here.core * wide, wide, 128))
    seat_t = exact(here.core * wide, wide, 16)
    given_t_ref = in_ref.at[pl.ds(0, wide), pl.ds(hidden, rows)]
    keep_t_ref = in_ref.at[pl.ds(0, wide), pl.ds(hidden + rows, rows)]
    for take, ref, ref_t in ((take_other, given_ref, given_t_ref), (take_own, keep_ref, keep_t_ref)):
        ref[:, : 2 * hidden] = dot_tn(take, recur[:, : 2 * hidden]).astype(BF16)
        ref[:, 2 * hidden :] = dot_tn(take, fresh).astype(BF16)
        for row, size, place in chunk_pieces(0, wide, share, chunk):
            ref_t[place : place + size, :] = ref[:, row : row + size].T
        if ref is given_ref:
            copies = [
                remote(ref, pair_hbm.at[seat], swap_sems.at[4], swap_sems.at[5], here.partner),
                remote(ref_t, turned_hbm.at[seat_t], swap_sems.at[6], swap_sems.at[7], here.partner),
            ]
        else:
            copies = [
                pltpu.make_async_copy(ref, pair_hbm.at[seat], load_sems.at[4]),
                pltpu.make_async_copy(ref_t, turned_hbm.at[seat_t], load_sems.at[5]),
            ]
        for copy in copies:
            copy.start()
            waits.append(copy.wait)
    prior = prior_ref[...].astype(BF16).T
    sums = jnp.sum(recur.astype(F32), axis=0, keepdims=True)
    sums_n = jnp.sum(fresh.astype(F32), axis=0, keepdims=True)
    rec_tiles = wide // TILE
    bias_ref[...] = jnp.zeros_like(bias_ref)
    for tile in range(rec_tiles):
        cols = slice(tile * TILE, (tile + 1) * TILE)
        rec_part_ref[tile * hidden : (tile + 1) * hidden, :] = dot(prior, recur[:, cols]).astype(BF16)
        if tile * TILE < 2 * hidden:
            bias_ref[tile : tile + 1, :] = sums[:, cols]
        else:
            bias_ref[tile : tile + 1, :] = sums_n[:, tile * TILE - 2 * hidden : (tile + 1) * TILE - 2 * hidden]
        bias_ref[rec_tiles + tile : rec_tiles + tile + 1, :] = sums[:, cols]
    rec_part_ref[rec_tiles * hidden :, :] = bias_ref[...].astype(BF16)
    for wait in waits:
        wait()


class Ring:
    def __init__(self, slots, sems, loads):
        self.slots, self.sems, self.loads = slots, sems, loads
        self.depth = slots.shape[0]
        self.copies = {}

    def start(self, index):
        if index < len(self.loads):
            source, place = self.loads[index]
            slot = index % self.depth
            self.copies[index] = pltpu.make_async_copy(source, place(self.slots.at[slot]), self.sems.at[slot])
            self.copies[index].start()

    def begin(self):
        for index in range(self.depth):
            self.start(index)

    def take(self, index):
        self.copies[index].wait()
        return self.slots.at[index % self.depth]

    def done(self, index):
        self.start(index + self.depth)


def tail_kernel(
    sizes, lens_ref, pair_hbm, turned_hbm, factor_hbm, slope_hbm, cross_hbm, taps_hbm, in_hbm, hwy_hbm, high_hbm, pool_hbm, rec_hbm,
    in_low, hwy_low, conv_out, rec_out, chars_box,
    weight_slots, factor_slots, slope_slots, rows_ref, full_slots,
    pair_ref, gates_own, dpre_ref, pre_t_ref, dy_ref, dconv_ref, bias_ref, chars_ref, cross_ref, taps_ref,
    in_box, hwy_box, in_got, hwy_got, in_outer, hwy_outer, in_inner, hwy_inner,
    conv_part, conv_got, conv_half, conv_box, conv_low, conv_outer, conv_inner, rec_box, rec_low, rec_outer, rec_inner,
    weight_sems, factor_sems, slope_sems, load_sems, in_spread, hwy_spread, chars_sems,
    in_sems, hwy_sems, conv_swap, conv_sems, rec_sems, conv_line, rec_line, conv_share, rec_share,
):
    sentences, span, segments, channels, embed, filters, dps, groups = sizes
    rows = sentences * segments
    tiles = channels // TILE
    wide = pair_hbm.shape[1] // 2
    here = Place(dps, groups)

    def tile_at(tile):
        return pl.ds(tile * TILE, TILE)

    weights = Ring(
        weight_slots, weight_sems,
        [(in_hbm.at[tile_at(tile)], lambda slot: slot.at[:, pl.ds(0, 2 * wide)]) for tile in range(tiles)]
        + [(hwy_hbm.at[tile_at(tile)], lambda slot: slot) for tile in range(tiles)],
    )
    factors = Ring(factor_slots, factor_sems, [(factor_hbm.at[tile], lambda slot: slot) for tile in range(tiles)])
    slopes = Ring(slope_slots, slope_sems, [(slope_hbm.at[tile], lambda slot: slot) for tile in range(tiles)])
    pair_load = pltpu.make_async_copy(pair_hbm, pair_ref, load_sems.at[0])
    pair_load.start()
    taps_load = pltpu.make_async_copy(taps_hbm, taps_ref, load_sems.at[1])
    cross_load = pltpu.make_async_copy(cross_hbm, cross_ref, load_sems.at[2])
    in_share, hwy_share = in_got.shape[0] * in_got.shape[1], hwy_got.shape[0] * hwy_got.shape[1]
    own_load = pltpu.make_async_copy(
        turned_hbm.at[exact(here.chip * 2 * in_share, 2 * in_share, 16)], gates_own, load_sems.at[4]
    )
    own_load.start()
    rows_load = pltpu.make_async_copy(high_hbm, rows_ref, load_sems.at[5])
    rows_load_2 = pltpu.make_async_copy(pool_hbm, rows_ref, load_sems.at[5])
    rows_load.start()
    weights.begin()
    factors.begin()
    greet([here.partner] + here.peers() + here.along())
    rec_load = pltpu.make_async_copy(
        rec_hbm.at[exact(here.chip * rec_low.shape[0], rec_low.shape[0], 16)], rec_low, load_sems.at[3]
    )
    rec_load.start()
    ids = row_ids(rows)
    segment, sentence = ids // sentences, ids % sentences
    length = row_lengths(own_lengths(lens_ref, here.seq * sentences, sentences), sentence)
    count = jnp.clip(length - STRIDE * segment, 0, STRIDE).astype(F32)
    scale = 1.0 / jnp.maximum(count, 1.0)
    bias_ref[...] = jnp.zeros_like(bias_ref)
    sent = []
    waits = []

    def spread(source, box, sends):
        share = box.shape[1]
        copies = []
        for hop in range(1, here.chips):
            at = exact(here.peer_chip(hop) * share, share, 16)
            copies.append(
                remote(source.at[at], box.at[hop - 1], sends.at[0, hop], sends.at[1, hop], here.peer(hop))
            )
            copies[-1].start()
        sent.extend(copies)
        return copies

    def chunk_spread(source, box, sends, share, chunk):
        lists = []
        for turn in range(share // chunk):
            lists.append([])
            for hop in range(1, here.chips):
                at = exact(here.peer_chip(hop) * 2 * share + turn * 2 * chunk, 2 * chunk, 16)
                lists[-1].append(
                    remote(
                        source.at[at], box.at[hop - 1, pl.ds(turn * 2 * chunk, 2 * chunk)],
                        sends.at[0, turn, hop], sends.at[1, turn, hop], here.peer(hop),
                    )
                )
                lists[-1][-1].start()
            sent.extend(lists[-1])
        return lists

    in_chunk, hwy_chunk = in_got.shape[1], hwy_got.shape[1]
    in_lists = chunk_spread(turned_hbm, in_box, in_spread, in_share, in_chunk)
    rec_copies = spread(rec_hbm, rec_box, rec_sems)
    pair_load.wait()

    def hwy_back(tile):
        cols = slice(tile * TILE, (tile + 1) * TILE)
        cols_2 = slice(channels + tile * TILE, channels + (tile + 1) * TILE)
        weight = weights.take(tile)
        dy = dot_nt(pair_ref[...], weight[:, : 2 * wide])
        weights.done(tile)
        factor = factors.take(tile)
        d_1 = (dy * factor[0]).astype(BF16)
        d_2 = (dy * factor[1]).astype(BF16)
        dy_ref[:, cols] = dy * factor[2]
        factors.done(tile)
        dpre_ref[:, cols] = d_1
        dpre_ref[:, cols_2] = d_2
        for at, turned in ((cols, d_1.T), (cols_2, d_2.T)):
            for row, size, place in chunk_pieces(at.start, at.stop, hwy_share, hwy_chunk):
                pre_t_ref[place : place + size, :] = turned[row - at.start : row - at.start + size]
        bias_ref[tiles + tile : tiles + tile + 1, :] = jnp.sum(d_1.astype(F32), axis=0, keepdims=True)
        bias_ref[2 * tiles + tile : 2 * tiles + tile + 1, :] = jnp.sum(d_2.astype(F32), axis=0, keepdims=True)

    hwy_lists = []

    def hwy_send():
        hwy_lists.extend(chunk_spread(pre_t_ref, hwy_box, hwy_spread, hwy_share, hwy_chunk))
        slopes.begin()
        taps_load.start()
        cross_load.start()

    def conv_back(tile):
        cols = slice(tile * TILE, (tile + 1) * TILE)
        weight = weights.take(tiles + tile)
        dy = (dy_ref[:, cols] + dot_nt(dpre_ref[...], weight[...])) * scale
        weights.done(tiles + tile)
        slope = slopes.take(tile)
        sums = jnp.zeros((1, TILE), F32)
        for place in range(STRIDE):
            alive = (segment * STRIDE + place < length).astype(F32)
            part = (dy * alive * slope[place].astype(F32)).astype(BF16)
            dconv_ref[place * rows : (place + 1) * rows, cols] = part
            sums = sums + jnp.sum(part.astype(F32), axis=0, keepdims=True)
        slopes.done(tile)
        bias_ref[tile : tile + 1, :] = sums

    spans = tile_taps(filters)
    starts = [0]
    for low, high in spans:
        starts.append(starts[-1] + (high - low) * embed)
    sums = {}
    half = conv_half.shape[0]
    conv_copy = remote(
        conv_part.at[exact((1 - here.core) * half, half, 16)], conv_got, conv_swap.at[0], conv_swap.at[1], here.partner
    )
    conv_copies = []

    def chars_part(begin_tap):
        begin = min(tile for tile, (low, high) in enumerate(spans) if low < begin_tap + 2 and high > begin_tap)
        part = dot(
            dconv_ref[:, begin * TILE :],
            taps_ref[begin * TILE :, begin_tap * embed : (begin_tap + 2) * embed],
        )
        for tap in (begin_tap, begin_tap + 1):
            for place in range(STRIDE):
                spot = place + tap - LEAD
                key = (spot // STRIDE, spot % STRIDE)
                piece = part[
                    place * rows : (place + 1) * rows, (tap - begin_tap) * embed : (tap - begin_tap + 1) * embed
                ]
                sums[key] = sums[key] + piece if key in sums else piece

    def chars_end():
        total = jnp.zeros((sentences * span, embed), F32)
        out_ids = row_ids(sentences * span)
        out_sentence, out_time = out_ids // span, out_ids % span
        for place in range(STRIDE):
            plane = jnp.zeros((rows, embed), F32)
            for hop in (-1, 0, 1):
                if (hop, place) in sums:
                    plane = plane + shift_rows(sums[hop, place], hop * sentences)
            plane = jnp.where(segment * STRIDE + place < length, plane, 0.0).astype(BF16)
            target = jnp.where(
                out_time % STRIDE == place, (out_time // STRIDE) * sentences + out_sentence, -1
            )
            total = total + dot(one_hot(sentences * span, rows, target), plane)
        for index in range(sentences):
            chars_ref[index] = total[index * span : (index + 1) * span].astype(BF16)
        chars_box[here.seq] = chars_ref[:, exact(here.seq * chars_share, chars_share, 16), :]

    chars_share = span // groups
    chars_copies = []
    for hop in range(1, groups):
        at = exact(here.along_place(hop) * chars_share, chars_share, 16)
        chars_copies.append(
            remote(
                chars_ref.at[:, at], chars_box.at[here.seq], chars_sems.at[0, hop], chars_sems.at[1, hop],
                (here.dp, here.along_place(hop)),
            )
        )
    waits.extend(copy.wait for copy in chars_copies)

    def chars_send(across):
        for hop, copy in enumerate(chars_copies):
            other = (here.along_place(hop + 1) < groups // 2) != (here.seq < groups // 2)
            pl.when(other if across else jnp.logical_not(other))(copy.start)

    def taps_part(tile):
        low, high = spans[tile]
        conv_part[starts[tile] : starts[tile + 1], :] = dot(
            cross_ref[low * embed : high * embed, :], dconv_ref[:, tile * TILE : (tile + 1) * TILE]
        ).astype(BF16)

    def taps_end():
        conv_part[starts[-1] :, :] = bias_ref[...].astype(BF16)
        conv_copy.start()
        sent.append(conv_copy)

    def conv_send():
        conv_copy.wait_recv()
        mine = conv_part[exact(here.core * half, half, 16), :]
        conv_half[...] = (mine.astype(F32) + conv_got[...].astype(F32)).astype(BF16)
        conv_copies.extend(spread(conv_half, conv_box, conv_sems))
        share = conv_low.shape[0]
        conv_low[...] = conv_half[exact(here.chip * share, share, 16), :]

    tasks = [cross_load.wait]
    tasks += [functools.partial(taps_part, tile) for tile in range(tiles)]
    tasks += [taps_end, taps_load.wait, functools.partial(chars_part, 0), conv_send]
    tasks += [functools.partial(chars_part, begin_tap) for begin_tap in range(2, NWID, 2)] + [chars_end]

    halves = []

    def multiply(box, own, own_first, lists, low, got, sems, turn):
        chunk = got.shape[1]
        index = len(halves)
        full = full_slots.at[index % full_slots.shape[0], pl.ds(0, 2 * chunk)]
        if index >= full_slots.shape[0]:
            halves[index - full_slots.shape[0]].wait_send()
        for copy in lists[turn]:
            copy.wait_recv()
        at = pl.ds(turn * 2 * chunk, 2 * chunk)
        for tile in range(tiles):
            cols = slice(tile * TILE, (tile + 1) * TILE)
            total = dot(own[exact(own_first + turn * 2 * chunk, 2 * chunk, 16), :], rows_ref[here.chip, :, cols])
            for hop in range(1, here.chips):
                chip = (here.chip + here.chips - hop) % here.chips
                total = total + dot(box[hop - 1, at, :], rows_ref[chip, :, cols])
            full[:, cols] = total.astype(BF16)
        low[turn] = full[exact(here.core * chunk, chunk, 16), :]
        copy = remote(
            full.at[exact((1 - here.core) * chunk, chunk, 16)], got.at[turn],
            sems.at[turn, 0, 0], sems.at[turn, 0, 1], here.partner,
        )
        copy.start()
        halves.append(copy)

    def line_item(found, low, from_outer, from_inner, sem, keep=None):
        out_to_in = remote(low, from_outer, sem(2), sem(3), here.inner)
        across = remote(low, from_inner, sem(2), sem(4), here.inner)
        in_to_out = remote(low, from_inner, sem(5), sem(4), here.outer)

        def inward():
            low[...] = found().astype(BF16)

            @pl.when(here.has_outer)
            def _():
                out_to_in.wait_recv()
                low[...] = (low[...].astype(F32) + from_outer[...].astype(F32)).astype(BF16)

            @pl.when(here.middle)
            def _():
                across.start()

            @pl.when(jnp.logical_not(here.middle))
            def _():
                out_to_in.start()

        def outward():
            across.wait()

            @pl.when(here.middle)
            def _():
                low[...] = (low[...].astype(F32) + from_inner[...].astype(F32)).astype(BF16)

            @pl.when(jnp.logical_not(here.middle))
            def _():
                low[...] = from_inner[...]

            @pl.when(here.has_outer)
            def _():
                in_to_out.start()

            if keep is not None:
                keep()

        def finish():
            @pl.when(here.has_outer)
            def _():
                in_to_out.wait_send()

        return inward, outward, finish

    onward = []

    def share_out(out, low, begin, size, sems):
        base = here.core * (out.shape[0] // 2) + begin
        share = low.shape[0]
        piece = low.at[pl.ds(begin, size)]
        at = exact(base + here.chip * share, size, 16)
        stay = pltpu.make_async_copy(piece, out.at[at], sems.at[2, 0])
        copies = [remote(piece, out.at[at], sems.at[0, 0], sems.at[1, 0], here.partner)]
        for hop in range(1, here.chips):
            copies.append(remote(piece, out.at[at], sems.at[0, hop], sems.at[1, hop], here.peer(hop)))
            source = (here.chip + here.chips - hop) % here.chips
            place = exact(base + source * share, size, 16)
            send_on = remote(out.at[place], out.at[place], sems.at[2, hop], sems.at[3, hop], here.partner)
            onward.append((copies[hop], send_on))
            waits.append(send_on.wait)
        waits.extend(copy.wait_send for copy in copies)
        waits.append(copies[0].wait_recv)
        waits.append(stay.wait)

        def keep():
            stay.start()
            for copy in copies:
                copy.start()

        return keep

    def chunk_items(low, got, first, outer, inner, sems, finer):
        found_lists = []

        def found(turn, part, at):
            if part == 0:
                halves[first + turn].wait_recv()
            return low[turn, :, at].astype(F32) + got[turn, :, at].astype(F32)

        for turn in range(low.shape[0]):
            count = ENDING if turn == finer else HALVES
            cuts = [-(-tiles * part // count) * TILE if count > 2 else part * channels // count for part in range(count + 1)]
            found_lists.append([])
            for part, (begin, end) in enumerate(zip(cuts, cuts[1:])):
                at = (turn, slice(None), pl.ds(begin, end - begin))
                found_lists[-1].append(
                    line_item(
                        functools.partial(found, turn, part, slice(begin, end)), low.at[at], outer.at[at], inner.at[at],
                        lambda index, turn=turn, part=part: sems.at[turn, 1 + part, index],
                    )
                )
        return found_lists

    def small_items(low, box, copies, outer, inner, line_sems, share_sems, out, ready):
        found_items = []
        size = low.shape[0] // 16
        cuts = [size * part // SMALL_PARTS * 16 for part in range(SMALL_PARTS + 1)]

        def found(part):
            if part == 0:
                ready()
                for copy in copies:
                    copy.wait_recv()
            at = slice(cuts[part], cuts[part + 1])
            total = low[at, :].astype(F32)
            for hop in range(here.chips - 1):
                total = total + box[hop, at, :].astype(F32)
            return total

        for part in range(SMALL_PARTS):
            at = pl.ds(cuts[part], cuts[part + 1] - cuts[part])
            found_items.append(
                line_item(
                    functools.partial(found, part), low.at[at], outer.at[at], inner.at[at],
                    lambda index, part=part: line_sems.at[part, index],
                    share_out(out, low, cuts[part], cuts[part + 1] - cuts[part], share_sems.at[part]),
                )
            )
        return found_items

    in_items = chunk_items(in_low, in_got, 0, in_outer, in_inner, in_sems, 0)
    hwy_items = chunk_items(hwy_low, hwy_got, in_low.shape[0], hwy_outer, hwy_inner, hwy_sems, hwy_low.shape[0] - 1)
    rec_items = small_items(
        rec_low, rec_box, rec_copies, rec_outer, rec_inner, rec_line, rec_share, rec_out, rec_load.wait
    )
    conv_items = small_items(
        conv_low, conv_box, conv_copies, conv_outer, conv_inner, conv_line, conv_share, conv_out, lambda: None
    )

    def in_multiply(turn):
        if turn == 0:
            own_load.wait()
            rows_load.wait()
        multiply(in_box, gates_own, 0, in_lists, in_low, in_got, in_sems, turn)
        if turn + 1 == in_low.shape[0]:
            rows_load_2.start()

    def hwy_multiply(turn):
        if turn == 0:
            rows_load_2.wait()
        multiply(hwy_box, pre_t_ref, here.chip * 2 * hwy_share, hwy_lists, hwy_low, hwy_got, hwy_sems, turn)

    tasks = [hwy_send] + [functools.partial(conv_back, tile) for tile in range(tiles)] + tasks
    tasks = [functools.partial(hwy_back, tile) for tile in range(tiles)] + tasks
    items = []
    plan = []

    def add(new):
        plan.extend(new)

    add([tiles + 1])
    for turn in range(in_low.shape[0]):
        add([functools.partial(in_multiply, turn), 1])
        for item in in_items[turn]:
            add([item, 1 if turn == 0 else 2])
    for item in rec_items:
        add([2, item])
    last = hwy_low.shape[0] - 1
    for turn in range(last):
        if turn == (last + 1) // 2:
            add(conv_items)
        add([functools.partial(hwy_multiply, turn), 1])
        for item in hwy_items[turn]:
            add([2, item])
    if last < 1:
        add([len(tasks)] + conv_items)
    add([functools.partial(hwy_multiply, last), len(tasks)])
    for item in hwy_items[last]:
        add([item])
    depths = groups // 2

    def outwards(index):
        for depth in range(depths):
            ready = index - 2 - LAG * depth
            if 0 <= ready < len(items):
                pl.when(here.depth == depth)(items[ready][1])

    for step in plan:
        if isinstance(step, int):
            for task in tasks[:step]:
                task()
            del tasks[:step]
        elif isinstance(step, tuple):
            items.append(step)
            step[0]()
            outwards(len(items) - 1)
        else:
            step()
    chars_send(True)
    for extra in range(2 + LAG * (depths - 1)):
        outwards(len(items) + extra)
        if extra == 1:
            chars_send(False)
    for copy, send_on in onward:
        copy.wait_recv()
        send_on.start()
    for item in items:
        item[2]()
    for copy in sent:
        copy.wait_send()
    for copy in halves[-full_slots.shape[0] :]:
        copy.wait_send()
    for wait in waits:
        wait()


def finish_kernel(
    sizes, in_hbm, hwy_hbm, conv_hbm, rec_hbm, chars_hbm,
    in_out, hwy_out, conv_out, rec_out, chars_out, conv_bias_out, hwy_bias_out, in_bias_out, rec_bias_out,
    in_ref, hwy_ref, conv_ref, rec_ref, chars_ref, in_full, hwy_full, conv_full, rec_full, chars_full,
    load_sems, store_sems,
):
    embed, filters, hidden = sizes
    tiles = in_ref.shape[2] // TILE
    half = rec_ref.shape[0] // 2
    loads = [
        pltpu.make_async_copy(rec_hbm.at[pl.ds(side * half, half)], rec_ref.at[pl.ds(side * half, half)], load_sems.at[side])
        for side in range(2)
    ]
    for place, (source, ref) in enumerate(((hwy_hbm, hwy_ref), (conv_hbm, conv_ref), (in_hbm, in_ref), (chars_hbm, chars_ref))):
        loads.append(pltpu.make_async_copy(source, ref, load_sems.at[2 + place]))
    for load in loads:
        load.start()
    stores = []

    def store(source, out):
        stores.append(pltpu.make_async_copy(source, out, store_sems.at[len(stores)]))
        stores[-1].start()

    rec_tiles = 3 * hidden // TILE
    for side in range(2):
        loads[side].wait()
        for tile in range(rec_tiles):
            row = side * half + tile * hidden
            at = slice(tile * TILE, (tile + 1) * TILE)
            rec_full[side, :, at] = rec_ref[row : row + hidden, :].astype(F32)
        store(rec_full.at[side], rec_out.at[side])
        row = side * half + rec_tiles * hidden
        rest = rec_ref[row : row + 16, :].astype(F32)
        for tile in range(rec_tiles):
            at = slice(tile * TILE, (tile + 1) * TILE)
            in_bias_out[pl.ds((side * rec_tiles + tile) * TILE, TILE)] = rest[tile]
            rec_bias_out[side : side + 1, at] = rest[rec_tiles + tile : rec_tiles + tile + 1]
    loads[2].wait()
    hwy_full[...] = hwy_ref[...].astype(F32).reshape(hwy_full.shape)
    store(hwy_full, hwy_out)
    loads[3].wait()
    spans = tile_taps(filters)
    starts = [0]
    for low, high in spans:
        starts.append(starts[-1] + (high - low) * embed)
    for width in range(1, NWID + 1):
        lead, first = (width - 1) // 2, width * (width - 1) // 2
        for tap in range(width):
            spot = LEAD - lead + tap
            begin, end = (width - 1) * filters, width * filters
            while begin < end:
                tile = begin // TILE
                stop = min(end, (tile + 1) * TILE)
                row = starts[tile] + (spot - spans[tile][0]) * embed
                piece = conv_ref[row : row + embed, :].astype(F32).T
                at = slice(begin - (width - 1) * filters, stop - (width - 1) * filters)
                conv_full[first + tap, at, :] = piece[begin - tile * TILE : stop - tile * TILE]
                begin = stop
    store(conv_full, conv_out)
    rest = conv_ref[starts[-1] :, :].astype(F32)
    for tile in range(tiles):
        at = slice(tile * TILE, (tile + 1) * TILE)
        conv_bias_out[pl.ds(tile * TILE, TILE)] = rest[tile]
    for tile in range(2 * tiles):
        hwy_bias_out[:, tile * TILE : (tile + 1) * TILE] = rest[tiles + tile : tiles + tile + 1]
    loads[4].wait()
    for turn in range(in_ref.shape[0]):
        at = slice(turn * in_ref.shape[1], (turn + 1) * in_ref.shape[1])
        in_full[:, at] = in_ref[turn].astype(F32).T
    store(in_full, in_out)
    loads[5].wait()
    chars_full[...] = chars_ref[...].astype(F32).reshape(chars_full.shape)
    store(chars_full, chars_out)
    for copy in stores:
        copy.wait()


VMEM = pl.BlockSpec(memory_space=pltpu.VMEM)
SMEM = pl.BlockSpec(memory_space=pltpu.SMEM)
ANY = pl.BlockSpec(memory_space=pl.ANY)


def params(**more):
    return pltpu.CompilerParams(vmem_limit_bytes=VMEM_LIMIT, **more)


def shape(*dims, dtype=F32):
    return jax.ShapeDtypeStruct(dims, dtype)


def block(*dims, dtype=BF16):
    return pltpu.VMEM(dims, dtype)


def flags(*dims):
    return pltpu.SemaphoreType.DMA(dims)


def head_call(sizes, hidden, dps, groups, given):
    sentences, span, segments, channels, embed, filters = sizes
    wide, rows, chips, tiles = 3 * hidden, sentences * segments, dps // 2, channels // TILE
    height = max(8, 2 * sentences)
    steps, part = segments * height, segments // groups
    rec_rows = wide // TILE * hidden + 16 * chips
    side = math.isqrt(chips)
    copies = 1 + 2 * (side - 1) * (side + 1)
    return pl.pallas_call(
        functools.partial(head_kernel, sizes + (hidden, height, dps, groups)),
        name="head",
        out_shape=[
            shape(groups * sentences, part, 2 * hidden, dtype=BF16),
            shape(chips, rows, channels, dtype=BF16),
            shape(chips, rows, channels, dtype=BF16),
            shape(tiles, STRIDE, rows, TILE, dtype=BF16),
            shape(tiles, 3, rows, TILE),
            shape(NWID * embed, STRIDE * rows, dtype=BF16),
            shape(channels, NWID * embed, dtype=BF16),
            shape(rows, 2 * wide, dtype=BF16),
            shape(2 * wide, rows, dtype=BF16),
            shape(rec_rows, TILE, dtype=BF16),
        ],
        in_specs=[SMEM] + [VMEM] * 4 + [ANY] * 6,
        out_specs=[VMEM] + [ANY] * 8 + [VMEM],
        scratch_shapes=[
            block(NWID * (NWID + 1) // 2, filters, embed),
            block(NWID * embed, STRIDE * rows),
            block(channels, NWID * embed),
            block(rows, wide),
            block(1, LENS, dtype=F32),
            block(1, LENS, dtype=F32),
            block(groups, sentences, span // groups, embed),
            block(4 if chips <= 8 else 2, 2, channels, TILE),
            block(STRIDE, rows, NWID * embed),
            block(tiles if chips <= 8 else 2, STRIDE, rows, TILE),
            block(tiles if chips <= 8 else 2, 3, rows, TILE, dtype=F32),
            block(rows, channels),
            block(rows, channels),
            block(rows, channels),
            block(channels, wide),
            block(hidden, wide),
            block(steps, wide, dtype=F32),
            block(steps, 5 * hidden, dtype=F32),
            block(steps, hidden, dtype=F32),
            block(steps, 128, dtype=F32),
            block(2, groups, sentences, part, hidden),
            block(2, groups, sentences, part, hidden),
            block(rows, wide),
            block(16 * chips, TILE, dtype=F32),
            flags(4, 2), flags(tiles), flags(tiles), flags(7), flags(8), flags(2, groups), flags(2, 2 * groups),
            flags(2, 2 * groups), flags(2, copies), flags(2, copies),
        ],
        compiler_params=params(collective_id=2, has_side_effects=True),
    )(*given)


def tail_call(sizes, hidden, dps, groups, given):
    sentences, span, segments, channels, embed, filters = sizes
    wide, rows, chips = 3 * hidden, sentences * segments, dps // 2
    rec_rows = wide // TILE * hidden + 16 * chips
    tiles = channels // TILE
    in_share, hwy_share = 2 * wide // dps, 2 * channels // dps
    spans = tile_taps(filters)
    conv_rows = (sum(high - low for low, high in spans) + 1) * embed

    def slots(lead, share):
        return pltpu.VMEM((lead, share, TILE), BF16)

    in_chunk, hwy_chunk = chunk_of(in_share, IN_CHUNKS), chunk_of(hwy_share, HWY_CHUNKS)
    in_turns, hwy_turns = in_share // in_chunk, hwy_share // hwy_chunk
    conv_share, rec_share = conv_rows // dps, rec_rows // chips
    return pl.pallas_call(
        functools.partial(tail_kernel, sizes + (dps, groups)),
        name="tail",
        out_shape=[
            shape(in_turns, in_chunk, channels, dtype=BF16),
            shape(hwy_turns, hwy_chunk, channels, dtype=BF16),
            shape(conv_rows, TILE, dtype=BF16),
            shape(2 * rec_rows, TILE, dtype=BF16),
            shape(groups, sentences, span // groups, embed, dtype=BF16),
        ],
        in_specs=[SMEM] + [ANY] * 11,
        out_specs=[VMEM, VMEM, ANY, ANY, VMEM],
        scratch_shapes=[
            block(3 if chips <= 8 else 2, TILE, 2 * channels),
            block(2, 3, rows, TILE, dtype=F32),
            block(2, STRIDE, rows, TILE),
            block(chips, rows, channels),
            block(2, 2 * max(in_chunk, hwy_chunk), channels),
            block(rows, 2 * wide),
            block(2 * in_share, rows),
            block(rows, 2 * channels),
            block(2 * channels, rows),
            block(rows, channels, dtype=F32),
            block(STRIDE * rows, channels),
            block(embed, TILE, dtype=F32),
            block(sentences, span, embed),
            block(NWID * embed, STRIDE * rows),
            block(channels, NWID * embed),
            block(chips - 1, 2 * in_share, rows),
            block(chips - 1, 2 * hwy_share, rows),
            block(in_turns, in_chunk, channels), block(hwy_turns, hwy_chunk, channels),
            block(in_turns, in_chunk, channels), block(hwy_turns, hwy_chunk, channels),
            block(in_turns, in_chunk, channels), block(hwy_turns, hwy_chunk, channels),
            block(conv_rows, TILE),
            block(conv_rows // 2, TILE),
            block(conv_rows // 2, TILE),
            slots(chips - 1, conv_share),
            block(conv_share, TILE),
            block(conv_share, TILE),
            block(conv_share, TILE),
            slots(chips - 1, rec_share),
            block(rec_share, TILE),
            block(rec_share, TILE),
            block(rec_share, TILE),
            flags(3), flags(2), flags(2), flags(6),
            flags(2, in_turns, chips), flags(2, hwy_turns, chips), flags(2, groups),
            flags(in_turns, 1 + ENDING, 6), flags(hwy_turns, 1 + ENDING, 6), flags(2), flags(2, chips), flags(2, chips),
            flags(SMALL_PARTS, 6), flags(SMALL_PARTS, 6), flags(SMALL_PARTS, 4, chips), flags(SMALL_PARTS, 4, chips),
        ],
        compiler_params=params(collective_id=1, has_side_effects=True),
    )(
        *given
    )


def local(
    char_embeds, lengths, conv_weight, conv_bias, hwy_weight, hwy_bias, gru_in_weight, gru_in_bias,
    gru_rec_weight, gru_rec_bias, out_grad,
):
    groups = lax.axis_size("seq")
    dps = lax.axis_size("dp")
    sentences = char_embeds.shape[0] // groups
    span = char_embeds.shape[1] * groups
    segments = span // STRIDE
    embed, filters = conv_weight.shape[1:]
    channels = NWID * filters
    hidden = gru_rec_weight.shape[1]
    wide = 3 * hidden
    sizes = (sentences, span, segments, channels, embed, filters)
    encoded, pool_all, high_all, slope, factor, cross, taps, pair, turned, rec_part = head_call(
        sizes, hidden, dps, groups,
        (
            lengths, conv_bias, hwy_bias, gru_in_bias, gru_rec_bias, char_embeds, conv_weight.transpose(0, 2, 1), hwy_weight[0], out_grad, gru_in_weight, gru_rec_weight,
        ),
    )
    in_sum, hwy_sum, conv_sum, rec_sum, chars_box = tail_call(
        sizes, hidden, dps, groups,
        (
            lengths, pair, turned, factor, slope, cross, taps, gru_in_weight, hwy_weight[0], high_all, pool_all, rec_part,
        ),
    )
    in_share, hwy_share = 2 * wide // dps, 2 * channels // dps
    whole = [
        (channels, in_share),
        (hwy_share, channels),
        (NWID * (NWID + 1) // 2, filters, embed),
        (2, hidden, wide),
        (groups * sentences, span // groups, embed),
    ]
    in_grad, hwy_grad, conv_grad, rec_grad, dchars, conv_bias_grad, hwy_bias_grad, in_bias_grad, rec_bias_grad = pl.pallas_call(
        functools.partial(finish_kernel, (embed, filters, hidden)),
        name="finish",
        out_shape=[shape(*dims) for dims in whole]
        + [shape(channels), shape(1, 2 * channels), shape(2 * wide), shape(2, wide)],
        in_specs=[ANY] * 5,
        out_specs=[ANY] * 5 + [VMEM] * 4,
        scratch_shapes=[
            block(*part.shape) for part in (in_sum, hwy_sum, conv_sum, rec_sum, chars_box)
        ]
        + [block(*dims, dtype=F32) for dims in whole]
        + [flags(6), flags(6)],
        compiler_params=params(),
    )(in_sum, hwy_sum, conv_sum, rec_sum, chars_box)
    return (
        encoded, dchars, conv_grad.transpose(0, 2, 1), conv_bias_grad, hwy_grad.T[None], hwy_bias_grad, in_grad,
        in_bias_grad, rec_grad, rec_bias_grad,
    )


def solution(mesh):
    whole = P()
    split = P("dp", "seq", None)
    return jax.shard_map(
        local,
        mesh=mesh,
        in_specs=(split, P("dp")) + (whole,) * 8 + (split,),
        out_specs=(split, split, whole, whole, P(None, None, "dp"), whole, P(None, "dp"), whole, whole, whole),
        check_vma=False,
    )
```

```python
import functools
import math

import jax
import jax.numpy as jnp
from jax import lax
from jax.experimental import pallas as pl
from jax.experimental.pallas import tpu as pltpu
from jax.sharding import PartitionSpec as P

MESH = pl.DeviceIdType.MESH
NWID = 8
STRIDE = 5
LEAD = (NWID - 1) // 2
TILE = 256
LENS = 128
SMALL_PARTS = 2
IN_CHUNKS = 4
HWY_CHUNKS = 4
HALVES = 2
ENDING = 4
LAG = 6
F32 = jnp.float32
BF16 = jnp.bfloat16
VMEM_LIMIT = 61 * 2**20


def tile_taps(filters):
    found = []
    for tile in range(NWID * filters // TILE):
        first_width = tile * TILE // filters + 1
        last_width = (tile * TILE + TILE - 1) // filters + 1
        low, high = NWID, 0
        for width in range(first_width, last_width + 1):
            lead = (width - 1) // 2
            low, high = min(low, LEAD - lead), max(high, LEAD - lead + width)
        found.append((low, high))
    return found


def chunk_of(share, most):
    units = share // 16
    return share // max(count for count in range(1, most + 1) if units % count == 0)


def chunk_pieces(first, last, share, chunk):
    pieces = []
    while first < last:
        chip, rest = divmod(first, 2 * share)
        core, rest = divmod(rest, share)
        turn, rest = divmod(rest, chunk)
        size = min(last - first, chunk - rest)
        pieces.append((first, size, chip * 2 * share + turn * 2 * chunk + core * chunk + rest))
        first += size
    return pieces


def lay_taps(weight_ref, taps_ref):
    _, filters, embed = weight_ref.shape
    taps_ref[...] = jnp.zeros_like(taps_ref)
    for width in range(1, NWID + 1):
        for tap in range(width):
            spot = LEAD - (width - 1) // 2 + tap
            taps_ref[(width - 1) * filters : width * filters, spot * embed : (spot + 1) * embed] = weight_ref[
                width * (width - 1) // 2 + tap
            ]


def sigmoid(value):
    return 0.5 * jnp.tanh(0.5 * value) + 0.5


def dot(left, right):
    return jnp.dot(left, right, preferred_element_type=F32)


def dot_nt(left, right):
    return lax.dot_general(left, right, (((1,), (1,)), ((), ())), preferred_element_type=F32)


def dot_tn(left, right):
    return lax.dot_general(left, right, (((0,), (0,)), ((), ())), preferred_element_type=F32)


def one_hot(rows, columns, target):
    places = lax.broadcasted_iota(jnp.int32, (rows, columns), 1)
    return jnp.where(places == target, 1.0, 0.0).astype(BF16)


def row_ids(rows):
    return lax.broadcasted_iota(jnp.int32, (rows, 1), 0)


def shift_rows(value, count):
    if count == 0:
        return value
    rows = value.shape[0]
    ids = row_ids(rows)
    moved = pltpu.roll(value, count % rows, axis=0)
    keep = ids >= count if count > 0 else ids < rows + count
    return jnp.where(keep, moved, 0.0)


class Place:
    def __init__(self, dps, groups):
        self.chips, self.groups = dps // 2, groups
        self.dp, self.seq = lax.axis_index("dp"), lax.axis_index("seq")
        self.chip, self.core = self.dp // 2, self.dp % 2
        self.partner = (self.chip * 2 + 1 - self.core, self.seq)
        half = groups // 2
        low = self.seq < half
        self.inner = (self.dp, jnp.where(low, self.seq + 1, self.seq - 1))
        self.outer = (self.dp, jnp.clip(jnp.where(low, self.seq - 1, self.seq + 1), 0, groups - 1))
        self.has_outer = (self.seq > 0) & (self.seq < groups - 1)
        self.depth = jnp.where(low, half - 1 - self.seq, self.seq - half)
        self.middle = self.depth == 0

    def peer_chip(self, hop):
        return (self.chip + hop) % self.chips

    def peer(self, hop):
        return (self.peer_chip(hop) * 2 + self.core, self.seq)

    def peers(self):
        return [self.peer(hop) for hop in range(1, self.chips)]

    def column(self):
        found = []
        for hop in range(self.groups):
            for flip in range(2):
                if hop or flip:
                    found.append((hop, flip, (self.chip * 2 + (self.core + flip) % 2, self.along_place(hop))))
        return found

    def grid(self, axis, hop):
        side = math.isqrt(self.chips)
        high, low = self.chip // side, self.chip % side
        if axis == 0:
            return (high + hop) % side * side + low
        return high * side + (low + hop) % side

    def along_place(self, hop):
        return (self.seq + hop) % self.groups

    def along(self):
        return [(self.dp, self.along_place(hop)) for hop in range(1, self.groups)]


def greet(devices):
    barrier = pltpu.get_barrier_semaphore()
    for device in devices:
        pl.semaphore_signal(barrier, inc=1, device_id=device, device_id_type=MESH)
    pl.semaphore_wait(barrier, len(devices))


def remote(src, dst, send, recv, device):
    return pltpu.make_async_remote_copy(
        src_ref=src, dst_ref=dst, send_sem=send, recv_sem=recv, device_id=device, device_id_type=MESH
    )


def exact(start, size, unit):
    return pl.ds(pl.multiple_of(start, unit), size)


def row_lengths(lens, which):
    found = jnp.zeros(which.shape, F32)
    for place, value in enumerate(lens):
        found = jnp.where(which == place, value, found)
    return found.astype(jnp.int32)


def own_lengths(lens_ref, first, count):
    return [jnp.full((1, 1), lens_ref[first + place].astype(F32)) for place in range(count)]


def row_values(row_ref, count):
    return [row_ref[:, place : place + 1] for place in range(count)]


def head_kernel(
    sizes, lens_ref, conv_bias_ref, hwy_bias_ref, in_bias_ref, rec_bias_ref, chars_hbm, weight_hbm, hwy_hbm, cot_hbm, in_hbm, rec_hbm,
    states_out, pool_all, high_all, slope_hbm, factor_hbm, cross_hbm, taps_hbm, pair_hbm, turned_hbm, rec_part_ref,
    weight_ref, cross_ref, taps_ref, keep_ref,
    lens_row, lens_other, chars_box, hwy_slots, stack_ref, slope_slots, factor_slots, pooled_ref, high_ref, other_ref,
    in_ref, rec_ref, gates_ref, coef_ref, prior_ref, emit_ref, cot_box, states_ref, given_ref, bias_ref,
    hwy_sems, slope_sems, factor_sems, load_sems, swap_sems, chars_sems, cot_sems, states_sems, pool_sems, high_sems,
):
    sentences, span, segments, channels, embed, filters, hidden, height, dps, groups = sizes
    rows = sentences * segments
    tiles = channels // TILE
    wide = 3 * hidden
    here = Place(dps, groups)
    waits = []
    in_bias = in_bias_ref[exact(here.core * wide, wide, 128)].astype(F32).reshape(1, wide)
    rec_bias = rec_bias_ref[...].astype(F32)
    rec_bias = jnp.where(here.core == 0, rec_bias[0:1], rec_bias[1:2])
    lens = own_lengths(lens_ref, here.seq * sentences, sentences)
    spots = lax.broadcasted_iota(jnp.int32, (1, LENS), 1)
    line = jnp.zeros((1, LENS), F32)
    for place, value in enumerate(lens):
        line = jnp.where(spots == place, value, line)
    lens_row[...] = line

    def columns(tile):
        return [(hwy_hbm.at[:, pl.ds(side * channels + tile * TILE, TILE)], side) for side in range(2)]

    hwy_loads = {}

    def hwy_start(tile):
        if tile < tiles:
            slot = tile % hwy_slots.shape[0]
            hwy_loads[tile] = [
                pltpu.make_async_copy(source, hwy_slots.at[slot, side], hwy_sems.at[slot, side])
                for source, side in columns(tile)
            ]
            for load in hwy_loads[tile]:
                load.start()

    loads = [
        pltpu.make_async_copy(in_hbm.at[:, exact(here.core * wide, wide, 128)], in_ref, load_sems.at[0]),
        pltpu.make_async_copy(rec_hbm.at[here.core], rec_ref, load_sems.at[1]),
    ]
    weight_load = pltpu.make_async_copy(weight_hbm, weight_ref, load_sems.at[6])
    weight_load.start()
    greet([device for _, _, device in here.column()] + here.peers())
    swap_lens = remote(lens_row, lens_other, swap_sems.at[0], swap_sems.at[1], here.partner)
    swap_lens.start()
    share = span // groups
    chars_copies = []
    for hop in range(1, groups):
        chars_copies.append(
            remote(
                chars_hbm.at[exact(here.along_place(hop) * sentences, sentences, 1)], chars_box.at[here.seq],
                chars_sems.at[0, hop], chars_sems.at[1, hop], (here.dp, here.along_place(hop)),
            )
        )
    chars_copies.append(
        pltpu.make_async_copy(
            chars_hbm.at[exact(here.seq * sentences, sentences, 1)], chars_box.at[here.seq], chars_sems.at[0, 0]
        )
    )
    for copy in chars_copies:
        copy.start()
    cot_copies = []
    for hop, flip, device in here.column():
        side = (here.core + flip) % 2
        cot_copies.append(
            remote(
                cot_hbm.at[
                    exact(here.along_place(hop) * sentences, sentences, 1), :, exact(side * hidden, hidden, 128)
                ],
                cot_box.at[here.core, here.seq], cot_sems.at[0, 2 * hop + flip], cot_sems.at[1, 2 * hop + flip], device,
            )
        )
    cot_copies.append(
        pltpu.make_async_copy(
            cot_hbm.at[exact(here.seq * sentences, sentences, 1), :, exact(here.core * hidden, hidden, 128)],
            cot_box.at[here.core, here.seq], cot_sems.at[0, 0],
        )
    )
    for tile in range(hwy_slots.shape[0]):
        hwy_start(tile)
    for load in loads:
        load.start()
    weight_load.wait()
    lay_taps(weight_ref, taps_ref)
    ids = row_ids(rows)
    segment, sentence = ids // sentences, ids % sentences
    length = row_lengths(lens, sentence)
    steps = segments * height
    step_ids = row_ids(steps)
    step, lane = step_ids // height, step_ids % height
    step_segment = jnp.where(here.core == 0, step, segments - 1 - step)
    whose, step_sentence = lane // sentences, lane % sentences
    real = lane < 2 * sentences
    order = step_segment * sentences + step_sentence
    mine = real & (whose == here.core)
    theirs = real & (whose != here.core)
    take_own = one_hot(steps, rows, jnp.where(mine, order, -1))
    take_other = one_hot(steps, rows, jnp.where(theirs, order, -1))
    part = segments // groups
    order_2 = ((whose * groups + step_segment // part) * sentences + step_sentence) * part + step_segment % part
    pick = one_hot(steps, 2 * rows, jnp.where(real, order_2, -1))
    live = []
    planes = {}
    for copy in chars_copies:
        copy.wait()
    for copy in cot_copies:
        copy.start()
    chars = chars_box[...].reshape(sentences * span, embed)
    for place in range(STRIDE):
        time = segment * STRIDE + place
        alive = time < length
        live.append(alive.astype(F32))
        target = jnp.where(alive, (time // share * sentences + sentence) * share + time % share, -1)
        plane = dot(one_hot(rows, sentences * span, target), chars)
        for hop in (-1, 0, 1):
            planes[hop, place] = shift_rows(plane, -hop * sentences).astype(BF16)
    turned = {key: plane.T for key, plane in planes.items()}
    for place in range(STRIDE):
        for tap in range(NWID):
            spot = place + tap - LEAD
            key = (spot // STRIDE, spot % STRIDE)
            stack_ref[place, :, tap * embed : (tap + 1) * embed] = planes[key]
            cross_ref[tap * embed : (tap + 1) * embed, place * rows : (place + 1) * rows] = turned[key]
    count = jnp.clip(length - STRIDE * segment, 0, STRIDE).astype(F32)
    scale = 1.0 / jnp.maximum(count, 1.0)

    for source, out, flag in ((cross_ref, cross_hbm, 2), (taps_ref, taps_hbm, 3)):
        copy = pltpu.make_async_copy(source, out, load_sems.at[flag])
        copy.start()
        waits.append(copy.wait)

    def stored(slots, out, sems, tile, copies):
        slot = tile % slots.shape[0]
        if tile >= slots.shape[0]:
            copies[tile - slots.shape[0]].wait()
        copies.append(pltpu.make_async_copy(slots.at[slot], out.at[tile], sems.at[slot]))
        return slots.at[slot]

    slope_copies, factor_copies = [], []
    for tile, (low, high) in enumerate(tile_taps(filters)):
        cols = slice(tile * TILE, (tile + 1) * TILE)
        total = jnp.zeros((rows, TILE), F32)
        conv_bias = conv_bias_ref[pl.ds(tile * TILE, TILE)].astype(F32).reshape(1, TILE)
        slot = stored(slope_slots, slope_hbm, slope_sems, tile, slope_copies)
        for place in range(STRIDE):
            pre = dot_nt(
                stack_ref[place, :, low * embed : high * embed],
                taps_ref[cols, low * embed : high * embed],
            ) + conv_bias
            gate = sigmoid(pre)
            act = pre * gate
            total = total + act * live[place]
            slot[place] = (gate + act * (1.0 - gate)).astype(BF16)
        slope_copies[tile].start()
        pooled_ref[:, cols] = (total * scale).astype(BF16)

    def gather(source, out, sems):
        side = math.isqrt(here.chips)
        half = rows // 2
        stay = pltpu.make_async_copy(source, out.at[here.chip], sems.at[0, 0])
        firsts, seconds, onwards = [], [], []
        flag = 1
        for axis in range(2):
            at = pl.ds(axis * half, half)
            for hop in range(1, side):
                chip = here.grid(axis, hop)
                firsts.append(
                    remote(
                        source.at[at], out.at[here.chip, at], sems.at[0, flag], sems.at[1, flag],
                        (chip * 2 + here.core, here.seq),
                    )
                )
                came = here.grid(axis, side - hop)
                flag += 1
                for hop_2 in range(1, side):
                    chip = here.grid(1 - axis, hop_2)
                    onwards.append(
                        (
                            firsts[-1],
                            remote(
                                out.at[came, at], out.at[came, at], sems.at[0, flag], sems.at[1, flag],
                                (chip * 2 + here.core, here.seq),
                            ),
                        )
                    )
                    flag += 1
            for hop in range(1, side):
                chip = here.grid(1 - axis, hop)
                seconds.append(
                    remote(
                        source.at[at], out.at[here.chip, at], sems.at[0, flag], sems.at[1, flag],
                        (chip * 2 + here.core, here.seq),
                    )
                )
                flag += 1
        for copy in [stay] + firsts + seconds:
            copy.start()
        waits.extend([stay.wait] + [copy.wait_send for copy in firsts] + [copy.wait for copy in seconds])
        return onwards

    pool_onwards = gather(pooled_ref, pool_all, pool_sems)
    for tile in range(tiles):
        cols = slice(tile * TILE, (tile + 1) * TILE)
        cols_2 = slice(channels + tile * TILE, channels + (tile + 1) * TILE)
        for load in hwy_loads[tile]:
            load.wait()
        slot = tile % hwy_slots.shape[0]
        pre_1 = dot(pooled_ref[...], hwy_slots[slot, 0]) + hwy_bias_ref[:, cols].astype(F32)
        pre_2 = dot(pooled_ref[...], hwy_slots[slot, 1]) + hwy_bias_ref[:, cols_2].astype(F32)
        hwy_start(tile + hwy_slots.shape[0])
        layer_in = pooled_ref[:, cols].astype(F32)
        gate, inner = sigmoid(pre_2), sigmoid(pre_1)
        act = pre_1 * inner
        off = 1.0 - gate
        high_ref[:, cols] = (gate * act + off * layer_in).astype(BF16)
        factor = stored(factor_slots, factor_hbm, factor_sems, tile, factor_copies)
        factor[0] = gate * (inner + act * (1.0 - inner))
        factor[1] = (act - layer_in) * gate * off
        factor[2] = off
        factor_copies[tile].start()
    swap = remote(high_ref, other_ref, swap_sems.at[2], swap_sems.at[3], here.partner)
    swap.start()
    high_onwards = gather(high_ref, high_all, high_sems)
    for copies, slots in ((slope_copies, slope_slots), (factor_copies, factor_slots)):
        waits.extend(copy.wait for copy in copies[-slots.shape[0] :])

    swap_lens.wait()
    lens_2 = row_values(lens_other, sentences)
    length = jnp.where(mine, row_lengths(lens, step_sentence), row_lengths(lens_2, step_sentence))
    live = real & (step_segment < (length + STRIDE - 1) // STRIDE)
    emit_ref[...] = jnp.broadcast_to(live.astype(F32), (steps, 128))
    own_part = dot(take_own, high_ref[...])
    loads[1].wait()
    for side in range(hidden // TILE):
        hwy_slots[0, side, pl.ds(0, wide), :] = rec_ref[pl.ds(side * TILE, TILE), :].T
    swap.wait()
    stepped = (own_part + dot(take_other, other_ref[...])).astype(BF16)
    loads[0].wait()
    gates_ref[...] = dot(stepped, in_ref[...]) + in_bias

    def ahead(index, state):
        at = pl.ds(pl.multiple_of(index * height, height), height)
        q = dot(state.astype(BF16), rec_ref[...]) + rec_bias
        gates = gates_ref[at, :]
        alive = emit_ref[at, 0:1] > 0.0
        reset = sigmoid(gates[:, :hidden] + q[:, :hidden])
        update = sigmoid(gates[:, hidden : 2 * hidden] + q[:, hidden : 2 * hidden])
        q_n = q[:, 2 * hidden :]
        fresh = jnp.tanh(gates[:, 2 * hidden :] + reset * q_n)
        keep = jnp.where(alive, update, 1.0)
        move = jnp.where(alive, 1.0 - update, 0.0)
        after = move * fresh + keep * state
        prior_ref[at, :] = state
        slope = move * (1.0 - fresh * fresh)
        slope_r = slope * reset
        coef_ref[at, :hidden] = slope_r * q_n * (1.0 - reset)
        coef_ref[at, hidden : 2 * hidden] = (state - fresh) * update * move
        coef_ref[at, 2 * hidden : wide] = slope_r
        coef_ref[at, wide : wide + hidden] = slope
        coef_ref[at, wide + hidden :] = keep
        gates_ref[at, :hidden] = jnp.where(alive, after, 0.0)
        return after

    lax.fori_loop(0, segments, ahead, jnp.zeros((height, hidden), F32), unroll=4)
    for came, onward in pool_onwards + high_onwards:
        came.wait_recv()
        onward.start()
        waits.append(onward.wait)
    states = dot_tn(pick, gates_ref[:, :hidden].astype(BF16)).astype(BF16)
    block = rows // groups
    for whose in range(2):
        for place in range(groups):
            at = (whose * groups + place) * block
            states_ref[whose, place] = states[at : at + block].reshape(sentences, part, hidden)
    seat = (exact(here.seq * sentences, sentences, 1), slice(None), exact(here.core * hidden, hidden, 128))
    for hop, flip, device in here.column():
        copy = remote(
            states_ref.at[(here.core + flip) % 2, here.along_place(hop)], states_out.at[seat],
            states_sems.at[0, 2 * hop + flip], states_sems.at[1, 2 * hop + flip], device,
        )
        copy.start()
        waits.append(copy.wait)
    stay = pltpu.make_async_copy(states_ref.at[here.core, here.seq], states_out.at[seat], states_sems.at[0, 0])
    stay.start()
    waits.append(stay.wait)
    for copy in cot_copies:
        copy.wait()
    cot = cot_box[...].reshape(2 * rows, hidden)
    gates_ref[:, :hidden] = dot(pick, cot) * emit_ref[:, 0:1]

    def back(index, carried):
        at = pl.ds(pl.multiple_of((segments - 1 - index) * height, height), height)
        total = carried + gates_ref[at, :hidden]
        d_r = total * coef_ref[at, :hidden]
        d_z = total * coef_ref[at, hidden : 2 * hidden]
        d_q = total * coef_ref[at, 2 * hidden : wide]
        d_n = total * coef_ref[at, wide : wide + hidden]
        kept = total * coef_ref[at, wide + hidden :]
        coef_ref[at, :hidden] = d_r
        coef_ref[at, hidden : 2 * hidden] = d_z
        coef_ref[at, 2 * hidden : wide] = d_q
        coef_ref[at, wide : wide + hidden] = d_n
        low = jnp.concatenate([d_r, d_z, d_q], axis=1).astype(BF16)
        pushed = [dot(low, hwy_slots[0, side, pl.ds(0, wide), :]) for side in range(hidden // TILE)]
        return kept + jnp.concatenate(pushed, axis=1)

    lax.fori_loop(0, segments, back, jnp.zeros((height, hidden), F32), unroll=4)
    recur = coef_ref[:, :wide].astype(BF16)
    fresh = coef_ref[:, wide : wide + hidden].astype(BF16)
    share = 2 * wide // dps
    chunk = chunk_of(share, IN_CHUNKS)
    seat = (slice(None), exact(here.core * wide, wide, 128))
    seat_t = exact(here.core * wide, wide, 16)
    given_t_ref = in_ref.at[pl.ds(0, wide), pl.ds(hidden, rows)]
    keep_t_ref = in_ref.at[pl.ds(0, wide), pl.ds(hidden + rows, rows)]
    for take, ref, ref_t in ((take_other, given_ref, given_t_ref), (take_own, keep_ref, keep_t_ref)):
        ref[:, : 2 * hidden] = dot_tn(take, recur[:, : 2 * hidden]).astype(BF16)
        ref[:, 2 * hidden :] = dot_tn(take, fresh).astype(BF16)
        for row, size, place in chunk_pieces(0, wide, share, chunk):
            ref_t[place : place + size, :] = ref[:, row : row + size].T
        if ref is given_ref:
            copies = [
                remote(ref, pair_hbm.at[seat], swap_sems.at[4], swap_sems.at[5], here.partner),
                remote(ref_t, turned_hbm.at[seat_t], swap_sems.at[6], swap_sems.at[7], here.partner),
            ]
        else:
            copies = [
                pltpu.make_async_copy(ref, pair_hbm.at[seat], load_sems.at[4]),
                pltpu.make_async_copy(ref_t, turned_hbm.at[seat_t], load_sems.at[5]),
            ]
        for copy in copies:
            copy.start()
            waits.append(copy.wait)
    prior = prior_ref[...].astype(BF16).T
    sums = jnp.sum(recur.astype(F32), axis=0, keepdims=True)
    sums_n = jnp.sum(fresh.astype(F32), axis=0, keepdims=True)
    rec_tiles = wide // TILE
    bias_ref[...] = jnp.zeros_like(bias_ref)
    for tile in range(rec_tiles):
        cols = slice(tile * TILE, (tile + 1) * TILE)
        rec_part_ref[tile * hidden : (tile + 1) * hidden, :] = dot(prior, recur[:, cols]).astype(BF16)
        if tile * TILE < 2 * hidden:
            bias_ref[tile : tile + 1, :] = sums[:, cols]
        else:
            bias_ref[tile : tile + 1, :] = sums_n[:, tile * TILE - 2 * hidden : (tile + 1) * TILE - 2 * hidden]
        bias_ref[rec_tiles + tile : rec_tiles + tile + 1, :] = sums[:, cols]
    rec_part_ref[rec_tiles * hidden :, :] = bias_ref[...].astype(BF16)
    for wait in waits:
        wait()


class Ring:
    def __init__(self, slots, sems, loads):
        self.slots, self.sems, self.loads = slots, sems, loads
        self.depth = slots.shape[0]
        self.copies = {}

    def start(self, index):
        if index < len(self.loads):
            source, place = self.loads[index]
            slot = index % self.depth
            self.copies[index] = pltpu.make_async_copy(source, place(self.slots.at[slot]), self.sems.at[slot])
            self.copies[index].start()

    def begin(self):
        for index in range(self.depth):
            self.start(index)

    def take(self, index):
        self.copies[index].wait()
        return self.slots.at[index % self.depth]

    def done(self, index):
        self.start(index + self.depth)


def tail_kernel(
    sizes, lens_ref, pair_hbm, turned_hbm, factor_hbm, slope_hbm, cross_hbm, taps_hbm, in_hbm, hwy_hbm, high_hbm, pool_hbm, rec_hbm,
    in_low, hwy_low, conv_out, rec_out, chars_box,
    weight_slots, factor_slots, slope_slots, rows_ref, full_slots,
    pair_ref, gates_own, dpre_ref, pre_t_ref, dy_ref, dconv_ref, bias_ref, chars_ref, cross_ref, taps_ref,
    in_box, hwy_box, in_got, hwy_got, in_outer, hwy_outer, in_inner, hwy_inner,
    conv_part, conv_got, conv_half, conv_box, conv_low, conv_outer, conv_inner, rec_box, rec_low, rec_outer, rec_inner,
    weight_sems, factor_sems, slope_sems, load_sems, in_spread, hwy_spread, chars_sems,
    in_sems, hwy_sems, conv_swap, conv_sems, rec_sems, conv_line, rec_line, conv_share, rec_share,
):
    sentences, span, segments, channels, embed, filters, dps, groups = sizes
    rows = sentences * segments
    tiles = channels // TILE
    wide = pair_hbm.shape[1] // 2
    here = Place(dps, groups)

    def tile_at(tile):
        return pl.ds(tile * TILE, TILE)

    weights = Ring(
        weight_slots, weight_sems,
        [(in_hbm.at[tile_at(tile)], lambda slot: slot.at[:, pl.ds(0, 2 * wide)]) for tile in range(tiles)]
        + [(hwy_hbm.at[tile_at(tile)], lambda slot: slot) for tile in range(tiles)],
    )
    factors = Ring(factor_slots, factor_sems, [(factor_hbm.at[tile], lambda slot: slot) for tile in range(tiles)])
    slopes = Ring(slope_slots, slope_sems, [(slope_hbm.at[tile], lambda slot: slot) for tile in range(tiles)])
    pair_load = pltpu.make_async_copy(pair_hbm, pair_ref, load_sems.at[0])
    pair_load.start()
    taps_load = pltpu.make_async_copy(taps_hbm, taps_ref, load_sems.at[1])
    cross_load = pltpu.make_async_copy(cross_hbm, cross_ref, load_sems.at[2])
    in_share, hwy_share = in_got.shape[0] * in_got.shape[1], hwy_got.shape[0] * hwy_got.shape[1]
    own_load = pltpu.make_async_copy(
        turned_hbm.at[exact(here.chip * 2 * in_share, 2 * in_share, 16)], gates_own, load_sems.at[4]
    )
    own_load.start()
    rows_load = pltpu.make_async_copy(high_hbm, rows_ref, load_sems.at[5])
    rows_load_2 = pltpu.make_async_copy(pool_hbm, rows_ref, load_sems.at[5])
    rows_load.start()
    weights.begin()
    factors.begin()
    greet([here.partner] + here.peers() + here.along())
    rec_load = pltpu.make_async_copy(
        rec_hbm.at[exact(here.chip * rec_low.shape[0], rec_low.shape[0], 16)], rec_low, load_sems.at[3]
    )
    rec_load.start()
    ids = row_ids(rows)
    segment, sentence = ids // sentences, ids % sentences
    length = row_lengths(own_lengths(lens_ref, here.seq * sentences, sentences), sentence)
    count = jnp.clip(length - STRIDE * segment, 0, STRIDE).astype(F32)
    scale = 1.0 / jnp.maximum(count, 1.0)
    bias_ref[...] = jnp.zeros_like(bias_ref)
    sent = []
    waits = []

    def spread(source, box, sends):
        share = box.shape[1]
        copies = []
        for hop in range(1, here.chips):
            at = exact(here.peer_chip(hop) * share, share, 16)
            copies.append(
                remote(source.at[at], box.at[hop - 1], sends.at[0, hop], sends.at[1, hop], here.peer(hop))
            )
            copies[-1].start()
        sent.extend(copies)
        return copies

    def chunk_spread(source, box, sends, share, chunk):
        lists = []
        for turn in range(share // chunk):
            lists.append([])
            for hop in range(1, here.chips):
                at = exact(here.peer_chip(hop) * 2 * share + turn * 2 * chunk, 2 * chunk, 16)
                lists[-1].append(
                    remote(
                        source.at[at], box.at[hop - 1, pl.ds(turn * 2 * chunk, 2 * chunk)],
                        sends.at[0, turn, hop], sends.at[1, turn, hop], here.peer(hop),
                    )
                )
                lists[-1][-1].start()
            sent.extend(lists[-1])
        return lists

    in_chunk, hwy_chunk = in_got.shape[1], hwy_got.shape[1]
    in_lists = chunk_spread(turned_hbm, in_box, in_spread, in_share, in_chunk)
    rec_copies = spread(rec_hbm, rec_box, rec_sems)
    pair_load.wait()

    def hwy_back(tile):
        cols = slice(tile * TILE, (tile + 1) * TILE)
        cols_2 = slice(channels + tile * TILE, channels + (tile + 1) * TILE)
        weight = weights.take(tile)
        dy = dot_nt(pair_ref[...], weight[:, : 2 * wide])
        weights.done(tile)
        factor = factors.take(tile)
        d_1 = (dy * factor[0]).astype(BF16)
        d_2 = (dy * factor[1]).astype(BF16)
        dy_ref[:, cols] = dy * factor[2]
        factors.done(tile)
        dpre_ref[:, cols] = d_1
        dpre_ref[:, cols_2] = d_2
        for at, turned in ((cols, d_1.T), (cols_2, d_2.T)):
            for row, size, place in chunk_pieces(at.start, at.stop, hwy_share, hwy_chunk):
                pre_t_ref[place : place + size, :] = turned[row - at.start : row - at.start + size]
        bias_ref[tiles + tile : tiles + tile + 1, :] = jnp.sum(d_1.astype(F32), axis=0, keepdims=True)
        bias_ref[2 * tiles + tile : 2 * tiles + tile + 1, :] = jnp.sum(d_2.astype(F32), axis=0, keepdims=True)

    hwy_lists = []

    def hwy_send():
        hwy_lists.extend(chunk_spread(pre_t_ref, hwy_box, hwy_spread, hwy_share, hwy_chunk))
        slopes.begin()
        taps_load.start()
        cross_load.start()

    def conv_back(tile):
        cols = slice(tile * TILE, (tile + 1) * TILE)
        weight = weights.take(tiles + tile)
        dy = (dy_ref[:, cols] + dot_nt(dpre_ref[...], weight[...])) * scale
        weights.done(tiles + tile)
        slope = slopes.take(tile)
        sums = jnp.zeros((1, TILE), F32)
        for place in range(STRIDE):
            alive = (segment * STRIDE + place < length).astype(F32)
            part = (dy * alive * slope[place].astype(F32)).astype(BF16)
            dconv_ref[place * rows : (place + 1) * rows, cols] = part
            sums = sums + jnp.sum(part.astype(F32), axis=0, keepdims=True)
        slopes.done(tile)
        bias_ref[tile : tile + 1, :] = sums

    spans = tile_taps(filters)
    starts = [0]
    for low, high in spans:
        starts.append(starts[-1] + (high - low) * embed)
    sums = {}
    half = conv_half.shape[0]
    conv_copy = remote(
        conv_part.at[exact((1 - here.core) * half, half, 16)], conv_got, conv_swap.at[0], conv_swap.at[1], here.partner
    )
    conv_copies = []

    def chars_part(begin_tap):
        begin = min(tile for tile, (low, high) in enumerate(spans) if low < begin_tap + 2 and high > begin_tap)
        part = dot(
            dconv_ref[:, begin * TILE :],
            taps_ref[begin * TILE :, begin_tap * embed : (begin_tap + 2) * embed],
        )
        for tap in (begin_tap, begin_tap + 1):
            for place in range(STRIDE):
                spot = place + tap - LEAD
                key = (spot // STRIDE, spot % STRIDE)
                piece = part[
                    place * rows : (place + 1) * rows, (tap - begin_tap) * embed : (tap - begin_tap + 1) * embed
                ]
                sums[key] = sums[key] + piece if key in sums else piece

    def chars_end():
        total = jnp.zeros((sentences * span, embed), F32)
        out_ids = row_ids(sentences * span)
        out_sentence, out_time = out_ids // span, out_ids % span
        for place in range(STRIDE):
            plane = jnp.zeros((rows, embed), F32)
            for hop in (-1, 0, 1):
                if (hop, place) in sums:
                    plane = plane + shift_rows(sums[hop, place], hop * sentences)
            plane = jnp.where(segment * STRIDE + place < length, plane, 0.0).astype(BF16)
            target = jnp.where(
                out_time % STRIDE == place, (out_time // STRIDE) * sentences + out_sentence, -1
            )
            total = total + dot(one_hot(sentences * span, rows, target), plane)
        for index in range(sentences):
            chars_ref[index] = total[index * span : (index + 1) * span].astype(BF16)
        chars_box[here.seq] = chars_ref[:, exact(here.seq * chars_share, chars_share, 16), :]

    chars_share = span // groups
    chars_copies = []
    for hop in range(1, groups):
        at = exact(here.along_place(hop) * chars_share, chars_share, 16)
        chars_copies.append(
            remote(
                chars_ref.at[:, at], chars_box.at[here.seq], chars_sems.at[0, hop], chars_sems.at[1, hop],
                (here.dp, here.along_place(hop)),
            )
        )
    waits.extend(copy.wait for copy in chars_copies)

    def chars_send(across):
        for hop, copy in enumerate(chars_copies):
            other = (here.along_place(hop + 1) < groups // 2) != (here.seq < groups // 2)
            pl.when(other if across else jnp.logical_not(other))(copy.start)

    def taps_part(tile):
        low, high = spans[tile]
        conv_part[starts[tile] : starts[tile + 1], :] = dot(
            cross_ref[low * embed : high * embed, :], dconv_ref[:, tile * TILE : (tile + 1) * TILE]
        ).astype(BF16)

    def taps_end():
        conv_part[starts[-1] :, :] = bias_ref[...].astype(BF16)
        conv_copy.start()
        sent.append(conv_copy)

    def conv_send():
        conv_copy.wait_recv()
        mine = conv_part[exact(here.core * half, half, 16), :]
        conv_half[...] = (mine.astype(F32) + conv_got[...].astype(F32)).astype(BF16)
        conv_copies.extend(spread(conv_half, conv_box, conv_sems))
        share = conv_low.shape[0]
        conv_low[...] = conv_half[exact(here.chip * share, share, 16), :]

    tasks = [cross_load.wait]
    tasks += [functools.partial(taps_part, tile) for tile in range(tiles)]
    tasks += [taps_end, taps_load.wait, functools.partial(chars_part, 0), conv_send]
    tasks += [functools.partial(chars_part, begin_tap) for begin_tap in range(2, NWID, 2)] + [chars_end]

    halves = []

    def multiply(box, own, own_first, lists, low, got, sems, turn):
        chunk = got.shape[1]
        index = len(halves)
        full = full_slots.at[index % full_slots.shape[0], pl.ds(0, 2 * chunk)]
        if index >= full_slots.shape[0]:
            halves[index - full_slots.shape[0]].wait_send()
        for copy in lists[turn]:
            copy.wait_recv()
        at = pl.ds(turn * 2 * chunk, 2 * chunk)
        for tile in range(tiles):
            cols = slice(tile * TILE, (tile + 1) * TILE)
            total = dot(own[exact(own_first + turn * 2 * chunk, 2 * chunk, 16), :], rows_ref[here.chip, :, cols])
            for hop in range(1, here.chips):
                chip = (here.chip + here.chips - hop) % here.chips
                total = total + dot(box[hop - 1, at, :], rows_ref[chip, :, cols])
            full[:, cols] = total.astype(BF16)
        low[turn] = full[exact(here.core * chunk, chunk, 16), :]
        copy = remote(
            full.at[exact((1 - here.core) * chunk, chunk, 16)], got.at[turn],
            sems.at[turn, 0, 0], sems.at[turn, 0, 1], here.partner,
        )
        copy.start()
        halves.append(copy)

    def line_item(found, low, from_outer, from_inner, sem, keep=None):
        out_to_in = remote(low, from_outer, sem(2), sem(3), here.inner)
        across = remote(low, from_inner, sem(2), sem(4), here.inner)
        in_to_out = remote(low, from_inner, sem(5), sem(4), here.outer)

        def inward():
            @pl.when(here.has_outer)
            def _():
                out_to_in.wait_recv()
                low[...] = (found() + from_outer[...].astype(F32)).astype(BF16)

            @pl.when(jnp.logical_not(here.has_outer))
            def _():
                low[...] = found().astype(BF16)

            @pl.when(here.middle)
            def _():
                across.start()

            @pl.when(jnp.logical_not(here.middle))
            def _():
                out_to_in.start()

        def outward():
            across.wait()

            @pl.when(here.middle)
            def _():
                low[...] = (low[...].astype(F32) + from_inner[...].astype(F32)).astype(BF16)

            @pl.when(jnp.logical_not(here.middle))
            def _():
                low[...] = from_inner[...]

            @pl.when(here.has_outer)
            def _():
                in_to_out.start()

            if keep is not None:
                keep()

        def finish():
            @pl.when(here.has_outer)
            def _():
                in_to_out.wait_send()

        return inward, outward, finish

    onward = []

    def share_out(out, low, begin, size, sems):
        base = here.core * (out.shape[0] // 2) + begin
        share = low.shape[0]
        piece = low.at[pl.ds(begin, size)]
        at = exact(base + here.chip * share, size, 16)
        stay = pltpu.make_async_copy(piece, out.at[at], sems.at[2, 0])
        copies = [remote(piece, out.at[at], sems.at[0, 0], sems.at[1, 0], here.partner)]
        for hop in range(1, here.chips):
            copies.append(remote(piece, out.at[at], sems.at[0, hop], sems.at[1, hop], here.peer(hop)))
            source = (here.chip + here.chips - hop) % here.chips
            place = exact(base + source * share, size, 16)
            send_on = remote(out.at[place], out.at[place], sems.at[2, hop], sems.at[3, hop], here.partner)
            onward.append((copies[hop], send_on))
            waits.append(send_on.wait)
        waits.extend(copy.wait_send for copy in copies)
        waits.append(copies[0].wait_recv)
        waits.append(stay.wait)

        def keep():
            stay.start()
            for copy in copies:
                copy.start()

        return keep

    def chunk_items(low, got, first, outer, inner, sems, finer):
        found_lists = []

        def found(turn, part, at):
            if part == 0:
                halves[first + turn].wait_recv()
            return low[turn, :, at].astype(F32) + got[turn, :, at].astype(F32)

        for turn in range(low.shape[0]):
            count = ENDING if turn == finer else HALVES
            cuts = [-(-tiles * part // count) * TILE if count > 2 else part * channels // count for part in range(count + 1)]
            found_lists.append([])
            for part, (begin, end) in enumerate(zip(cuts, cuts[1:])):
                at = (turn, slice(None), pl.ds(begin, end - begin))
                found_lists[-1].append(
                    line_item(
                        functools.partial(found, turn, part, slice(begin, end)), low.at[at], outer.at[at], inner.at[at],
                        lambda index, turn=turn, part=part: sems.at[turn, 1 + part, index],
                    )
                )
        return found_lists

    def small_items(low, box, copies, outer, inner, line_sems, share_sems, out, ready):
        found_items = []
        size = low.shape[0] // 16
        cuts = [size * part // SMALL_PARTS * 16 for part in range(SMALL_PARTS + 1)]

        def found(part):
            if part == 0:
                ready()
                for copy in copies:
                    copy.wait_recv()
            at = slice(cuts[part], cuts[part + 1])
            total = low[at, :].astype(F32)
            for hop in range(here.chips - 1):
                total = total + box[hop, at, :].astype(F32)
            return total

        for part in range(SMALL_PARTS):
            at = pl.ds(cuts[part], cuts[part + 1] - cuts[part])
            found_items.append(
                line_item(
                    functools.partial(found, part), low.at[at], outer.at[at], inner.at[at],
                    lambda index, part=part: line_sems.at[part, index],
                    share_out(out, low, cuts[part], cuts[part + 1] - cuts[part], share_sems.at[part]),
                )
            )
        return found_items

    in_items = chunk_items(in_low, in_got, 0, in_outer, in_inner, in_sems, 0)
    hwy_items = chunk_items(hwy_low, hwy_got, in_low.shape[0], hwy_outer, hwy_inner, hwy_sems, hwy_low.shape[0] - 1)
    rec_items = small_items(
        rec_low, rec_box, rec_copies, rec_outer, rec_inner, rec_line, rec_share, rec_out, rec_load.wait
    )
    conv_items = small_items(
        conv_low, conv_box, conv_copies, conv_outer, conv_inner, conv_line, conv_share, conv_out, lambda: None
    )

    def in_multiply(turn):
        if turn == 0:
            own_load.wait()
            rows_load.wait()
        multiply(in_box, gates_own, 0, in_lists, in_low, in_got, in_sems, turn)
        if turn + 1 == in_low.shape[0]:
            rows_load_2.start()

    def hwy_multiply(turn):
        if turn == 0:
            rows_load_2.wait()
        multiply(hwy_box, pre_t_ref, here.chip * 2 * hwy_share, hwy_lists, hwy_low, hwy_got, hwy_sems, turn)

    tasks = [hwy_send] + [functools.partial(conv_back, tile) for tile in range(tiles)] + tasks
    tasks = [functools.partial(hwy_back, tile) for tile in range(tiles)] + tasks
    items = []
    plan = []

    def add(new):
        plan.extend(new)

    add([tiles + 1])
    for turn in range(in_low.shape[0]):
        add([functools.partial(in_multiply, turn), 1])
        for item in in_items[turn]:
            add([item, 1 if turn == 0 else 2])
    for item in rec_items:
        add([2, item])
    last = hwy_low.shape[0] - 1
    for turn in range(last):
        if turn == (last + 1) // 2:
            add(conv_items)
        add([functools.partial(hwy_multiply, turn), 1])
        for item in hwy_items[turn]:
            add([2, item])
    if last < 1:
        add([len(tasks)] + conv_items)
    add([functools.partial(hwy_multiply, last), len(tasks)])
    for item in hwy_items[last]:
        add([item])
    depths = groups // 2

    def outwards(index):
        for depth in range(depths):
            ready = index - 2 - LAG * depth
            if 0 <= ready < len(items):
                pl.when(here.depth == depth)(items[ready][1])

    for step in plan:
        if isinstance(step, int):
            for task in tasks[:step]:
                task()
            del tasks[:step]
        elif isinstance(step, tuple):
            items.append(step)
            step[0]()
            outwards(len(items) - 1)
        else:
            step()
    chars_send(True)
    for extra in range(2 + LAG * (depths - 1)):
        outwards(len(items) + extra)
        if extra == 1:
            chars_send(False)
    for copy, send_on in onward:
        copy.wait_recv()
        send_on.start()
    for item in items:
        item[2]()
    for copy in sent:
        copy.wait_send()
    for copy in halves[-full_slots.shape[0] :]:
        copy.wait_send()
    for wait in waits:
        wait()


def finish_kernel(
    sizes, in_hbm, hwy_hbm, conv_hbm, rec_hbm, chars_hbm,
    in_out, hwy_out, conv_out, rec_out, chars_out, conv_bias_out, hwy_bias_out, in_bias_out, rec_bias_out,
    in_ref, hwy_ref, conv_ref, rec_ref, chars_ref, in_full, hwy_full, conv_full, rec_full, chars_full,
    load_sems, store_sems,
):
    embed, filters, hidden = sizes
    tiles = in_ref.shape[2] // TILE
    half = rec_ref.shape[0] // 2
    loads = [
        pltpu.make_async_copy(rec_hbm.at[pl.ds(side * half, half)], rec_ref.at[pl.ds(side * half, half)], load_sems.at[side])
        for side in range(2)
    ]
    for place, (source, ref) in enumerate(((hwy_hbm, hwy_ref), (conv_hbm, conv_ref), (in_hbm, in_ref), (chars_hbm, chars_ref))):
        loads.append(pltpu.make_async_copy(source, ref, load_sems.at[2 + place]))
    for load in loads:
        load.start()
    stores = []

    def store(source, out):
        stores.append(pltpu.make_async_copy(source, out, store_sems.at[len(stores)]))
        stores[-1].start()

    rec_tiles = 3 * hidden // TILE
    for side in range(2):
        loads[side].wait()
        for tile in range(rec_tiles):
            row = side * half + tile * hidden
            at = slice(tile * TILE, (tile + 1) * TILE)
            rec_full[side, :, at] = rec_ref[row : row + hidden, :].astype(F32)
        store(rec_full.at[side], rec_out.at[side])
        row = side * half + rec_tiles * hidden
        rest = rec_ref[row : row + 16, :].astype(F32)
        for tile in range(rec_tiles):
            at = slice(tile * TILE, (tile + 1) * TILE)
            in_bias_out[pl.ds((side * rec_tiles + tile) * TILE, TILE)] = rest[tile]
            rec_bias_out[side : side + 1, at] = rest[rec_tiles + tile : rec_tiles + tile + 1]
    loads[2].wait()
    hwy_full[...] = hwy_ref[...].astype(F32).reshape(hwy_full.shape)
    store(hwy_full, hwy_out)
    loads[3].wait()
    spans = tile_taps(filters)
    starts = [0]
    for low, high in spans:
        starts.append(starts[-1] + (high - low) * embed)
    for width in range(1, NWID + 1):
        lead, first = (width - 1) // 2, width * (width - 1) // 2
        for tap in range(width):
            spot = LEAD - lead + tap
            begin, end = (width - 1) * filters, width * filters
            while begin < end:
                tile = begin // TILE
                stop = min(end, (tile + 1) * TILE)
                row = starts[tile] + (spot - spans[tile][0]) * embed
                piece = conv_ref[row : row + embed, :].astype(F32).T
                at = slice(begin - (width - 1) * filters, stop - (width - 1) * filters)
                conv_full[first + tap, at, :] = piece[begin - tile * TILE : stop - tile * TILE]
                begin = stop
    store(conv_full, conv_out)
    rest = conv_ref[starts[-1] :, :].astype(F32)
    for tile in range(tiles):
        at = slice(tile * TILE, (tile + 1) * TILE)
        conv_bias_out[pl.ds(tile * TILE, TILE)] = rest[tile]
    for tile in range(2 * tiles):
        hwy_bias_out[:, tile * TILE : (tile + 1) * TILE] = rest[tiles + tile : tiles + tile + 1]
    loads[4].wait()
    for turn in range(in_ref.shape[0]):
        at = slice(turn * in_ref.shape[1], (turn + 1) * in_ref.shape[1])
        in_full[:, at] = in_ref[turn].astype(F32).T
    store(in_full, in_out)
    loads[5].wait()
    chars_full[...] = chars_ref[...].astype(F32).reshape(chars_full.shape)
    store(chars_full, chars_out)
    for copy in stores:
        copy.wait()


VMEM = pl.BlockSpec(memory_space=pltpu.VMEM)
SMEM = pl.BlockSpec(memory_space=pltpu.SMEM)
ANY = pl.BlockSpec(memory_space=pl.ANY)


def params(**more):
    return pltpu.CompilerParams(vmem_limit_bytes=VMEM_LIMIT, **more)


def shape(*dims, dtype=F32):
    return jax.ShapeDtypeStruct(dims, dtype)


def block(*dims, dtype=BF16):
    return pltpu.VMEM(dims, dtype)


def flags(*dims):
    return pltpu.SemaphoreType.DMA(dims)


def head_call(sizes, hidden, dps, groups, given):
    sentences, span, segments, channels, embed, filters = sizes
    wide, rows, chips, tiles = 3 * hidden, sentences * segments, dps // 2, channels // TILE
    height = max(8, 2 * sentences)
    steps, part = segments * height, segments // groups
    rec_rows = wide // TILE * hidden + 16 * chips
    side = math.isqrt(chips)
    copies = 1 + 2 * (side - 1) * (side + 1)
    return pl.pallas_call(
        functools.partial(head_kernel, sizes + (hidden, height, dps, groups)),
        name="head",
        out_shape=[
            shape(groups * sentences, part, 2 * hidden, dtype=BF16),
            shape(chips, rows, channels, dtype=BF16),
            shape(chips, rows, channels, dtype=BF16),
            shape(tiles, STRIDE, rows, TILE, dtype=BF16),
            shape(tiles, 3, rows, TILE),
            shape(NWID * embed, STRIDE * rows, dtype=BF16),
            shape(channels, NWID * embed, dtype=BF16),
            shape(rows, 2 * wide, dtype=BF16),
            shape(2 * wide, rows, dtype=BF16),
            shape(rec_rows, TILE, dtype=BF16),
        ],
        in_specs=[SMEM] + [VMEM] * 4 + [ANY] * 6,
        out_specs=[VMEM] + [ANY] * 8 + [VMEM],
        scratch_shapes=[
            block(NWID * (NWID + 1) // 2, filters, embed),
            block(NWID * embed, STRIDE * rows),
            block(channels, NWID * embed),
            block(rows, wide),
            block(1, LENS, dtype=F32),
            block(1, LENS, dtype=F32),
            block(groups, sentences, span // groups, embed),
            block(4 if chips <= 8 else 2, 2, channels, TILE),
            block(STRIDE, rows, NWID * embed),
            block(tiles if chips <= 8 else 2, STRIDE, rows, TILE),
            block(tiles if chips <= 8 else 2, 3, rows, TILE, dtype=F32),
            block(rows, channels),
            block(rows, channels),
            block(rows, channels),
            block(channels, wide),
            block(hidden, wide),
            block(steps, wide, dtype=F32),
            block(steps, 5 * hidden, dtype=F32),
            block(steps, hidden, dtype=F32),
            block(steps, 128, dtype=F32),
            block(2, groups, sentences, part, hidden),
            block(2, groups, sentences, part, hidden),
            block(rows, wide),
            block(16 * chips, TILE, dtype=F32),
            flags(4, 2), flags(tiles), flags(tiles), flags(7), flags(8), flags(2, groups), flags(2, 2 * groups),
            flags(2, 2 * groups), flags(2, copies), flags(2, copies),
        ],
        compiler_params=params(collective_id=2, has_side_effects=True),
    )(*given)


def tail_call(sizes, hidden, dps, groups, given):
    sentences, span, segments, channels, embed, filters = sizes
    wide, rows, chips = 3 * hidden, sentences * segments, dps // 2
    rec_rows = wide // TILE * hidden + 16 * chips
    tiles = channels // TILE
    in_share, hwy_share = 2 * wide // dps, 2 * channels // dps
    spans = tile_taps(filters)
    conv_rows = (sum(high - low for low, high in spans) + 1) * embed

    def slots(lead, share):
        return pltpu.VMEM((lead, share, TILE), BF16)

    in_chunk, hwy_chunk = chunk_of(in_share, IN_CHUNKS), chunk_of(hwy_share, HWY_CHUNKS)
    in_turns, hwy_turns = in_share // in_chunk, hwy_share // hwy_chunk
    conv_share, rec_share = conv_rows // dps, rec_rows // chips
    return pl.pallas_call(
        functools.partial(tail_kernel, sizes + (dps, groups)),
        name="tail",
        out_shape=[
            shape(in_turns, in_chunk, channels, dtype=BF16),
            shape(hwy_turns, hwy_chunk, channels, dtype=BF16),
            shape(conv_rows, TILE, dtype=BF16),
            shape(2 * rec_rows, TILE, dtype=BF16),
            shape(groups, sentences, span // groups, embed, dtype=BF16),
        ],
        in_specs=[SMEM] + [ANY] * 11,
        out_specs=[VMEM, VMEM, ANY, ANY, VMEM],
        scratch_shapes=[
            block(3 if chips <= 8 else 2, TILE, 2 * channels),
            block(2, 3, rows, TILE, dtype=F32),
            block(2, STRIDE, rows, TILE),
            block(chips, rows, channels),
            block(2, 2 * max(in_chunk, hwy_chunk), channels),
            block(rows, 2 * wide),
            block(2 * in_share, rows),
            block(rows, 2 * channels),
            block(2 * channels, rows),
            block(rows, channels, dtype=F32),
            block(STRIDE * rows, channels),
            block(embed, TILE, dtype=F32),
            block(sentences, span, embed),
            block(NWID * embed, STRIDE * rows),
            block(channels, NWID * embed),
            block(chips - 1, 2 * in_share, rows),
            block(chips - 1, 2 * hwy_share, rows),
            block(in_turns, in_chunk, channels), block(hwy_turns, hwy_chunk, channels),
            block(in_turns, in_chunk, channels), block(hwy_turns, hwy_chunk, channels),
            block(in_turns, in_chunk, channels), block(hwy_turns, hwy_chunk, channels),
            block(conv_rows, TILE),
            block(conv_rows // 2, TILE),
            block(conv_rows // 2, TILE),
            slots(chips - 1, conv_share),
            block(conv_share, TILE),
            block(conv_share, TILE),
            block(conv_share, TILE),
            slots(chips - 1, rec_share),
            block(rec_share, TILE),
            block(rec_share, TILE),
            block(rec_share, TILE),
            flags(3), flags(2), flags(2), flags(6),
            flags(2, in_turns, chips), flags(2, hwy_turns, chips), flags(2, groups),
            flags(in_turns, 1 + ENDING, 6), flags(hwy_turns, 1 + ENDING, 6), flags(2), flags(2, chips), flags(2, chips),
            flags(SMALL_PARTS, 6), flags(SMALL_PARTS, 6), flags(SMALL_PARTS, 4, chips), flags(SMALL_PARTS, 4, chips),
        ],
        compiler_params=params(collective_id=1, has_side_effects=True),
    )(
        *given
    )


def local(
    char_embeds, lengths, conv_weight, conv_bias, hwy_weight, hwy_bias, gru_in_weight, gru_in_bias,
    gru_rec_weight, gru_rec_bias, out_grad,
):
    groups = lax.axis_size("seq")
    dps = lax.axis_size("dp")
    sentences = char_embeds.shape[0] // groups
    span = char_embeds.shape[1] * groups
    segments = span // STRIDE
    embed, filters = conv_weight.shape[1:]
    channels = NWID * filters
    hidden = gru_rec_weight.shape[1]
    wide = 3 * hidden
    sizes = (sentences, span, segments, channels, embed, filters)
    encoded, pool_all, high_all, slope, factor, cross, taps, pair, turned, rec_part = head_call(
        sizes, hidden, dps, groups,
        (
            lengths, conv_bias, hwy_bias, gru_in_bias, gru_rec_bias, char_embeds, conv_weight.transpose(0, 2, 1), hwy_weight[0], out_grad, gru_in_weight, gru_rec_weight,
        ),
    )
    in_sum, hwy_sum, conv_sum, rec_sum, chars_box = tail_call(
        sizes, hidden, dps, groups,
        (
            lengths, pair, turned, factor, slope, cross, taps, gru_in_weight, hwy_weight[0], high_all, pool_all, rec_part,
        ),
    )
    in_share, hwy_share = 2 * wide // dps, 2 * channels // dps
    whole = [
        (channels, in_share),
        (hwy_share, channels),
        (NWID * (NWID + 1) // 2, filters, embed),
        (2, hidden, wide),
        (groups * sentences, span // groups, embed),
    ]
    in_grad, hwy_grad, conv_grad, rec_grad, dchars, conv_bias_grad, hwy_bias_grad, in_bias_grad, rec_bias_grad = pl.pallas_call(
        functools.partial(finish_kernel, (embed, filters, hidden)),
        name="finish",
        out_shape=[shape(*dims) for dims in whole]
        + [shape(channels), shape(1, 2 * channels), shape(2 * wide), shape(2, wide)],
        in_specs=[ANY] * 5,
        out_specs=[ANY] * 5 + [VMEM] * 4,
        scratch_shapes=[
            block(*part.shape) for part in (in_sum, hwy_sum, conv_sum, rec_sum, chars_box)
        ]
        + [block(*dims, dtype=F32) for dims in whole]
        + [flags(6), flags(6)],
        compiler_params=params(),
    )(in_sum, hwy_sum, conv_sum, rec_sum, chars_box)
    return (
        encoded, dchars, conv_grad.transpose(0, 2, 1), conv_bias_grad, hwy_grad.T[None], hwy_bias_grad, in_grad,
        in_bias_grad, rec_grad, rec_bias_grad,
    )


def solution(mesh):
    whole = P()
    split = P("dp", "seq", None)
    return jax.shard_map(
        local,
        mesh=mesh,
        in_specs=(split, P("dp")) + (whole,) * 8 + (split,),
        out_specs=(split, split, whole, whole, P(None, None, "dp"), whole, P(None, "dp"), whole, whole, whole),
        check_vma=False,
    )
```

```python
import functools
import math

import jax
import jax.numpy as jnp
from jax import lax
from jax.experimental import pallas as pl
from jax.experimental.pallas import tpu as pltpu
from jax.sharding import PartitionSpec as P

MESH = pl.DeviceIdType.MESH
NWID = 8
STRIDE = 5
LEAD = (NWID - 1) // 2
TILE = 256
LENS = 128
SMALL_PARTS = 2
IN_CHUNKS = 4
HWY_CHUNKS = 4
HALVES = 2
ENDING = 4
LAG = 6
F32 = jnp.float32
BF16 = jnp.bfloat16
VMEM_LIMIT = 61 * 2**20


def tile_taps(filters):
    found = []
    for tile in range(NWID * filters // TILE):
        first_width = tile * TILE // filters + 1
        last_width = (tile * TILE + TILE - 1) // filters + 1
        low, high = NWID, 0
        for width in range(first_width, last_width + 1):
            lead = (width - 1) // 2
            low, high = min(low, LEAD - lead), max(high, LEAD - lead + width)
        found.append((low, high))
    return found


def chunk_of(share, most):
    units = share // 16
    return share // max(count for count in range(1, most + 1) if units % count == 0)


def chunk_pieces(first, last, share, chunk):
    pieces = []
    while first < last:
        chip, rest = divmod(first, 2 * share)
        core, rest = divmod(rest, share)
        turn, rest = divmod(rest, chunk)
        size = min(last - first, chunk - rest)
        pieces.append((first, size, chip * 2 * share + turn * 2 * chunk + core * chunk + rest))
        first += size
    return pieces


def lay_taps(weight_ref, taps_ref):
    _, filters, embed = weight_ref.shape
    taps_ref[...] = jnp.zeros_like(taps_ref)
    for width in range(1, NWID + 1):
        for tap in range(width):
            spot = LEAD - (width - 1) // 2 + tap
            taps_ref[(width - 1) * filters : width * filters, spot * embed : (spot + 1) * embed] = weight_ref[
                width * (width - 1) // 2 + tap
            ]


def sigmoid(value):
    return 0.5 * jnp.tanh(0.5 * value) + 0.5


def dot(left, right):
    return jnp.dot(left, right, preferred_element_type=F32)


def dot_nt(left, right):
    return lax.dot_general(left, right, (((1,), (1,)), ((), ())), preferred_element_type=F32)


def dot_tn(left, right):
    return lax.dot_general(left, right, (((0,), (0,)), ((), ())), preferred_element_type=F32)


def one_hot(rows, columns, target):
    places = lax.broadcasted_iota(jnp.int32, (rows, columns), 1)
    return jnp.where(places == target, 1.0, 0.0).astype(BF16)


def row_ids(rows):
    return lax.broadcasted_iota(jnp.int32, (rows, 1), 0)


def shift_rows(value, count):
    if count == 0:
        return value
    rows = value.shape[0]
    ids = row_ids(rows)
    moved = pltpu.roll(value, count % rows, axis=0)
    keep = ids >= count if count > 0 else ids < rows + count
    return jnp.where(keep, moved, 0.0)


class Place:
    def __init__(self, dps, groups):
        self.chips, self.groups = dps // 2, groups
        self.dp, self.seq = lax.axis_index("dp"), lax.axis_index("seq")
        self.chip, self.core = self.dp // 2, self.dp % 2
        self.partner = (self.chip * 2 + 1 - self.core, self.seq)
        half = groups // 2
        low = self.seq < half
        self.inner = (self.dp, jnp.where(low, self.seq + 1, self.seq - 1))
        self.outer = (self.dp, jnp.clip(jnp.where(low, self.seq - 1, self.seq + 1), 0, groups - 1))
        self.has_outer = (self.seq > 0) & (self.seq < groups - 1)
        self.depth = jnp.where(low, half - 1 - self.seq, self.seq - half)
        self.middle = self.depth == 0

    def peer_chip(self, hop):
        return (self.chip + hop) % self.chips

    def peer(self, hop):
        return (self.peer_chip(hop) * 2 + self.core, self.seq)

    def peers(self):
        return [self.peer(hop) for hop in range(1, self.chips)]

    def column(self):
        found = []
        for hop in range(self.groups):
            for flip in range(2):
                if hop or flip:
                    found.append((hop, flip, (self.chip * 2 + (self.core + flip) % 2, self.along_place(hop))))
        return found

    def grid(self, axis, hop):
        side = math.isqrt(self.chips)
        high, low = self.chip // side, self.chip % side
        if axis == 0:
            return (high + hop) % side * side + low
        return high * side + (low + hop) % side

    def along_place(self, hop):
        return (self.seq + hop) % self.groups

    def along(self):
        return [(self.dp, self.along_place(hop)) for hop in range(1, self.groups)]


def greet(devices):
    barrier = pltpu.get_barrier_semaphore()
    for device in devices:
        pl.semaphore_signal(barrier, inc=1, device_id=device, device_id_type=MESH)
    pl.semaphore_wait(barrier, len(devices))


def remote(src, dst, send, recv, device):
    return pltpu.make_async_remote_copy(
        src_ref=src, dst_ref=dst, send_sem=send, recv_sem=recv, device_id=device, device_id_type=MESH
    )


def exact(start, size, unit):
    return pl.ds(pl.multiple_of(start, unit), size)


def row_lengths(lens, which):
    found = jnp.zeros(which.shape, F32)
    for place, value in enumerate(lens):
        found = jnp.where(which == place, value, found)
    return found.astype(jnp.int32)


def own_lengths(lens_ref, first, count):
    return [jnp.full((1, 1), lens_ref[first + place].astype(F32)) for place in range(count)]


def row_values(row_ref, count):
    return [row_ref[:, place : place + 1] for place in range(count)]


def head_kernel(
    sizes, lens_ref, conv_bias_ref, hwy_bias_ref, in_bias_ref, rec_bias_ref, chars_hbm, weight_hbm, hwy_hbm, cot_hbm, in_hbm, rec_hbm,
    states_out, pool_all, high_all, slope_hbm, factor_hbm, cross_hbm, taps_hbm, pair_hbm, turned_hbm, rec_part_ref,
    weight_ref, cross_ref, taps_ref, keep_ref,
    lens_row, lens_other, chars_box, hwy_slots, stack_ref, slope_slots, factor_slots, pooled_ref, high_ref, other_ref,
    in_ref, rec_ref, gates_ref, coef_ref, prior_ref, emit_ref, cot_box, states_ref, given_ref, bias_ref,
    hwy_sems, slope_sems, factor_sems, load_sems, swap_sems, chars_sems, cot_sems, states_sems, pool_sems, high_sems,
):
    sentences, span, segments, channels, embed, filters, hidden, height, dps, groups = sizes
    rows = sentences * segments
    tiles = channels // TILE
    wide = 3 * hidden
    here = Place(dps, groups)
    waits = []
    in_bias = in_bias_ref[exact(here.core * wide, wide, 128)].astype(F32).reshape(1, wide)
    rec_bias = rec_bias_ref[...].astype(F32)
    rec_bias = jnp.where(here.core == 0, rec_bias[0:1], rec_bias[1:2])
    lens = own_lengths(lens_ref, here.seq * sentences, sentences)
    spots = lax.broadcasted_iota(jnp.int32, (1, LENS), 1)
    line = jnp.zeros((1, LENS), F32)
    for place, value in enumerate(lens):
        line = jnp.where(spots == place, value, line)
    lens_row[...] = line

    def columns(tile):
        return [(hwy_hbm.at[:, pl.ds(side * channels + tile * TILE, TILE)], side) for side in range(2)]

    hwy_loads = {}

    def hwy_start(tile):
        if tile < tiles:
            slot = tile % hwy_slots.shape[0]
            hwy_loads[tile] = [
                pltpu.make_async_copy(source, hwy_slots.at[slot, side], hwy_sems.at[slot, side])
                for source, side in columns(tile)
            ]
            for load in hwy_loads[tile]:
                load.start()

    loads = [
        pltpu.make_async_copy(in_hbm.at[:, exact(here.core * wide, wide, 128)], in_ref, load_sems.at[0]),
        pltpu.make_async_copy(rec_hbm.at[here.core], rec_ref, load_sems.at[1]),
    ]
    weight_load = pltpu.make_async_copy(weight_hbm, weight_ref, load_sems.at[6])
    weight_load.start()
    greet([device for _, _, device in here.column()] + here.peers())
    swap_lens = remote(lens_row, lens_other, swap_sems.at[0], swap_sems.at[1], here.partner)
    swap_lens.start()
    share = span // groups
    chars_copies = []
    for hop in range(1, groups):
        chars_copies.append(
            remote(
                chars_hbm.at[exact(here.along_place(hop) * sentences, sentences, 1)], chars_box.at[here.seq],
                chars_sems.at[0, hop], chars_sems.at[1, hop], (here.dp, here.along_place(hop)),
            )
        )
    chars_copies.append(
        pltpu.make_async_copy(
            chars_hbm.at[exact(here.seq * sentences, sentences, 1)], chars_box.at[here.seq], chars_sems.at[0, 0]
        )
    )
    for copy in chars_copies:
        copy.start()
    cot_copies = []
    for hop, flip, device in here.column():
        side = (here.core + flip) % 2
        cot_copies.append(
            remote(
                cot_hbm.at[
                    exact(here.along_place(hop) * sentences, sentences, 1), :, exact(side * hidden, hidden, 128)
                ],
                cot_box.at[here.core, here.seq], cot_sems.at[0, 2 * hop + flip], cot_sems.at[1, 2 * hop + flip], device,
            )
        )
    cot_copies.append(
        pltpu.make_async_copy(
            cot_hbm.at[exact(here.seq * sentences, sentences, 1), :, exact(here.core * hidden, hidden, 128)],
            cot_box.at[here.core, here.seq], cot_sems.at[0, 0],
        )
    )
    for tile in range(hwy_slots.shape[0]):
        hwy_start(tile)
    for load in loads:
        load.start()
    weight_load.wait()
    lay_taps(weight_ref, taps_ref)
    ids = row_ids(rows)
    segment, sentence = ids // sentences, ids % sentences
    length = row_lengths(lens, sentence)
    steps = segments * height
    step_ids = row_ids(steps)
    step, lane = step_ids // height, step_ids % height
    step_segment = jnp.where(here.core == 0, step, segments - 1 - step)
    whose, step_sentence = lane // sentences, lane % sentences
    real = lane < 2 * sentences
    order = step_segment * sentences + step_sentence
    mine = real & (whose == here.core)
    theirs = real & (whose != here.core)
    take_own = one_hot(steps, rows, jnp.where(mine, order, -1))
    take_other = one_hot(steps, rows, jnp.where(theirs, order, -1))
    part = segments // groups
    order_2 = ((whose * groups + step_segment // part) * sentences + step_sentence) * part + step_segment % part
    pick = one_hot(steps, 2 * rows, jnp.where(real, order_2, -1))
    live = []
    planes = {}
    for copy in chars_copies:
        copy.wait()
    for copy in cot_copies:
        copy.start()
    chars = chars_box[...].reshape(sentences * span, embed)
    for place in range(STRIDE):
        time = segment * STRIDE + place
        alive = time < length
        live.append(alive.astype(F32))
        target = jnp.where(alive, (time // share * sentences + sentence) * share + time % share, -1)
        plane = dot(one_hot(rows, sentences * span, target), chars)
        for hop in (-1, 0, 1):
            planes[hop, place] = shift_rows(plane, -hop * sentences).astype(BF16)
    turned = {key: plane.T for key, plane in planes.items()}
    for place in range(STRIDE):
        for tap in range(NWID):
            spot = place + tap - LEAD
            key = (spot // STRIDE, spot % STRIDE)
            stack_ref[place, :, tap * embed : (tap + 1) * embed] = planes[key]
            cross_ref[tap * embed : (tap + 1) * embed, place * rows : (place + 1) * rows] = turned[key]
    count = jnp.clip(length - STRIDE * segment, 0, STRIDE).astype(F32)
    scale = 1.0 / jnp.maximum(count, 1.0)

    for source, out, flag in ((cross_ref, cross_hbm, 2), (taps_ref, taps_hbm, 3)):
        copy = pltpu.make_async_copy(source, out, load_sems.at[flag])
        copy.start()
        waits.append(copy.wait)

    def stored(slots, out, sems, tile, copies):
        slot = tile % slots.shape[0]
        if tile >= slots.shape[0]:
            copies[tile - slots.shape[0]].wait()
        copies.append(pltpu.make_async_copy(slots.at[slot], out.at[tile], sems.at[slot]))
        return slots.at[slot]

    slope_copies, factor_copies = [], []
    for tile, (low, high) in enumerate(tile_taps(filters)):
        cols = slice(tile * TILE, (tile + 1) * TILE)
        total = jnp.zeros((rows, TILE), F32)
        conv_bias = conv_bias_ref[pl.ds(tile * TILE, TILE)].astype(F32).reshape(1, TILE)
        slot = stored(slope_slots, slope_hbm, slope_sems, tile, slope_copies)
        for place in range(STRIDE):
            pre = dot_nt(
                stack_ref[place, :, low * embed : high * embed],
                taps_ref[cols, low * embed : high * embed],
            ) + conv_bias
            gate = sigmoid(pre)
            act = pre * gate
            total = total + act * live[place]
            slot[place] = (gate + act * (1.0 - gate)).astype(BF16)
        slope_copies[tile].start()
        pooled_ref[:, cols] = (total * scale).astype(BF16)

    def gather(source, out, sems):
        side = math.isqrt(here.chips)
        half = rows // 2
        stay = pltpu.make_async_copy(source, out.at[here.chip], sems.at[0, 0])
        firsts, seconds, onwards = [], [], []
        flag = 1
        for axis in range(2):
            at = pl.ds(axis * half, half)
            for hop in range(1, side):
                chip = here.grid(axis, hop)
                firsts.append(
                    remote(
                        source.at[at], out.at[here.chip, at], sems.at[0, flag], sems.at[1, flag],
                        (chip * 2 + here.core, here.seq),
                    )
                )
                came = here.grid(axis, side - hop)
                flag += 1
                for hop_2 in range(1, side):
                    chip = here.grid(1 - axis, hop_2)
                    onwards.append(
                        (
                            firsts[-1],
                            remote(
                                out.at[came, at], out.at[came, at], sems.at[0, flag], sems.at[1, flag],
                                (chip * 2 + here.core, here.seq),
                            ),
                        )
                    )
                    flag += 1
            for hop in range(1, side):
                chip = here.grid(1 - axis, hop)
                seconds.append(
                    remote(
                        source.at[at], out.at[here.chip, at], sems.at[0, flag], sems.at[1, flag],
                        (chip * 2 + here.core, here.seq),
                    )
                )
                flag += 1
        for copy in [stay] + firsts + seconds:
            copy.start()
        waits.extend([stay.wait] + [copy.wait_send for copy in firsts] + [copy.wait for copy in seconds])
        return onwards

    pool_onwards = gather(pooled_ref, pool_all, pool_sems)
    for tile in range(tiles):
        cols = slice(tile * TILE, (tile + 1) * TILE)
        cols_2 = slice(channels + tile * TILE, channels + (tile + 1) * TILE)
        for load in hwy_loads[tile]:
            load.wait()
        slot = tile % hwy_slots.shape[0]
        pre_1 = dot(pooled_ref[...], hwy_slots[slot, 0]) + hwy_bias_ref[:, cols].astype(F32)
        pre_2 = dot(pooled_ref[...], hwy_slots[slot, 1]) + hwy_bias_ref[:, cols_2].astype(F32)
        hwy_start(tile + hwy_slots.shape[0])
        layer_in = pooled_ref[:, cols].astype(F32)
        gate, inner = sigmoid(pre_2), sigmoid(pre_1)
        act = pre_1 * inner
        off = 1.0 - gate
        high_ref[:, cols] = (gate * act + off * layer_in).astype(BF16)
        factor = stored(factor_slots, factor_hbm, factor_sems, tile, factor_copies)
        factor[0] = gate * (inner + act * (1.0 - inner))
        factor[1] = (act - layer_in) * gate * off
        factor[2] = off
        factor_copies[tile].start()
    swap = remote(high_ref, other_ref, swap_sems.at[2], swap_sems.at[3], here.partner)
    swap.start()
    high_onwards = gather(high_ref, high_all, high_sems)
    for copies, slots in ((slope_copies, slope_slots), (factor_copies, factor_slots)):
        waits.extend(copy.wait for copy in copies[-slots.shape[0] :])

    swap_lens.wait()
    lens_2 = row_values(lens_other, sentences)
    length = jnp.where(mine, row_lengths(lens, step_sentence), row_lengths(lens_2, step_sentence))
    live = real & (step_segment < (length + STRIDE - 1) // STRIDE)
    emit_ref[...] = jnp.broadcast_to(live.astype(F32), (steps, 128))
    own_part = dot(take_own, high_ref[...])
    loads[1].wait()
    for side in range(hidden // TILE):
        hwy_slots[0, side, pl.ds(0, wide), :] = rec_ref[pl.ds(side * TILE, TILE), :].T
    swap.wait()
    stepped = (own_part + dot(take_other, other_ref[...])).astype(BF16)
    loads[0].wait()
    gates_ref[...] = dot(stepped, in_ref[...]) + in_bias

    def ahead(index, state):
        at = pl.ds(pl.multiple_of(index * height, height), height)
        q = dot(state.astype(BF16), rec_ref[...]) + rec_bias
        gates = gates_ref[at, :]
        alive = emit_ref[at, 0:1] > 0.0
        reset = sigmoid(gates[:, :hidden] + q[:, :hidden])
        update = sigmoid(gates[:, hidden : 2 * hidden] + q[:, hidden : 2 * hidden])
        q_n = q[:, 2 * hidden :]
        fresh = jnp.tanh(gates[:, 2 * hidden :] + reset * q_n)
        keep = jnp.where(alive, update, 1.0)
        move = jnp.where(alive, 1.0 - update, 0.0)
        after = move * fresh + keep * state
        prior_ref[at, :] = state
        slope = move * (1.0 - fresh * fresh)
        slope_r = slope * reset
        coef_ref[at, :hidden] = slope_r * q_n * (1.0 - reset)
        coef_ref[at, hidden : 2 * hidden] = (state - fresh) * update * move
        coef_ref[at, 2 * hidden : wide] = slope_r
        coef_ref[at, wide : wide + hidden] = slope
        coef_ref[at, wide + hidden :] = keep
        gates_ref[at, :hidden] = jnp.where(alive, after, 0.0)
        return after

    lax.fori_loop(0, segments, ahead, jnp.zeros((height, hidden), F32), unroll=4)
    for came, onward in pool_onwards + high_onwards:
        came.wait_recv()
        onward.start()
        waits.append(onward.wait)
    states = dot_tn(pick, gates_ref[:, :hidden].astype(BF16)).astype(BF16)
    block = rows // groups
    for whose in range(2):
        for place in range(groups):
            at = (whose * groups + place) * block
            states_ref[whose, place] = states[at : at + block].reshape(sentences, part, hidden)
    seat = (exact(here.seq * sentences, sentences, 1), slice(None), exact(here.core * hidden, hidden, 128))
    for hop, flip, device in here.column():
        copy = remote(
            states_ref.at[(here.core + flip) % 2, here.along_place(hop)], states_out.at[seat],
            states_sems.at[0, 2 * hop + flip], states_sems.at[1, 2 * hop + flip], device,
        )
        copy.start()
        waits.append(copy.wait)
    stay = pltpu.make_async_copy(states_ref.at[here.core, here.seq], states_out.at[seat], states_sems.at[0, 0])
    stay.start()
    waits.append(stay.wait)
    for copy in cot_copies:
        copy.wait()
    cot = cot_box[...].reshape(2 * rows, hidden)
    gates_ref[:, :hidden] = dot(pick, cot) * emit_ref[:, 0:1]

    def back(index, carried):
        at = pl.ds(pl.multiple_of((segments - 1 - index) * height, height), height)
        total = carried + gates_ref[at, :hidden]
        d_r = total * coef_ref[at, :hidden]
        d_z = total * coef_ref[at, hidden : 2 * hidden]
        d_q = total * coef_ref[at, 2 * hidden : wide]
        d_n = total * coef_ref[at, wide : wide + hidden]
        kept = total * coef_ref[at, wide + hidden :]
        coef_ref[at, :hidden] = d_r
        coef_ref[at, hidden : 2 * hidden] = d_z
        coef_ref[at, 2 * hidden : wide] = d_q
        coef_ref[at, wide : wide + hidden] = d_n
        low = jnp.concatenate([d_r, d_z, d_q], axis=1).astype(BF16)
        pushed = [dot(low, hwy_slots[0, side, pl.ds(0, wide), :]) for side in range(hidden // TILE)]
        return kept + jnp.concatenate(pushed, axis=1)

    lax.fori_loop(0, segments, back, jnp.zeros((height, hidden), F32), unroll=4)
    recur = coef_ref[:, :wide].astype(BF16)
    fresh = coef_ref[:, wide : wide + hidden].astype(BF16)
    share = 2 * wide // dps
    chunk = chunk_of(share, IN_CHUNKS)
    seat = (slice(None), exact(here.core * wide, wide, 128))
    seat_t = exact(here.core * wide, wide, 16)
    given_t_ref = in_ref.at[pl.ds(0, wide), pl.ds(hidden, rows)]
    keep_t_ref = in_ref.at[pl.ds(0, wide), pl.ds(hidden + rows, rows)]
    for take, ref, ref_t in ((take_other, given_ref, given_t_ref), (take_own, keep_ref, keep_t_ref)):
        ref[:, : 2 * hidden] = dot_tn(take, recur[:, : 2 * hidden]).astype(BF16)
        ref[:, 2 * hidden :] = dot_tn(take, fresh).astype(BF16)
        for row, size, place in chunk_pieces(0, wide, share, chunk):
            ref_t[place : place + size, :] = ref[:, row : row + size].T
        if ref is given_ref:
            copies = [
                remote(ref, pair_hbm.at[seat], swap_sems.at[4], swap_sems.at[5], here.partner),
                remote(ref_t, turned_hbm.at[seat_t], swap_sems.at[6], swap_sems.at[7], here.partner),
            ]
        else:
            copies = [
                pltpu.make_async_copy(ref, pair_hbm.at[seat], load_sems.at[4]),
                pltpu.make_async_copy(ref_t, turned_hbm.at[seat_t], load_sems.at[5]),
            ]
        for copy in copies:
            copy.start()
            waits.append(copy.wait)
    prior = prior_ref[...].astype(BF16).T
    sums = jnp.sum(recur.astype(F32), axis=0, keepdims=True)
    sums_n = jnp.sum(fresh.astype(F32), axis=0, keepdims=True)
    rec_tiles = wide // TILE
    bias_ref[...] = jnp.zeros_like(bias_ref)
    for tile in range(rec_tiles):
        cols = slice(tile * TILE, (tile + 1) * TILE)
        rec_part_ref[tile * hidden : (tile + 1) * hidden, :] = dot(prior, recur[:, cols]).astype(BF16)
        if tile * TILE < 2 * hidden:
            bias_ref[tile : tile + 1, :] = sums[:, cols]
        else:
            bias_ref[tile : tile + 1, :] = sums_n[:, tile * TILE - 2 * hidden : (tile + 1) * TILE - 2 * hidden]
        bias_ref[rec_tiles + tile : rec_tiles + tile + 1, :] = sums[:, cols]
    rec_part_ref[rec_tiles * hidden :, :] = bias_ref[...].astype(BF16)
    for wait in waits:
        wait()


class Ring:
    def __init__(self, slots, sems, loads):
        self.slots, self.sems, self.loads = slots, sems, loads
        self.depth = slots.shape[0]
        self.copies = {}

    def start(self, index):
        if index < len(self.loads):
            source, place = self.loads[index]
            slot = index % self.depth
            self.copies[index] = pltpu.make_async_copy(source, place(self.slots.at[slot]), self.sems.at[slot])
            self.copies[index].start()

    def begin(self):
        for index in range(self.depth):
            self.start(index)

    def take(self, index):
        self.copies[index].wait()
        return self.slots.at[index % self.depth]

    def done(self, index):
        self.start(index + self.depth)


def tail_kernel(
    sizes, lens_ref, pair_hbm, turned_hbm, factor_hbm, slope_hbm, cross_hbm, taps_hbm, in_hbm, hwy_hbm, high_hbm, pool_hbm, rec_hbm,
    in_low, hwy_low, conv_out, rec_out, chars_box,
    weight_slots, factor_slots, slope_slots, rows_ref, full_slots,
    pair_ref, gates_own, dpre_ref, pre_t_ref, dy_ref, dconv_ref, bias_ref, chars_ref, cross_ref, taps_ref,
    in_box, hwy_box, in_got, hwy_got, in_outer, hwy_outer, in_inner, hwy_inner,
    conv_part, conv_got, conv_half, conv_box, conv_low, conv_outer, conv_inner, rec_box, rec_low, rec_outer, rec_inner,
    weight_sems, factor_sems, slope_sems, load_sems, in_spread, hwy_spread, chars_sems,
    in_sems, hwy_sems, conv_swap, conv_sems, rec_sems, conv_line, rec_line, conv_share, rec_share,
):
    sentences, span, segments, channels, embed, filters, dps, groups = sizes
    rows = sentences * segments
    tiles = channels // TILE
    wide = pair_hbm.shape[1] // 2
    here = Place(dps, groups)

    def tile_at(tile):
        return pl.ds(tile * TILE, TILE)

    weights = Ring(
        weight_slots, weight_sems,
        [(in_hbm.at[tile_at(tile)], lambda slot: slot.at[:, pl.ds(0, 2 * wide)]) for tile in range(tiles)]
        + [(hwy_hbm.at[tile_at(tile)], lambda slot: slot) for tile in range(tiles)],
    )
    factors = Ring(factor_slots, factor_sems, [(factor_hbm.at[tile], lambda slot: slot) for tile in range(tiles)])
    slopes = Ring(slope_slots, slope_sems, [(slope_hbm.at[tile], lambda slot: slot) for tile in range(tiles)])
    pair_load = pltpu.make_async_copy(pair_hbm, pair_ref, load_sems.at[0])
    pair_load.start()
    taps_load = pltpu.make_async_copy(taps_hbm, taps_ref, load_sems.at[1])
    cross_load = pltpu.make_async_copy(cross_hbm, cross_ref, load_sems.at[2])
    in_share, hwy_share = in_got.shape[0] * in_got.shape[1], hwy_got.shape[0] * hwy_got.shape[1]
    own_load = pltpu.make_async_copy(
        turned_hbm.at[exact(here.chip * 2 * in_share, 2 * in_share, 16)], gates_own, load_sems.at[4]
    )
    own_load.start()
    rows_load = pltpu.make_async_copy(high_hbm, rows_ref, load_sems.at[5])
    rows_load_2 = pltpu.make_async_copy(pool_hbm, rows_ref, load_sems.at[5])
    rows_load.start()
    weights.begin()
    factors.begin()
    greet([here.partner] + here.peers() + here.along())
    rec_load = pltpu.make_async_copy(
        rec_hbm.at[exact(here.chip * rec_low.shape[0], rec_low.shape[0], 16)], rec_low, load_sems.at[3]
    )
    rec_load.start()
    ids = row_ids(rows)
    segment, sentence = ids // sentences, ids % sentences
    length = row_lengths(own_lengths(lens_ref, here.seq * sentences, sentences), sentence)
    count = jnp.clip(length - STRIDE * segment, 0, STRIDE).astype(F32)
    scale = 1.0 / jnp.maximum(count, 1.0)
    bias_ref[...] = jnp.zeros_like(bias_ref)
    sent = []
    waits = []

    def spread(source, box, sends):
        share = box.shape[1]
        copies = []
        for hop in range(1, here.chips):
            at = exact(here.peer_chip(hop) * share, share, 16)
            copies.append(
                remote(source.at[at], box.at[hop - 1], sends.at[0, hop], sends.at[1, hop], here.peer(hop))
            )
            copies[-1].start()
        sent.extend(copies)
        return copies

    def chunk_spread(source, box, sends, share, chunk):
        lists = []
        for turn in range(share // chunk):
            lists.append([])
            for hop in range(1, here.chips):
                at = exact(here.peer_chip(hop) * 2 * share + turn * 2 * chunk, 2 * chunk, 16)
                lists[-1].append(
                    remote(
                        source.at[at], box.at[hop - 1, pl.ds(turn * 2 * chunk, 2 * chunk)],
                        sends.at[0, turn, hop], sends.at[1, turn, hop], here.peer(hop),
                    )
                )
                lists[-1][-1].start()
            sent.extend(lists[-1])
        return lists

    in_chunk, hwy_chunk = in_got.shape[1], hwy_got.shape[1]
    in_lists = chunk_spread(turned_hbm, in_box, in_spread, in_share, in_chunk)
    rec_copies = spread(rec_hbm, rec_box, rec_sems)
    pair_load.wait()

    def hwy_back(tile):
        cols = slice(tile * TILE, (tile + 1) * TILE)
        cols_2 = slice(channels + tile * TILE, channels + (tile + 1) * TILE)
        weight = weights.take(tile)
        dy = dot_nt(pair_ref[...], weight[:, : 2 * wide])
        weights.done(tile)
        factor = factors.take(tile)
        d_1 = (dy * factor[0]).astype(BF16)
        d_2 = (dy * factor[1]).astype(BF16)
        dy_ref[:, cols] = dy * factor[2]
        factors.done(tile)
        dpre_ref[:, cols] = d_1
        dpre_ref[:, cols_2] = d_2
        for at, turned in ((cols, d_1.T), (cols_2, d_2.T)):
            for row, size, place in chunk_pieces(at.start, at.stop, hwy_share, hwy_chunk):
                pre_t_ref[place : place + size, :] = turned[row - at.start : row - at.start + size]
        bias_ref[tiles + tile : tiles + tile + 1, :] = jnp.sum(d_1.astype(F32), axis=0, keepdims=True)
        bias_ref[2 * tiles + tile : 2 * tiles + tile + 1, :] = jnp.sum(d_2.astype(F32), axis=0, keepdims=True)

    hwy_lists = []

    def hwy_send():
        hwy_lists.extend(chunk_spread(pre_t_ref, hwy_box, hwy_spread, hwy_share, hwy_chunk))
        slopes.begin()
        taps_load.start()
        cross_load.start()

    def conv_back(tile):
        cols = slice(tile * TILE, (tile + 1) * TILE)
        weight = weights.take(tiles + tile)
        dy = (dy_ref[:, cols] + dot_nt(dpre_ref[...], weight[...])) * scale
        weights.done(tiles + tile)
        slope = slopes.take(tile)
        sums = jnp.zeros((1, TILE), F32)
        for place in range(STRIDE):
            alive = (segment * STRIDE + place < length).astype(F32)
            part = (dy * alive * slope[place].astype(F32)).astype(BF16)
            dconv_ref[place * rows : (place + 1) * rows, cols] = part
            sums = sums + jnp.sum(part.astype(F32), axis=0, keepdims=True)
        slopes.done(tile)
        bias_ref[tile : tile + 1, :] = sums

    spans = tile_taps(filters)
    starts = [0]
    for low, high in spans:
        starts.append(starts[-1] + (high - low) * embed)
    sums = {}
    half = conv_half.shape[0]
    conv_copy = remote(
        conv_part.at[exact((1 - here.core) * half, half, 16)], conv_got, conv_swap.at[0], conv_swap.at[1], here.partner
    )
    conv_copies = []

    def chars_part(begin_tap):
        begin = min(tile for tile, (low, high) in enumerate(spans) if low < begin_tap + 2 and high > begin_tap)
        part = dot(
            dconv_ref[:, begin * TILE :],
            taps_ref[begin * TILE :, begin_tap * embed : (begin_tap + 2) * embed],
        )
        for tap in (begin_tap, begin_tap + 1):
            for place in range(STRIDE):
                spot = place + tap - LEAD
                key = (spot // STRIDE, spot % STRIDE)
                piece = part[
                    place * rows : (place + 1) * rows, (tap - begin_tap) * embed : (tap - begin_tap + 1) * embed
                ]
                sums[key] = sums[key] + piece if key in sums else piece

    def chars_end():
        total = jnp.zeros((sentences * span, embed), F32)
        out_ids = row_ids(sentences * span)
        out_sentence, out_time = out_ids // span, out_ids % span
        for place in range(STRIDE):
            plane = jnp.zeros((rows, embed), F32)
            for hop in (-1, 0, 1):
                if (hop, place) in sums:
                    plane = plane + shift_rows(sums[hop, place], hop * sentences)
            plane = jnp.where(segment * STRIDE + place < length, plane, 0.0).astype(BF16)
            target = jnp.where(
                out_time % STRIDE == place, (out_time // STRIDE) * sentences + out_sentence, -1
            )
            total = total + dot(one_hot(sentences * span, rows, target), plane)
        for index in range(sentences):
            chars_ref[index] = total[index * span : (index + 1) * span].astype(BF16)
        chars_box[here.seq] = chars_ref[:, exact(here.seq * chars_share, chars_share, 16), :]

    chars_share = span // groups
    chars_copies = []
    for hop in range(1, groups):
        at = exact(here.along_place(hop) * chars_share, chars_share, 16)
        chars_copies.append(
            remote(
                chars_ref.at[:, at], chars_box.at[here.seq], chars_sems.at[0, hop], chars_sems.at[1, hop],
                (here.dp, here.along_place(hop)),
            )
        )
    waits.extend(copy.wait for copy in chars_copies)

    def chars_send(across):
        for hop, copy in enumerate(chars_copies):
            other = (here.along_place(hop + 1) < groups // 2) != (here.seq < groups // 2)
            pl.when(other if across else jnp.logical_not(other))(copy.start)

    def taps_part(tile):
        low, high = spans[tile]
        conv_part[starts[tile] : starts[tile + 1], :] = dot(
            cross_ref[low * embed : high * embed, :], dconv_ref[:, tile * TILE : (tile + 1) * TILE]
        ).astype(BF16)

    def taps_end():
        conv_part[starts[-1] :, :] = bias_ref[...].astype(BF16)
        conv_copy.start()
        sent.append(conv_copy)

    def conv_send():
        conv_copy.wait_recv()
        mine = conv_part[exact(here.core * half, half, 16), :]
        conv_half[...] = (mine.astype(F32) + conv_got[...].astype(F32)).astype(BF16)
        conv_copies.extend(spread(conv_half, conv_box, conv_sems))
        share = conv_low.shape[0]
        conv_low[...] = conv_half[exact(here.chip * share, share, 16), :]

    tasks = [cross_load.wait]
    tasks += [functools.partial(taps_part, tile) for tile in range(tiles)]
    tasks += [taps_end, taps_load.wait, functools.partial(chars_part, 0), conv_send]
    tasks += [functools.partial(chars_part, begin_tap) for begin_tap in range(2, NWID, 2)] + [chars_end]

    halves = []

    def multiply(box, own, own_first, lists, low, got, sems, turn):
        chunk = got.shape[1]
        index = len(halves)
        full = full_slots.at[index % full_slots.shape[0], pl.ds(0, 2 * chunk)]
        if index >= full_slots.shape[0]:
            halves[index - full_slots.shape[0]].wait_send()
        for copy in lists[turn]:
            copy.wait_recv()
        at = pl.ds(turn * 2 * chunk, 2 * chunk)
        for tile in range(tiles):
            cols = slice(tile * TILE, (tile + 1) * TILE)
            total = dot(own[exact(own_first + turn * 2 * chunk, 2 * chunk, 16), :], rows_ref[here.chip, :, cols])
            for hop in range(1, here.chips):
                chip = (here.chip + here.chips - hop) % here.chips
                total = total + dot(box[hop - 1, at, :], rows_ref[chip, :, cols])
            full[:, cols] = total.astype(BF16)
        low[turn] = full[exact(here.core * chunk, chunk, 16), :]
        copy = remote(
            full.at[exact((1 - here.core) * chunk, chunk, 16)], got.at[turn],
            sems.at[turn, 0, 0], sems.at[turn, 0, 1], here.partner,
        )
        copy.start()
        halves.append(copy)

    def line_item(found, low, from_outer, from_inner, sem, keep=None):
        out_to_in = remote(low, from_outer, sem(2), sem(3), here.inner)
        across = remote(low, from_inner, sem(2), sem(4), here.inner)
        in_to_out = remote(low, from_inner, sem(5), sem(4), here.outer)

        def inward():
            @pl.when(here.has_outer)
            def _():
                out_to_in.wait_recv()
                low[...] = (found() + from_outer[...].astype(F32)).astype(BF16)

            @pl.when(jnp.logical_not(here.has_outer))
            def _():
                low[...] = found().astype(BF16)

            @pl.when(here.middle)
            def _():
                across.start()

            @pl.when(jnp.logical_not(here.middle))
            def _():
                out_to_in.start()

        def outward():
            across.wait()

            @pl.when(here.middle)
            def _():
                low[...] = (low[...].astype(F32) + from_inner[...].astype(F32)).astype(BF16)

            @pl.when(jnp.logical_not(here.middle))
            def _():
                low[...] = from_inner[...]

            @pl.when(here.has_outer)
            def _():
                in_to_out.start()

            if keep is not None:
                keep()

        def finish():
            @pl.when(here.has_outer)
            def _():
                in_to_out.wait_send()

        return inward, outward, finish

    onward = []

    def share_out(out, low, begin, size, sems):
        base = here.core * (out.shape[0] // 2) + begin
        share = low.shape[0]
        piece = low.at[pl.ds(begin, size)]
        at = exact(base + here.chip * share, size, 16)
        stay = pltpu.make_async_copy(piece, out.at[at], sems.at[2, 0])
        copies = [remote(piece, out.at[at], sems.at[0, 0], sems.at[1, 0], here.partner)]
        for hop in range(1, here.chips):
            copies.append(remote(piece, out.at[at], sems.at[0, hop], sems.at[1, hop], here.peer(hop)))
            source = (here.chip + here.chips - hop) % here.chips
            place = exact(base + source * share, size, 16)
            send_on = remote(out.at[place], out.at[place], sems.at[2, hop], sems.at[3, hop], here.partner)
            onward.append((copies[hop], send_on))
            waits.append(send_on.wait)
        waits.extend(copy.wait_send for copy in copies)
        waits.append(copies[0].wait_recv)
        waits.append(stay.wait)

        def keep():
            stay.start()
            for copy in copies:
                copy.start()

        return keep

    def chunk_items(low, got, first, outer, inner, sems, finer):
        found_lists = []

        def found(turn, part, at):
            if part == 0:
                halves[first + turn].wait_recv()
            return low[turn, :, at].astype(F32) + got[turn, :, at].astype(F32)

        for turn in range(low.shape[0]):
            count = ENDING if turn == finer else HALVES
            cuts = [-(-tiles * part // count) * TILE if count > 2 else part * channels // count for part in range(count + 1)]
            found_lists.append([])
            for part, (begin, end) in enumerate(zip(cuts, cuts[1:])):
                at = (turn, slice(None), pl.ds(begin, end - begin))
                found_lists[-1].append(
                    line_item(
                        functools.partial(found, turn, part, slice(begin, end)), low.at[at], outer.at[at], inner.at[at],
                        lambda index, turn=turn, part=part: sems.at[turn, 1 + part, index],
                    )
                )
        return found_lists

    def small_items(low, box, copies, outer, inner, line_sems, share_sems, out, ready):
        found_items = []
        size = low.shape[0] // 16
        cuts = [size * part // SMALL_PARTS * 16 for part in range(SMALL_PARTS + 1)]

        def found(part):
            if part == 0:
                ready()
                for copy in copies:
                    copy.wait_recv()
            at = slice(cuts[part], cuts[part + 1])
            total = low[at, :].astype(F32)
            for hop in range(here.chips - 1):
                total = total + box[hop, at, :].astype(F32)
            return total

        for part in range(SMALL_PARTS):
            at = pl.ds(cuts[part], cuts[part + 1] - cuts[part])
            found_items.append(
                line_item(
                    functools.partial(found, part), low.at[at], outer.at[at], inner.at[at],
                    lambda index, part=part: line_sems.at[part, index],
                    share_out(out, low, cuts[part], cuts[part + 1] - cuts[part], share_sems.at[part]),
                )
            )
        return found_items

    in_items = chunk_items(in_low, in_got, 0, in_outer, in_inner, in_sems, 0)
    hwy_items = chunk_items(hwy_low, hwy_got, in_low.shape[0], hwy_outer, hwy_inner, hwy_sems, hwy_low.shape[0] - 1)
    rec_items = small_items(
        rec_low, rec_box, rec_copies, rec_outer, rec_inner, rec_line, rec_share, rec_out, rec_load.wait
    )
    conv_items = small_items(
        conv_low, conv_box, conv_copies, conv_outer, conv_inner, conv_line, conv_share, conv_out, lambda: None
    )

    def in_multiply(turn):
        if turn == 0:
            own_load.wait()
            rows_load.wait()
        multiply(in_box, gates_own, 0, in_lists, in_low, in_got, in_sems, turn)
        if turn + 1 == in_low.shape[0]:
            rows_load_2.start()

    def hwy_multiply(turn):
        if turn == 0:
            rows_load_2.wait()
        multiply(hwy_box, pre_t_ref, here.chip * 2 * hwy_share, hwy_lists, hwy_low, hwy_got, hwy_sems, turn)

    tasks = [hwy_send] + [functools.partial(conv_back, tile) for tile in range(tiles)] + tasks
    tasks = [functools.partial(hwy_back, tile) for tile in range(tiles)] + tasks
    items = []
    plan = []

    def add(new):
        plan.extend(new)

    add([tiles + 1])
    for turn in range(in_low.shape[0]):
        add([functools.partial(in_multiply, turn), 1])
        for item in in_items[turn]:
            add([item, 1 if turn == 0 else 2])
    for item in rec_items:
        add([2, item])
    last = hwy_low.shape[0] - 1
    for turn in range(last):
        if turn == (last + 1) // 2:
            add(conv_items)
        add([functools.partial(hwy_multiply, turn), 1])
        for item in hwy_items[turn]:
            add([2, item])
    if last < 1:
        add([len(tasks)] + conv_items)
    add([functools.partial(hwy_multiply, last), len(tasks)])
    for item in hwy_items[last]:
        add([item])
    depths = groups // 2

    def outwards(index):
        for depth in range(depths):
            ready = index - 2 - LAG * depth
            if 0 <= ready < len(items):
                pl.when(here.depth == depth)(items[ready][1])

    for step in plan:
        if isinstance(step, int):
            for task in tasks[:step]:
                task()
            del tasks[:step]
        elif isinstance(step, tuple):
            items.append(step)
            step[0]()
            outwards(len(items) - 1)
        else:
            step()
    chars_send(True)
    extras = 2 + LAG * (depths - 1)
    shared = min(max(items.index(conv_items[-1]) + extras - len(items) + 4, 1), extras - 1)
    for extra in range(extras):
        outwards(len(items) + extra)
        if extra == 1:
            chars_send(False)
        if extra == shared:
            for copy, send_on in onward:
                copy.wait_recv()
                send_on.start()
    for item in items:
        item[2]()
    for copy in sent:
        copy.wait_send()
    for copy in halves[-full_slots.shape[0] :]:
        copy.wait_send()
    for wait in waits:
        wait()


def finish_kernel(
    sizes, in_hbm, hwy_hbm, conv_hbm, rec_hbm, chars_hbm,
    in_out, hwy_out, conv_out, rec_out, chars_out, conv_bias_out, hwy_bias_out, in_bias_out, rec_bias_out,
    in_ref, hwy_ref, conv_ref, rec_ref, chars_ref, in_full, hwy_full, conv_full, rec_full, chars_full,
    load_sems, store_sems,
):
    embed, filters, hidden = sizes
    tiles = in_ref.shape[2] // TILE
    half = rec_ref.shape[0] // 2
    loads = [
        pltpu.make_async_copy(rec_hbm.at[pl.ds(side * half, half)], rec_ref.at[pl.ds(side * half, half)], load_sems.at[side])
        for side in range(2)
    ]
    for place, (source, ref) in enumerate(((hwy_hbm, hwy_ref), (conv_hbm, conv_ref), (in_hbm, in_ref), (chars_hbm, chars_ref))):
        loads.append(pltpu.make_async_copy(source, ref, load_sems.at[2 + place]))
    for load in loads:
        load.start()
    stores = []

    def store(source, out):
        stores.append(pltpu.make_async_copy(source, out, store_sems.at[len(stores)]))
        stores[-1].start()

    rec_tiles = 3 * hidden // TILE
    for side in range(2):
        loads[side].wait()
        for tile in range(rec_tiles):
            row = side * half + tile * hidden
            at = slice(tile * TILE, (tile + 1) * TILE)
            rec_full[side, :, at] = rec_ref[row : row + hidden, :].astype(F32)
        store(rec_full.at[side], rec_out.at[side])
        row = side * half + rec_tiles * hidden
        rest = rec_ref[row : row + 16, :].astype(F32)
        for tile in range(rec_tiles):
            at = slice(tile * TILE, (tile + 1) * TILE)
            in_bias_out[pl.ds((side * rec_tiles + tile) * TILE, TILE)] = rest[tile]
            rec_bias_out[side : side + 1, at] = rest[rec_tiles + tile : rec_tiles + tile + 1]
    loads[2].wait()
    hwy_full[...] = hwy_ref[...].astype(F32).reshape(hwy_full.shape)
    store(hwy_full, hwy_out)
    loads[3].wait()
    spans = tile_taps(filters)
    starts = [0]
    for low, high in spans:
        starts.append(starts[-1] + (high - low) * embed)
    for width in range(1, NWID + 1):
        lead, first = (width - 1) // 2, width * (width - 1) // 2
        for tap in range(width):
            spot = LEAD - lead + tap
            begin, end = (width - 1) * filters, width * filters
            while begin < end:
                tile = begin // TILE
                stop = min(end, (tile + 1) * TILE)
                row = starts[tile] + (spot - spans[tile][0]) * embed
                piece = conv_ref[row : row + embed, :].astype(F32).T
                at = slice(begin - (width - 1) * filters, stop - (width - 1) * filters)
                conv_full[first + tap, at, :] = piece[begin - tile * TILE : stop - tile * TILE]
                begin = stop
    store(conv_full, conv_out)
    rest = conv_ref[starts[-1] :, :].astype(F32)
    for tile in range(tiles):
        at = slice(tile * TILE, (tile + 1) * TILE)
        conv_bias_out[pl.ds(tile * TILE, TILE)] = rest[tile]
    for tile in range(2 * tiles):
        hwy_bias_out[:, tile * TILE : (tile + 1) * TILE] = rest[tiles + tile : tiles + tile + 1]
    loads[4].wait()
    for turn in range(in_ref.shape[0]):
        at = slice(turn * in_ref.shape[1], (turn + 1) * in_ref.shape[1])
        in_full[:, at] = in_ref[turn].astype(F32).T
    store(in_full, in_out)
    loads[5].wait()
    chars_full[...] = chars_ref[...].astype(F32).reshape(chars_full.shape)
    store(chars_full, chars_out)
    for copy in stores:
        copy.wait()


VMEM = pl.BlockSpec(memory_space=pltpu.VMEM)
SMEM = pl.BlockSpec(memory_space=pltpu.SMEM)
ANY = pl.BlockSpec(memory_space=pl.ANY)


def params(**more):
    return pltpu.CompilerParams(vmem_limit_bytes=VMEM_LIMIT, **more)


def shape(*dims, dtype=F32):
    return jax.ShapeDtypeStruct(dims, dtype)


def block(*dims, dtype=BF16):
    return pltpu.VMEM(dims, dtype)


def flags(*dims):
    return pltpu.SemaphoreType.DMA(dims)


def head_call(sizes, hidden, dps, groups, given):
    sentences, span, segments, channels, embed, filters = sizes
    wide, rows, chips, tiles = 3 * hidden, sentences * segments, dps // 2, channels // TILE
    height = max(8, 2 * sentences)
    steps, part = segments * height, segments // groups
    rec_rows = wide // TILE * hidden + 16 * chips
    side = math.isqrt(chips)
    copies = 1 + 2 * (side - 1) * (side + 1)
    return pl.pallas_call(
        functools.partial(head_kernel, sizes + (hidden, height, dps, groups)),
        name="head",
        out_shape=[
            shape(groups * sentences, part, 2 * hidden, dtype=BF16),
            shape(chips, rows, channels, dtype=BF16),
            shape(chips, rows, channels, dtype=BF16),
            shape(tiles, STRIDE, rows, TILE, dtype=BF16),
            shape(tiles, 3, rows, TILE),
            shape(NWID * embed, STRIDE * rows, dtype=BF16),
            shape(channels, NWID * embed, dtype=BF16),
            shape(rows, 2 * wide, dtype=BF16),
            shape(2 * wide, rows, dtype=BF16),
            shape(rec_rows, TILE, dtype=BF16),
        ],
        in_specs=[SMEM] + [VMEM] * 4 + [ANY] * 6,
        out_specs=[VMEM] + [ANY] * 8 + [VMEM],
        scratch_shapes=[
            block(NWID * (NWID + 1) // 2, filters, embed),
            block(NWID * embed, STRIDE * rows),
            block(channels, NWID * embed),
            block(rows, wide),
            block(1, LENS, dtype=F32),
            block(1, LENS, dtype=F32),
            block(groups, sentences, span // groups, embed),
            block(4 if chips <= 8 else 2, 2, channels, TILE),
            block(STRIDE, rows, NWID * embed),
            block(tiles if chips <= 8 else 2, STRIDE, rows, TILE),
            block(tiles if chips <= 8 else 2, 3, rows, TILE, dtype=F32),
            block(rows, channels),
            block(rows, channels),
            block(rows, channels),
            block(channels, wide),
            block(hidden, wide),
            block(steps, wide, dtype=F32),
            block(steps, 5 * hidden, dtype=F32),
            block(steps, hidden, dtype=F32),
            block(steps, 128, dtype=F32),
            block(2, groups, sentences, part, hidden),
            block(2, groups, sentences, part, hidden),
            block(rows, wide),
            block(16 * chips, TILE, dtype=F32),
            flags(4, 2), flags(tiles), flags(tiles), flags(7), flags(8), flags(2, groups), flags(2, 2 * groups),
            flags(2, 2 * groups), flags(2, copies), flags(2, copies),
        ],
        compiler_params=params(collective_id=2, has_side_effects=True),
    )(*given)


def tail_call(sizes, hidden, dps, groups, given):
    sentences, span, segments, channels, embed, filters = sizes
    wide, rows, chips = 3 * hidden, sentences * segments, dps // 2
    rec_rows = wide // TILE * hidden + 16 * chips
    tiles = channels // TILE
    in_share, hwy_share = 2 * wide // dps, 2 * channels // dps
    spans = tile_taps(filters)
    conv_rows = (sum(high - low for low, high in spans) + 1) * embed

    def slots(lead, share):
        return pltpu.VMEM((lead, share, TILE), BF16)

    in_chunk, hwy_chunk = chunk_of(in_share, IN_CHUNKS), chunk_of(hwy_share, HWY_CHUNKS)
    in_turns, hwy_turns = in_share // in_chunk, hwy_share // hwy_chunk
    conv_share, rec_share = conv_rows // dps, rec_rows // chips
    return pl.pallas_call(
        functools.partial(tail_kernel, sizes + (dps, groups)),
        name="tail",
        out_shape=[
            shape(in_turns, in_chunk, channels, dtype=BF16),
            shape(hwy_turns, hwy_chunk, channels, dtype=BF16),
            shape(conv_rows, TILE, dtype=BF16),
            shape(2 * rec_rows, TILE, dtype=BF16),
            shape(groups, sentences, span // groups, embed, dtype=BF16),
        ],
        in_specs=[SMEM] + [ANY] * 11,
        out_specs=[VMEM, VMEM, ANY, ANY, VMEM],
        scratch_shapes=[
            block(3 if chips <= 8 else 2, TILE, 2 * channels),
            block(2, 3, rows, TILE, dtype=F32),
            block(2, STRIDE, rows, TILE),
            block(chips, rows, channels),
            block(2, 2 * max(in_chunk, hwy_chunk), channels),
            block(rows, 2 * wide),
            block(2 * in_share, rows),
            block(rows, 2 * channels),
            block(2 * channels, rows),
            block(rows, channels, dtype=F32),
            block(STRIDE * rows, channels),
            block(embed, TILE, dtype=F32),
            block(sentences, span, embed),
            block(NWID * embed, STRIDE * rows),
            block(channels, NWID * embed),
            block(chips - 1, 2 * in_share, rows),
            block(chips - 1, 2 * hwy_share, rows),
            block(in_turns, in_chunk, channels), block(hwy_turns, hwy_chunk, channels),
            block(in_turns, in_chunk, channels), block(hwy_turns, hwy_chunk, channels),
            block(in_turns, in_chunk, channels), block(hwy_turns, hwy_chunk, channels),
            block(conv_rows, TILE),
            block(conv_rows // 2, TILE),
            block(conv_rows // 2, TILE),
            slots(chips - 1, conv_share),
            block(conv_share, TILE),
            block(conv_share, TILE),
            block(conv_share, TILE),
            slots(chips - 1, rec_share),
            block(rec_share, TILE),
            block(rec_share, TILE),
            block(rec_share, TILE),
            flags(3), flags(2), flags(2), flags(6),
            flags(2, in_turns, chips), flags(2, hwy_turns, chips), flags(2, groups),
            flags(in_turns, 1 + ENDING, 6), flags(hwy_turns, 1 + ENDING, 6), flags(2), flags(2, chips), flags(2, chips),
            flags(SMALL_PARTS, 6), flags(SMALL_PARTS, 6), flags(SMALL_PARTS, 4, chips), flags(SMALL_PARTS, 4, chips),
        ],
        compiler_params=params(collective_id=1, has_side_effects=True),
    )(
        *given
    )


def local(
    char_embeds, lengths, conv_weight, conv_bias, hwy_weight, hwy_bias, gru_in_weight, gru_in_bias,
    gru_rec_weight, gru_rec_bias, out_grad,
):
    groups = lax.axis_size("seq")
    dps = lax.axis_size("dp")
    sentences = char_embeds.shape[0] // groups
    span = char_embeds.shape[1] * groups
    segments = span // STRIDE
    embed, filters = conv_weight.shape[1:]
    channels = NWID * filters
    hidden = gru_rec_weight.shape[1]
    wide = 3 * hidden
    sizes = (sentences, span, segments, channels, embed, filters)
    encoded, pool_all, high_all, slope, factor, cross, taps, pair, turned, rec_part = head_call(
        sizes, hidden, dps, groups,
        (
            lengths, conv_bias, hwy_bias, gru_in_bias, gru_rec_bias, char_embeds, conv_weight.transpose(0, 2, 1), hwy_weight[0], out_grad, gru_in_weight, gru_rec_weight,
        ),
    )
    in_sum, hwy_sum, conv_sum, rec_sum, chars_box = tail_call(
        sizes, hidden, dps, groups,
        (
            lengths, pair, turned, factor, slope, cross, taps, gru_in_weight, hwy_weight[0], high_all, pool_all, rec_part,
        ),
    )
    in_share, hwy_share = 2 * wide // dps, 2 * channels // dps
    whole = [
        (channels, in_share),
        (hwy_share, channels),
        (NWID * (NWID + 1) // 2, filters, embed),
        (2, hidden, wide),
        (groups * sentences, span // groups, embed),
    ]
    in_grad, hwy_grad, conv_grad, rec_grad, dchars, conv_bias_grad, hwy_bias_grad, in_bias_grad, rec_bias_grad = pl.pallas_call(
        functools.partial(finish_kernel, (embed, filters, hidden)),
        name="finish",
        out_shape=[shape(*dims) for dims in whole]
        + [shape(channels), shape(1, 2 * channels), shape(2 * wide), shape(2, wide)],
        in_specs=[ANY] * 5,
        out_specs=[ANY] * 5 + [VMEM] * 4,
        scratch_shapes=[
            block(*part.shape) for part in (in_sum, hwy_sum, conv_sum, rec_sum, chars_box)
        ]
        + [block(*dims, dtype=F32) for dims in whole]
        + [flags(6), flags(6)],
        compiler_params=params(),
    )(in_sum, hwy_sum, conv_sum, rec_sum, chars_box)
    return (
        encoded, dchars, conv_grad.transpose(0, 2, 1), conv_bias_grad, hwy_grad.T[None], hwy_bias_grad, in_grad,
        in_bias_grad, rec_grad, rec_bias_grad,
    )


def solution(mesh):
    whole = P()
    split = P("dp", "seq", None)
    return jax.shard_map(
        local,
        mesh=mesh,
        in_specs=(split, P("dp")) + (whole,) * 8 + (split,),
        out_specs=(split, split, whole, whole, P(None, None, "dp"), whole, P(None, "dp"), whole, whole, whole),
        check_vma=False,
    )
```
